32 devices in a mesh: axial: 4 (over x, core), azim: 8 (over z, y).
Axes of the slice: x: 2, y: 2, z: 4, core: 2. Of those that a mesh axis runs over, the one named last changes fastest.
Arguments:
- cycle_state: float32 [5, 32, 1024, 256], P(None, 'axial', 'azim'), as said below
- core_state: float32 [5, 32, 192, 192], P(None, 'axial', 'azim'), as said below
- core_taps: int32 [768, 4], replicated, may hold values from 0 to 1023, as said below
- core_weights: float32 [768, 4], replicated, may hold values from 0.1 to 1
- cycle_taps: int32 [1024, 4], replicated, may hold values from 0 to 36863, as said below
- cycle_weights: float32 [1024, 4], replicated, may hold values from 0.1 to 1
Outputs:
- cycle_new: float32 [5, 32, 1024, 256], P(None, 'axial', 'azim')
- core_new: float32 [5, 32, 192, 192], P(None, 'axial', 'azim')
The draws below stay inside these ranges and needn't reach their ends.
Inputs may be any that keep to these rules, and one draw needn't show every extreme that they name: `core_taps`: cycle positions, each within 8 positions (cyclically) of position g * 1024 // 768. `cycle_taps`: flat indices of core cells within three cells of the core's edge. `cycle_state`: density (component 0) lies in 0.5 to 1.5. `core_state`: density (component 0) lies in 0.5 to 1.5.
All inputs are finite; a program needn't handle non-finite values.
Results may differ from the reference program's by a relative error of at most 0.0003.
Values sent between devices are 32-bit elements; how exact they have to be, the bound alone decides.
No kernel may reach another device: no remote copies, remote signals or barrier semaphores. Data moves between devices by JAX's collectives and lax.ppermute only.
A program may use at most 128 MiB of HBM per device.

```python
import math
import jax
import jax.numpy as jnp
from jax import lax

CA = 8
R = 256
CORE_N = 192
TAPS = 4
NX = 32
NT = 1024
GHOST = 768


def state_law(key, shape):
    keys = jax.random.split(key, 3)
    density = jax.random.uniform(keys[0], shape, jnp.float32, 0.5, 1.5)
    momenta = 0.6 * jax.random.normal(keys[1], (3,) + shape, jnp.float32)
    momenta = jnp.clip(momenta, -3.0, 3.0)
    energy = jax.random.uniform(keys[2], shape, jnp.float32, 2.0, 4.0)
    return jnp.concatenate([density[None], momenta, energy[None]], axis=0)


def draw_cycle_state(key, part):
    return state_law(jax.random.fold_in(key, 11), (NX, NT, R))


def draw_core_state(key, part):
    return state_law(jax.random.fold_in(key, 13), (NX, CORE_N, CORE_N))


def draw_core_taps(key, part):
    base = jnp.arange(GHOST, dtype=jnp.int32) * NT // GHOST
    jitter = jax.random.randint(jax.random.fold_in(key, 17), (GHOST, TAPS), -8, 9)
    taps = ((base[:, None] + jitter) % NT).astype(jnp.int32)
    taps = taps.at[0, 0].set(NT - 1)
    taps = taps.at[0, 1].set(0)
    return taps.astype(jnp.int32)


def draw_cycle_taps(key, part):
    perimeter = jnp.arange(NT, dtype=jnp.int32) * GHOST // NT
    jitter = jax.random.randint(jax.random.fold_in(key, 19), (NT, TAPS), -4, 5)
    inward = jax.random.randint(jax.random.fold_in(key, 23), (NT, TAPS), 0, 3)
    spot = (perimeter[:, None] + jitter) % GHOST
    side = spot // CORE_N
    along = spot % CORE_N
    row_idx = jnp.where(side < 2, along, jnp.where(side == 2, inward, CORE_N - 1 - inward))
    col_idx = jnp.where(side == 0, inward, jnp.where(side == 1, CORE_N - 1 - inward, along))
    taps = (row_idx * CORE_N + col_idx).astype(jnp.int32)
    taps = taps.at[0, 0].set(0)
    taps = taps.at[NT // 2 - 1, 0].set(CORE_N * CORE_N - 1)
    return taps.astype(jnp.int32)


def setup_inputs(seed: int = 0) -> dict:
    key_list = jax.random.split(jax.random.key(seed), 7)
    cycle_state = draw_cycle_state(jax.random.fold_in(key_list[6], 71), 0)
    core_state = draw_core_state(jax.random.fold_in(key_list[6], 71), 0)
    core_taps = draw_core_taps(jax.random.fold_in(key_list[6], 71), 0)
    core_weights = jnp.clip(jax.random.uniform(key_list[3], (GHOST, TAPS), jnp.float32, 0.1, 1.0), 0.1, 1.0)
    cycle_taps = draw_cycle_taps(jax.random.fold_in(key_list[6], 71), 0)
    cycle_weights = jnp.clip(jax.random.uniform(key_list[5], (NT, TAPS), jnp.float32, 0.1, 1.0), 0.1, 1.0)
    return dict(cycle_state=cycle_state, core_state=core_state, core_taps=core_taps, core_weights=core_weights, cycle_taps=cycle_taps, cycle_weights=cycle_weights)


time_step = 0.001
axial_step = 0.004
radial_step = 1.0 / 256.0
core_step = 2.0 / 192.0
inner_radius = 1.0
viscosity = 0.002
gamma_minus = 0.4


def pressure_of(state):
    kinetic = 0.5 * (state[1] * state[1] + state[2] * state[2] + state[3] * state[3]) / state[0]
    return gamma_minus * (state[4] - kinetic)


def fluxes(state, component):
    pressure = pressure_of(state)
    velocity = state[component] / state[0]
    parts = [state[component], state[1] * velocity, state[2] * velocity, state[3] * velocity, (state[4] + pressure) * velocity]
    parts[component] = parts[component] + pressure
    return jnp.stack(parts, axis=0)


def angle_of(positions, total):
    return (positions.astype(jnp.float32) + 0.5) * (2.0 * math.pi / total)


def to_cartesian(trace, angles):
    cosine = jnp.cos(angles)
    sine = jnp.sin(angles)
    y_part = trace[3] * cosine - trace[2] * sine
    z_part = trace[3] * sine + trace[2] * cosine
    return jnp.stack([trace[0], trace[1], y_part, z_part, trace[4]], axis=0)


def to_polar(trace, angles):
    cosine = jnp.cos(angles)
    sine = jnp.sin(angles)
    azimuthal = trace[3] * cosine - trace[2] * sine
    radial = trace[2] * cosine + trace[3] * sine
    return jnp.stack([trace[0], trace[1], azimuthal, radial, trace[4]], axis=0)


def interpolate(values, taps, weights):
    normed = weights / jnp.sum(weights, axis=1, keepdims=True)
    picked = jnp.take(values, taps, axis=2)
    return jnp.sum(picked * normed, axis=3)


def radius_full(count):
    return inner_radius + (jnp.arange(count + 2).astype(jnp.float32) - 0.5) * radial_step


def cycle_rhs(padded, inner_ghost, angle_step):
    center = padded[:, 1:-1, 1:-1]
    reflect = jnp.array([1.0, 1.0, 1.0, -1.0, 1.0], jnp.float32)[:, None, None]
    outer_ghost = center[:, :, :, -1] * reflect
    radial_pad = jnp.concatenate([inner_ghost[..., None], center, outer_ghost[..., None]], axis=3)
    radius = radius_full(center.shape[3])
    mid_radius = radius[1:-1]
    arc = angle_step * mid_radius
    axial_flux = fluxes(padded[:, :, 1:-1], 1)
    azim_flux = fluxes(padded[:, 1:-1], 2)
    radial_flux = fluxes(radial_pad, 3)
    divergence = (axial_flux[:, 2:] - axial_flux[:, :-2]) / (2.0 * axial_step)
    divergence = divergence + (azim_flux[:, :, 2:] - azim_flux[:, :, :-2]) / (2.0 * arc)
    divergence = divergence + (radius[2:] * radial_flux[..., 2:] - radius[:-2] * radial_flux[..., :-2]) / (2.0 * radial_step * mid_radius)
    laplace = (padded[:, 2:, 1:-1] - 2.0 * center + padded[:, :-2, 1:-1]) / (axial_step * axial_step)
    laplace = laplace + (padded[:, 1:-1, 2:] - 2.0 * center + padded[:, 1:-1, :-2]) / (arc * arc)
    laplace = laplace + (radial_pad[..., 2:] - 2.0 * center + radial_pad[..., :-2]) / (radial_step * radial_step)
    pressure = pressure_of(center)
    swirl = -center[2] * center[3] / (center[0] * mid_radius)
    outward = (center[2] * center[2] / center[0] + pressure) / mid_radius
    zero_part = jnp.zeros_like(swirl)
    source = jnp.stack([zero_part, zero_part, swirl, outward, zero_part], axis=0)
    return -divergence + source + viscosity * laplace


def core_rhs(axial_pad, row_pad, left_col, right_col):
    center = axial_pad[:, 1:-1]
    col_pad = jnp.concatenate([left_col[..., None], center, right_col[..., None]], axis=3)
    axial_flux = fluxes(axial_pad, 1)
    row_flux = fluxes(row_pad, 2)
    col_flux = fluxes(col_pad, 3)
    divergence = (axial_flux[:, 2:] - axial_flux[:, :-2]) / (2.0 * axial_step)
    divergence = divergence + (row_flux[:, :, 2:] - row_flux[:, :, :-2]) / (2.0 * core_step)
    divergence = divergence + (col_flux[..., 2:] - col_flux[..., :-2]) / (2.0 * core_step)
    laplace = (axial_pad[:, 2:] - 2.0 * center + axial_pad[:, :-2]) / (axial_step * axial_step)
    laplace = laplace + (row_pad[:, :, 2:] - 2.0 * center + row_pad[:, :, :-2]) / (core_step * core_step)
    laplace = laplace + (col_pad[..., 2:] - 2.0 * center + col_pad[..., :-2]) / (core_step * core_step)
    return -divergence + viscosity * laplace


def reference(cycle_state, core_state, core_taps, core_weights, cycle_taps, cycle_weights):
    channels, planes, positions_all, radial_cells = cycle_state.shape
    core_cells = core_state.shape[3]
    angles = angle_of(jnp.arange(positions_all), positions_all)
    angle_step = 2.0 * math.pi / positions_all
    cart_trace = to_cartesian(cycle_state[:, :, :, 0], angles)
    ghosts = interpolate(cart_trace, core_taps, core_weights)
    axial_pad = jnp.concatenate([core_state[:, -1:], core_state, core_state[:, :1]], axis=1)
    lower = ghosts[:, :, 2 * core_cells:3 * core_cells]
    upper = ghosts[:, :, 3 * core_cells:4 * core_cells]
    row_pad = jnp.concatenate([lower[:, :, None], core_state, upper[:, :, None]], axis=2)
    left_col = ghosts[:, :, 0:core_cells]
    right_col = ghosts[:, :, core_cells:2 * core_cells]
    core_new = core_state + time_step * core_rhs(axial_pad, row_pad, left_col, right_col)
    flat_core = core_state.reshape(channels, planes, core_cells * core_cells)
    inner_ghost = to_polar(interpolate(flat_core, cycle_taps, cycle_weights), angles)
    count = planes // CA

    def one_block(block):
        index_list = ((block * CA - 1 + jnp.arange(CA + 2)) % planes).astype(jnp.int32)
        slab = jnp.take(cycle_state, index_list, axis=1)
        slab = jnp.concatenate([slab[:, :, -1:], slab, slab[:, :, :1]], axis=2)
        inner_part = lax.dynamic_slice_in_dim(inner_ghost, (block * CA).astype(jnp.int32), CA, 1)
        own_part = lax.dynamic_slice_in_dim(cycle_state, (block * CA).astype(jnp.int32), CA, 1)
        return own_part + time_step * cycle_rhs(slab, inner_part, angle_step)

    stacked = lax.map(one_block, jnp.arange(count).astype(jnp.int32))
    cycle_new = jnp.moveaxis(stacked, 0, 1).reshape(channels, planes, positions_all, radial_cells)
    return cycle_new, core_new
```

```python
import functools
import math

import jax
import jax.numpy as jnp
from jax import lax
from jax.experimental import pallas as pl
from jax.experimental.pallas import tpu as pltpu
from jax.sharding import PartitionSpec as P

time_step = 0.001
axial_step = 0.004
radial_step = 1.0 / 256.0
core_step = 2.0 / 192.0
inner_radius = 1.0
viscosity = 0.002
gamma_minus = 0.4

LANES = 128
SUB = 8
PAIR = 64
GRANT = 40 * 1024 * 1024


def in_hbm(x):
    return pltpu.with_memory_space_constraint(x, pltpu.HBM)
f32 = jnp.float32
AX_ALPHA = time_step * viscosity / (axial_step * axial_step)
AX_BETA = time_step / (2.0 * axial_step)
RAD_ALPHA = time_step * viscosity / (radial_step * radial_step)
RAD_BETA = time_step / (2.0 * radial_step)
CORE_ALPHA = time_step * viscosity / (core_step * core_step)
CORE_BETA = time_step / (2.0 * core_step)


def velocities(q):
    inv = 1.0 / q[0]
    u = (q[1] * inv, q[2] * inv, q[3] * inv)
    kinetic = 0.5 * (q[1] * u[0] + q[2] * u[1] + q[3] * u[2])
    pressure = gamma_minus * (q[4] - kinetic)
    return u, pressure, q[4] + pressure


def scaled_flux(q, u, pressure, enthalpy, k, scale):
    su = u[k - 1] * scale
    parts = [q[k] * scale, q[1] * su, q[2] * su, q[3] * su, enthalpy * su]
    parts[k] = parts[k] + pressure * scale
    return parts


def to_sides(q, u, pressure, enthalpy, k, alpha, beta):
    flux = scaled_flux(q, u, pressure, enthalpy, k, beta)
    before, after = [], []
    for c in range(5):
        spread = q[c] * alpha
        before.append(spread - flux[c])
        after.append(spread + flux[c])
    return before, after


def radial_tables(cells):
    lane = lax.broadcasted_iota(jnp.int32, (1, cells), 1).astype(f32)
    radius = inner_radius + (lane + 0.5) * radial_step
    return radius, 1.0 / radius


def azim_coefs(radius_inv, angle_step):
    arc_inv = radius_inv * (1.0 / angle_step)
    return (time_step * viscosity) * arc_inv * arc_inv, (0.5 * time_step) * arc_inv


def edge_rows(q, alpha, beta):
    u, pressure, enthalpy = velocities(q)
    return to_sides(q, u, pressure, enthalpy, 2, alpha, beta)


def all_fluxes(q):
    inv = 1.0 / q[0]
    u1, u2, u3 = q[1] * inv, q[2] * inv, q[3] * inv
    m11, m22, m33 = q[1] * u1, q[2] * u2, q[3] * u3
    m12, m13, m23 = q[1] * u2, q[1] * u3, q[2] * u3
    pressure = gamma_minus * (q[4] - 0.5 * (m11 + m22 + m33))
    enthalpy = q[4] + pressure
    return (
        [q[1], m11 + pressure, m12, m13, enthalpy * u1],
        [q[2], m12, m22 + pressure, m23, enthalpy * u2],
        [q[3], m13, m23, m33 + pressure, enthalpy * u3],
    )


def main_kernel(first, count, angle_step, q_hbm, *rest):
    out_hbm, q_ref, out_ref, next_ref, prev_ref, in_sem, out_sem = rest[-7:]
    planes = q_hbm.shape[1]
    sector, cells = q_hbm.shape[2], q_hbm.shape[3]
    chunks = in_sem.shape[0]
    rows = sector // chunks
    lo = max(first - 1, 0)
    hi = min(first + count + 1, planes)
    strips = cells // LANES

    def in_copy(h, s):
        part = pl.ds(h * rows, rows)
        return pltpu.make_async_copy(
            q_hbm.at[:, pl.ds(lo, hi - lo), part, pl.ds(s * LANES, LANES)],
            q_ref.at[:, :, s, part],
            in_sem.at[h, s],
        )

    def out_copy(h):
        part = pl.ds(h * rows, rows)
        return pltpu.make_async_copy(
            out_ref.at[:, :, part], out_hbm.at[:, pl.ds(first, count), part], out_sem.at[h]
        )

    for h in range(chunks):
        for s in range(strips):
            in_copy(h, s).start()
    unit = 1.0 / AX_BETA
    lane = lax.broadcasted_iota(jnp.int32, (1, LANES), 1)
    first_lane = lane == 0
    last_lane = lane == LANES - 1
    row = lax.broadcasted_iota(jnp.int32, (SUB, 1), 0)
    first_row = row == 0
    last_row = row == SUB - 1
    coefs = []
    for s in range(strips):
        radius = inner_radius + ((lane + s * LANES).astype(f32) + 0.5) * radial_step
        radius_inv = 1.0 / radius
        alpha2, beta2 = azim_coefs(radius_inv, angle_step)
        beta_before = RAD_BETA * radius / (radius - radial_step)
        beta_after = RAD_BETA * radius / (radius + radial_step)
        if s == strips - 1:
            wall = RAD_BETA * (radius + radial_step) / radius
            beta_after = jnp.where(last_lane, wall, beta_after)
        center = 1.0 - 2.0 * AX_ALPHA - 2.0 * RAD_ALPHA - 2.0 * alpha2
        table = (alpha2, beta2, beta_before, beta_after, center, time_step * radius_inv)
        coefs.append([jnp.broadcast_to(t * unit, (SUB, LANES)) for t in table])
    ratio = AX_ALPHA / AX_BETA
    radial_alpha = RAD_ALPHA * unit

    tiles = sector // SUB
    chunk_tiles = tiles // chunks
    zero = jnp.zeros((1, cells), f32)
    for i in range(count):
        for c in range(5):
            prev_ref[i, c, SUB - 1 : SUB, :] = zero
            next_ref[i, c, tiles : tiles + 1, :] = zero

    def edges(h):
        for i in range(count):
            x = first + i - lo
            for s in range(strips):
                alpha2, beta2 = coefs[s][0][:chunk_tiles], coefs[s][1][:chunk_tiles]
                wide = slice(s * LANES, (s + 1) * LANES)
                q = [q_ref[c, x, s, pl.ds(h * rows, chunk_tiles, stride=SUB), :] for c in range(5)]
                before, _ = edge_rows(q, alpha2, beta2)
                q = [
                    q_ref[c, x, s, pl.ds(h * rows + SUB - 1, chunk_tiles, stride=SUB), :]
                    for c in range(5)
                ]
                _, after = edge_rows(q, alpha2, beta2)
                for c in range(5):
                    next_ref[i, c, pl.ds(h * chunk_tiles, chunk_tiles), wide] = before[c]
                    prev_ref[i, c, pl.ds(SUB + h * chunk_tiles, chunk_tiles), wide] = after[c]

    def straight(q):
        return q if abs(ratio - 1.0) < 1e-9 else q * ratio

    def tile(j):
        part = pl.ds(pl.multiple_of(j * SUB, SUB), SUB)

        def load(x):
            return [[q_ref[c, x, s, part, :] for c in range(5)] for s in range(strips)]

        def axial(q, sign):
            flux = all_fluxes(q)[0]
            return [straight(q[c]) + sign * flux[c] for c in range(5)]

        def finish(i, held, before):
            for s in range(strips):
                for c in range(5):
                    value = held[s][c] if before is None else held[s][c] + before[s][c]
                    out_ref[c, i, part, s * LANES : (s + 1) * LANES] = value * AX_BETA

        carry = [axial(q, 1.0) for q in load(0)] if first > 0 else None
        held = None
        for i in range(count):
            q = load(first + i - lo)
            flux = [all_fluxes(q[s]) for s in range(strips)]
            if held is not None:
                finish(
                    i - 1,
                    held,
                    [[straight(q[s][c]) - flux[s][0][c] for c in range(5)] for s in range(strips)],
                )
            total = []
            for s in range(strips):
                alpha2, beta2, _, _, center, source = coefs[s]
                part_sum = [q[s][c] * center for c in range(5)]
                if carry is not None:
                    part_sum = [part_sum[c] + carry[s][c] for c in range(5)]
                wide = slice(s * LANES, (s + 1) * LANES)
                for c in range(5):
                    spread = q[s][c] * alpha2
                    moved = flux[s][1][c] * beta2
                    above = next_ref[i, c, pl.ds(j + 1, 1), :][:, wide]
                    below = prev_ref[i, c, pl.ds(j + SUB - 1, 1), :][:, wide]
                    up = pltpu.roll(spread - moved, SUB - 1, 0)
                    down = pltpu.roll(spread + moved, 1, 0)
                    part_sum[c] = part_sum[c] + (
                        jnp.where(last_row, above, up) + jnp.where(first_row, below, down)
                    )
                part_sum[2] = part_sum[2] - flux[s][1][3] * source
                part_sum[3] = part_sum[3] + flux[s][1][2] * source
                total.append(part_sum)
            carry = [[straight(q[s][c]) + flux[s][0][c] for c in range(5)] for s in range(strips)]
            for c in range(5):
                ups, downs, walls = [], [], None
                for s in range(strips):
                    spread = q[s][c] * radial_alpha
                    outward = spread + flux[s][2][c] * coefs[s][3]
                    ups.append(pltpu.roll(spread - flux[s][2][c] * coefs[s][2], LANES - 1, 1))
                    downs.append(pltpu.roll(outward, 1, 1))
                    walls = -outward if c == 3 else outward
                for s in range(strips):
                    up = jnp.where(last_lane, ups[s + 1] if s + 1 < strips else walls, ups[s])
                    down = jnp.where(first_lane, downs[s - 1] if s else 0.0, downs[s])
                    total[s][c] = total[s][c] + (up + down)
            held = total
        before = None
        if first + count < planes:
            before = [axial(q, -1.0) for q in load(first + count - lo)]
        finish(count - 1, held, before)

    def arrive(h):
        for s in range(strips):
            in_copy(h, s).wait()
        edges(h)

    arrive(0)
    for h in range(chunks):
        if h + 1 < chunks:
            arrive(h + 1)

        @pl.loop(h * chunk_tiles, (h + 1) * chunk_tiles)
        def _(j):
            tile(j)

        out_copy(h).start()
    for h in range(chunks):
        out_copy(h).wait()


def main_call(first, count, angle_step, cycle, after, base=None):
    channels, planes, sector, cells = cycle.shape
    held = min(first + count + 1, planes) - max(first - 1, 0)
    anywhere = pl.BlockSpec(memory_space=pl.ANY)
    args = [in_hbm(cycle), after]
    if base is not None:
        args.append(base)
    tiles = sector // SUB
    chunks = 4 if tiles % 4 == 0 else 1
    return pl.pallas_call(
        functools.partial(main_kernel, first, count, angle_step),
        out_shape=jax.ShapeDtypeStruct(cycle.shape, f32),
        in_specs=[anywhere] * len(args),
        out_specs=anywhere,
        input_output_aliases={} if base is None else {2: 0},
        scratch_shapes=[
            pltpu.VMEM((channels, held, cells // LANES, sector, LANES), f32),
            pltpu.VMEM((channels, count, sector, cells), f32),
            pltpu.VMEM((count, channels, tiles + SUB, cells), f32),
            pltpu.VMEM((count, channels, tiles + SUB, cells), f32),
            pltpu.SemaphoreType.DMA((chunks, cells // LANES)),
            pltpu.SemaphoreType.DMA((chunks,)),
        ],
        compiler_params=pltpu.CompilerParams(vmem_limit_bytes=GRANT),
        name="cycle_planes_%d" % first,
    )(*args)


def pick(total, values, lanes, weights):
    for k in range(lanes.shape[0]):
        index = jnp.broadcast_to(lanes[k : k + 1], values.shape)
        term = jnp.take_along_axis(values, index, axis=1, mode="promise_in_bounds") * weights[k : k + 1]
        total = term if total is None else total + term
    return total


def norm_rows(weights):
    total = weights[0:1]
    for k in range(1, weights.shape[0]):
        total = total + weights[k : k + 1]
    return weights / total


def angles_of(own, sector, count):
    lane = lax.broadcasted_iota(jnp.int32, (1, sector), 1) + own * sector
    angle = (lane.astype(f32) + 0.5) * (2.0 * math.pi / count)
    return jnp.cos(angle), jnp.sin(angle)


DEEP = 4
SLOT = 32


def outgoing_kernel(ring, cycle, core, taps, raw_weights, far_ref, near_ref, odd_ref, send_ref, keep_ref,
                    core_ref, taps_ref, weights_ref, strip_ref, cycle_rows, side_ref, turn_ref, ends_ref, lane_ref, weight_ref, share_ref, sems):
    channels, planes, sector, cells = cycle.shape
    core_rows, core_cells = core_ref.shape[2:]
    lead = channels * planes
    own = lax.axis_index("azim")
    parity = lax.rem(own, 2)
    ring_even = parity == 0
    near = jnp.where(lax.rem(lax.axis_index("axial"), 2) == 0, planes - 1, 0)
    far = planes - 1 - near
    lane = lax.broadcasted_iota(jnp.int32, (1, LANES), 1)
    per = LANES // DEEP
    strip = pltpu.make_async_copy(cycle.at[:, :, :, pl.ds(0, LANES)], strip_ref, sems.at[4])
    copies = [
        pltpu.make_async_copy(cycle.at[:, :, pl.ds(0, SUB)], cycle_rows.at[0], sems.at[0]),
        pltpu.make_async_copy(cycle.at[:, :, pl.ds(sector - SUB, SUB)], cycle_rows.at[1], sems.at[1]),
        pltpu.make_async_copy(cycle.at[:, far], far_ref.at[:, pl.ds(0, sector)], sems.at[2]),
        pltpu.make_async_copy(cycle.at[:, near], near_ref.at[:, pl.ds(0, sector)], sems.at[3]),
    ]
    early = [
        pltpu.make_async_copy(core, core_ref, sems.at[5]),
        pltpu.make_async_copy(taps, taps_ref, sems.at[6]),
        pltpu.make_async_copy(raw_weights, weights_ref, sems.at[7]),
    ]
    for copy in early:
        copy.start()
    strip.start()
    for copy in copies:
        copy.start()
    groups = ring // 2
    for copy in early:
        copy.wait()

    sides = []
    side_ref[...] = jnp.zeros_like(side_ref)
    strips = -(-core_cells // LANES)
    width = core_cells - (strips - 1) * LANES
    for side in range(2):
        start = 0 if side == 0 else (strips - 1) * LANES
        at = 0 if side == 0 else width - DEEP
        for part in range(-(-lead // per)):
            total = None
            for i in range(part * per, min(lead, (part + 1) * per)):
                block = core_ref[i // planes, i % planes, :, start : min(start + LANES, core_cells)]
                if block.shape[1] < LANES:
                    block = jnp.concatenate(
                        [block, jnp.zeros((core_rows, LANES - block.shape[1]), f32)], axis=1
                    )
                turn = (DEEP * (i - part * per) - at) % LANES
                moved = pltpu.roll(block, turn, 1) if turn else block
                total = moved if total is None else jnp.where(lane // DEEP == i - part * per, moved, total)
            side_ref[0:core_rows, :] = total
            turn_ref[part * LANES : (part + 1) * LANES, 0:SLOT] = jnp.transpose(side_ref[...])
        total = turn_ref[pl.ds(0, lead, stride=DEEP), :]
        for d in range(1, DEEP):
            moved = pltpu.roll(turn_ref[pl.ds(d, lead, stride=DEEP), :], d * SLOT, 1)
            total = jnp.where(lane // SLOT == d, moved, total)
        sides.append(jnp.where(lane < DEEP * SLOT, total, 0.0))

    weights = norm_rows(weights_ref[...])
    cell = taps_ref[...]
    row = ((cell.astype(f32) + 0.5) * (1.0 / core_cells)).astype(jnp.int32)
    column = cell - row * core_cells
    row = row - own * core_rows
    here = (row >= 0) & (row < core_rows)
    left = here & (column < DEEP)
    right = here & (column >= core_cells - DEEP)
    depth = jnp.where(column < DEEP, column, column - (core_cells - DEEP))
    lane_ref[0] = jnp.where(left | right, depth * SLOT + row, 0)
    weight_ref[0] = jnp.where(left, weights, 0.0)
    weight_ref[1] = jnp.where(right, weights, 0.0)

    @pl.loop(0, ring)
    def _(s):
        part = pl.ds(pl.multiple_of(s * sector, sector), sector)
        lanes = lane_ref[0, :, part]
        total = pick(None, sides[0], lanes, weight_ref[0, :, part])
        share_ref[:, part] = pick(total, sides[1], lanes, weight_ref[1, :, part])

    whole = (strips - 1) * DEEP
    pairs = ends_ref.shape[0] - whole
    fold = DEEP // pairs

    @pl.when((own == 0) | (own == ring - 1))
    def _():
        base = jnp.where(own == 0, 0, core_rows - DEEP)
        if fold * width < LANES:
            ends_ref[...] = jnp.zeros_like(ends_ref)
        for i in range(lead):
            plane = core_ref[i // planes, i % planes]
            rows = jnp.where(own == 0, plane[:DEEP], plane[core_rows - DEEP :])
            for d in range(DEEP):
                for s in range(strips - 1):
                    ends_ref[s * DEEP + d, i : i + 1, :] = rows[d : d + 1, s * LANES : (s + 1) * LANES]
                at = (d % fold) * width
                ends_ref[whole + d // fold, i : i + 1, at : at + width] = rows[d : d + 1, (strips - 1) * LANES :]
        inside = here & (column >= DEEP) & (column < core_cells - DEEP)
        depth = row - base
        inside = inside & (depth >= 0) & (depth < DEEP)
        tail = column >= (strips - 1) * LANES
        lane_ref[0] = jnp.where(
            inside, jnp.where(tail, column - (strips - 1) * LANES + (depth % fold) * width, column % LANES), 0
        )
        for d in range(DEEP):
            for s in range(strips - 1):
                strip = inside & (column >= s * LANES) & (column < (s + 1) * LANES) & (depth == d)
                weight_ref[s * DEEP + d] = jnp.where(strip, weights, 0.0)
        for d in range(pairs):
            strip = inside & tail & (depth >= d * fold) & (depth < (d + 1) * fold)
            weight_ref[whole + d] = jnp.where(strip, weights, 0.0)

        @pl.loop(0, ring)
        def _(s):
            part = pl.ds(pl.multiple_of(s * sector, sector), sector)
            lanes = lane_ref[0, :, part]
            total = share_ref[:, part]
            for d in range(whole + pairs):
                total = pick(total, ends_ref[d], lanes, weight_ref[d, :, part])
            share_ref[:, part] = total

    strip.wait()
    trace = None
    for i in range(lead):
        block = strip_ref[i // planes, i % planes]
        moved = pltpu.roll(block, i, 1) if i else block
        trace = moved if trace is None else jnp.where(lane == i, moved, trace)
    trace = jnp.transpose(trace)[:lead]
    cosine, sine = angles_of(own, sector, sector * ring)
    last = pl.ds(groups * sector, sector)
    azimuthal, radial = trace[2 * planes : 3 * planes], trace[3 * planes : 4 * planes]
    send_ref[0 : 2 * planes, last] = trace[0 : 2 * planes]
    send_ref[2 * planes : 3 * planes, last] = radial * cosine - azimuthal * sine
    send_ref[3 * planes : 4 * planes, last] = radial * sine + azimuthal * cosine
    send_ref[4 * planes :, last] = trace[4 * planes :]

    for g in range(groups):
        to = pl.ds(g * sector, sector)
        mine = pl.ds(pl.multiple_of((2 * g + parity) * sector, sector), sector)
        other = pl.ds(pl.multiple_of((2 * g + 1 - parity) * sector, sector), sector)
        keep_ref[:, to] = share_ref[:, mine]
        send_ref[:, to] = share_ref[:, other]

    for c in range(channels):
        near_ref[c, sector:, 0:core_cells] = core_ref[c, near]
        far_ref[c, sector:, 0:core_cells] = core_ref[c, far]
    for copy in copies:
        copy.wait()
    at = (groups + 1) * sector
    for c in range(channels):
        for x in range(planes):
            i = c * planes + x
            low = cycle_rows[0, c, x, 0:1, :]
            high = cycle_rows[1, c, x, SUB - 1 : SUB, :]
            send_ref[i : i + 1, at : at + cells] = jnp.where(ring_even, high, low)
            odd_ref[i : i + 1, 0:cells] = jnp.where(ring_even, low, high)
            low = core_ref[c, x, 0:1, :]
            high = core_ref[c, x, core_rows - 1 : core_rows, :]
            send_ref[i : i + 1, at + cells : at + cells + core_cells] = jnp.where(ring_even, high, low)
            odd_ref[i : i + 1, cells : cells + core_cells] = jnp.where(ring_even, low, high)


def outgoing_call(ring, cycle, core, taps, weights):
    channels, planes, sector, cells = cycle.shape
    core_rows, core_cells = core.shape[2:]
    lead = channels * planes
    groups = ring // 2
    strips = -(-core_cells // LANES)
    fold = 2 if 2 * (core_cells - (strips - 1) * LANES) <= LANES else 1
    slots = (strips - 1) * DEEP + DEEP // fold
    parts = -(-lead * DEEP // LANES)
    whole = pl.BlockSpec(memory_space=pltpu.VMEM)
    anywhere = pl.BlockSpec(memory_space=pl.ANY)
    edge = cells + strips * LANES
    plane = jax.ShapeDtypeStruct((channels, sector + core_rows, cells), f32)
    return pl.pallas_call(
        functools.partial(outgoing_kernel, ring),
        out_shape=(
            plane,
            plane,
            jax.ShapeDtypeStruct((lead, edge), f32),
            jax.ShapeDtypeStruct((lead, (groups + 1) * sector + edge), f32),
            jax.ShapeDtypeStruct((lead, groups * sector), f32),
        ),
        in_specs=[anywhere] * 4,
        out_specs=(whole,) * 5,
        scratch_shapes=[
            pltpu.VMEM(core.shape, f32),
            pltpu.VMEM(taps.shape, jnp.int32),
            pltpu.VMEM(weights.shape, f32),
            pltpu.VMEM((channels, planes, sector, LANES), f32),
            pltpu.VMEM((2, channels, planes, SUB, cells), f32),
            pltpu.VMEM((SLOT, LANES), f32),
            pltpu.VMEM((parts * LANES, LANES), f32),
            pltpu.VMEM((slots, lead, LANES), f32),
            pltpu.VMEM((1,) + taps.shape, jnp.int32),
            pltpu.VMEM((slots,) + taps.shape, f32),
            pltpu.VMEM((lead, ring * sector), f32),
            pltpu.SemaphoreType.DMA((8,)),
        ],
        compiler_params=pltpu.CompilerParams(vmem_limit_bytes=GRANT),
        name="outgoing",
    )(in_hbm(cycle), in_hbm(core), in_hbm(taps), in_hbm(weights))


def relay_kernel(groups, sent, kept, got, after, own_ref, *outs):
    sector = own_ref.shape[1] // 3
    own = lax.axis_index("azim")
    group = own // 2
    even = lax.rem(own, 2) == 0
    last = pl.ds(groups * sector, sector)
    mine, other = sent[:, last], got[:, last]
    first = jnp.where(even, mine, other)
    second = jnp.where(even, other, mine)
    for s in range(groups):
        to = own_ref if s == 0 else outs[s - 1]
        target = group ^ s
        part = pl.ds(pl.multiple_of(target * sector, sector), sector)
        to[:, 0:sector] = kept[:, part] + got[:, part]
        to[:, sector : 2 * sector] = first
        to[:, 2 * sector :] = second


def relay_call(ring, sector, sent, kept, got, after):
    groups = ring // 2
    whole = pl.BlockSpec(memory_space=pltpu.VMEM)
    block = jax.ShapeDtypeStruct((kept.shape[0], 3 * sector), f32)
    return pl.pallas_call(
        functools.partial(relay_kernel, groups),
        out_shape=(block,) * groups,
        in_specs=[whole] * 3 + [pl.BlockSpec(memory_space=pl.ANY)],
        out_specs=(whole,) * groups,
        compiler_params=pltpu.CompilerParams(vmem_limit_bytes=GRANT),
        name="ghost_relay",
    )(sent, kept, got, in_hbm(after))


def final_kernel(ring, core_ref, taps_ref, weights_ref, got_ref, odd_ref, near_ref, far_ref, partial, *rest):
    groups = ring // 2
    blocks = rest[:groups]
    (cycle_out, core_out, k_ref, next_ref, prev_ref, turn_ref, strip, wing, brim,
     in_sem, out_sem) = rest[groups:]
    channels, planes, sector, cells = cycle_out.shape
    core_rows, core_cells = core_ref.shape[2:]
    lead = channels * planes
    own = lax.axis_index("azim")
    group = own // 2
    ring_even = lax.rem(own, 2) == 0
    core_even = lax.rem(lax.axis_index("axial"), 2) == 0
    inner = pl.ds(0, LANES)
    outer = pl.ds(LANES, cells - LANES)
    middle = pl.ds(1, planes - 2)
    ends = (pl.ds(0, SUB), pl.ds(sector - SUB, SUB))

    def places(ref):
        found = [(ref.at[:, x, :, inner], strip.at[x]) for x in range(planes)]
        found += [(ref.at[:, x, :, outer], wing.at[n]) for n, x in enumerate((0, planes - 1))]
        found += [(ref.at[:, middle, ends[n], outer], brim.at[n]) for n in range(2)]
        return found

    def in_copies():
        return [
            pltpu.make_async_copy(a, b, in_sem.at[n]) for n, (a, b) in enumerate(places(partial))
        ]

    def out_copies():
        return [
            pltpu.make_async_copy(b, a, out_sem.at[n]) for n, (a, b) in enumerate(places(cycle_out))
        ]

    coming, leaving = in_copies(), out_copies()
    for copy in coming:
        copy.start()
    lane = lax.broadcasted_iota(jnp.int32, (1, LANES), 1)

    total = blocks[0][:, 0:sector]
    for s in range(1, groups):
        total = total + blocks[s][:, 0:sector]
    cosine, sine = angles_of(own, sector, sector * ring)
    q = [total[c * planes : (c + 1) * planes] for c in range(5)]
    q[2], q[3] = q[3] * cosine - q[2] * sine, q[2] * cosine + q[3] * sine
    u, pressure, enthalpy = velocities(q)
    inside = inner_radius - 0.5 * radial_step
    beta = RAD_BETA * inside / (inside + radial_step)
    _, after = to_sides(q, u, pressure, enthalpy, 3, RAD_ALPHA, beta)
    turn_ref[...] = jnp.zeros_like(turn_ref)
    for c in range(5):
        turn_ref[c * planes : (c + 1) * planes, :] = after[c]
    gift = jnp.transpose(turn_ref[...])

    taps, weights = taps_ref[...], norm_rows(weights_ref[...])
    ghosts = taps.shape[1]
    wide = 2 * LANES
    span = lax.broadcasted_iota(jnp.int32, (1, wide), 1)
    shift = own * core_rows
    side_end = jnp.where(own == 0, 2 * core_cells, 3 * core_cells)

    def targets(t):
        left = pltpu.roll(t, ghosts - shift, 1)[:, :wide]
        right = pltpu.roll(t, lax.rem(2 * ghosts + core_rows - core_cells - shift, ghosts), 1)[:, :wide]
        end = pltpu.roll(t, lax.rem(2 * ghosts + PAIR - side_end, ghosts), 1)[:, :wide]
        return jnp.where(span < core_rows, left, jnp.where(span < PAIR, right, end))

    taps, weights = targets(taps), targets(weights)
    lanes = taps % sector
    home = taps // sector
    found = [None, None]
    for s in range(groups):
        for y in range(2):
            values = blocks[s][:, (1 + y) * sector : (2 + y) * sector]
            masked = jnp.where(home == 2 * (group ^ s) + y, weights, 0.0)
            for h in range(2):
                part = slice(h * LANES, (h + 1) * LANES)
                found[h] = pick(found[h], values, lanes[:, part], masked[:, part])
    found = jnp.concatenate(found, axis=1)
    turn_ref[0:lead, :] = found[:, 0:LANES]
    sides = jnp.transpose(turn_ref[...])
    left_side = sides[0:core_rows]
    right_side = sides[core_rows : 2 * core_rows]
    found = found[:, PAIR : PAIR + core_cells]

    for x in range(planes):
        coming[x].wait()
        for c in range(5):
            i = c * planes + x
            moved = pltpu.roll(gift, (LANES - i) % LANES, 1)
            strip[x, c, :, :] += jnp.where(lane == 0, moved, 0.0)
    for copy in coming[planes:]:
        copy.wait()

    def sides(q):
        u, pressure, enthalpy = velocities(q)
        return to_sides(q, u, pressure, enthalpy, 1, AX_ALPHA, AX_BETA)

    @pl.loop(0, sector // SUB)
    def _(j):
        part = pl.ds(pl.multiple_of(j * SUB, SUB), SUB)
        near = [near_ref[c, part, :] for c in range(5)]
        far = [far_ref[c, part, :] for c in range(5)]
        _, low = sides([jnp.where(core_even, far[c], near[c]) for c in range(5)])
        high, _ = sides([jnp.where(core_even, near[c], far[c]) for c in range(5)])
        for n, value in enumerate((low, high)):
            for c in range(5):
                strip[n * (planes - 1), c, part, :] += value[c][:, :LANES]
                wing[n, c, part, :] += value[c][:, LANES:]

    _, radius_inv = radial_tables(cells)
    alpha2, beta2 = azim_coefs(radius_inv, 2.0 * math.pi / (sector * ring))
    def row_pair(start, width):
        pairs = []
        for c in range(5):
            odd = odd_ref[c * planes : (c + 1) * planes, start : start + width]
            even = got_ref[c * planes : (c + 1) * planes, edge + start : edge + start + width]
            pairs.append((jnp.where(ring_even, odd, even), jnp.where(ring_even, even, odd)))
        return [p[0] for p in pairs], [p[1] for p in pairs]

    edge = (groups + 1) * sector
    low, high = row_pair(0, cells)
    _, low = edge_rows(low, alpha2, beta2)
    high, _ = edge_rows(high, alpha2, beta2)
    for n, value in enumerate((low, high)):
        at = n * (sector - 1)
        small = n * (SUB - 1)
        for c in range(5):
            for x in range(planes):
                strip[x, c, at : at + 1, :] += value[c][x : x + 1, :LANES]
                rest_row = value[c][x : x + 1, LANES:]
                if 0 < x < planes - 1:
                    brim[n, c, x - 1, small : small + 1, :] += rest_row
                else:
                    wing[min(x, 1), c, at : at + 1, :] += rest_row
    for copy in leaving:
        copy.start()

    strips = k_ref.shape[2]
    padded = k_ref.shape[3]
    tail = strips * LANES - core_cells
    body = LANES - tail
    lows, highs = row_pair(cells, core_cells)
    for c in range(5):
        low, high = lows[c], highs[c]
        ends = found[c * planes : (c + 1) * planes]
        low = jnp.where(own == 0, ends, low)
        high = jnp.where(own == ring - 1, ends, high)
        for x in range(planes):
            i = c * planes + x
            for s in range(strips - 1):
                k_ref[c, x, s, 0:core_rows, :] = core_ref[c, x, :, s * LANES : (s + 1) * LANES]
            k_ref[c, x, strips - 1, 0:core_rows, 0:body] = core_ref[c, x, :, (strips - 1) * LANES :]
            pad = jnp.where(
                lane == LANES - 1,
                pltpu.roll(left_side, (LANES - 1 - i) % LANES, 1),
                pltpu.roll(right_side, (body - i) % LANES, 1),
            )
            k_ref[c, x, strips - 1, 0:core_rows, body:] = pad[:, body:]
            for row, value in ((core_rows, high), (padded - 1, low)):
                for s in range(strips - 1):
                    k_ref[c, x, s, row : row + 1, :] = value[x : x + 1, s * LANES : (s + 1) * LANES]
                k_ref[c, x, strips - 1, row : row + 1, 0:body] = value[x : x + 1, (strips - 1) * LANES :]

    def load(c, x, part):
        return jnp.concatenate([k_ref[c, x, s, part, :] for s in range(strips)], axis=1)

    tiles = padded // SUB
    for x in range(planes):
        start = [load(c, x, pl.ds(0, tiles, stride=SUB)) for c in range(5)]
        before, _ = edge_rows(start, CORE_ALPHA, CORE_BETA)
        end = [load(c, x, pl.ds(SUB - 1, tiles, stride=SUB)) for c in range(5)]
        _, after = edge_rows(end, CORE_ALPHA, CORE_BETA)
        for c in range(5):
            next_ref[x, c, 0:tiles, :] = before[c]
            prev_ref[x, c, SUB : SUB + tiles, :] = after[c]
            prev_ref[x, c, SUB - 1 : SUB, :] = after[c][tiles - 1 : tiles]

    row = lax.broadcasted_iota(jnp.int32, (SUB, 1), 0)
    center = 1.0 - 2.0 * AX_ALPHA - 4.0 * CORE_ALPHA
    full = strips * LANES
    for j in range(-(-core_rows // SUB)):
        size = min(SUB, core_rows - j * SUB)
        part = pl.ds(j * SUB, SUB)
        here = pl.ds(j * SUB, size)

        def outside(ref):
            q = [ref[c, pl.ds(sector + j * SUB, size), 0:core_cells] for c in range(5)]
            u, pressure, enthalpy = velocities(q)
            return to_sides(q, u, pressure, enthalpy, 1, AX_ALPHA, AX_BETA)

        near_before, near_after = outside(near_ref)
        far_before, far_after = outside(far_ref)
        from_low = [jnp.where(core_even, a, b) for a, b in zip(far_after, near_after)]
        from_high = [jnp.where(core_even, a, b) for a, b in zip(near_before, far_before)]
        carry, held = None, None
        for x in range(planes):
            q = [load(c, x, part) for c in range(5)]
            u, pressure, enthalpy = velocities(q)
            before, after = to_sides(q, u, pressure, enthalpy, 1, AX_ALPHA, AX_BETA)
            if held is not None:
                for c in range(5):
                    core_out[c, x - 1, here, :] = (held[c] + before[c])[:size, :core_cells]
            result = [q[c] * center for c in range(5)]
            if carry is not None:
                result = [result[c] + carry[c] for c in range(5)]
            carry = after
            before, after = to_sides(q, u, pressure, enthalpy, 2, CORE_ALPHA, CORE_BETA)
            for c in range(5):
                above = next_ref[x, c, pl.ds((j + 1) % tiles, 1), :]
                below = prev_ref[x, c, pl.ds(j + SUB - 1, 1), :]
                up = pltpu.roll(before[c], SUB - 1, 0)
                down = pltpu.roll(after[c], 1, 0)
                result[c] = result[c] + (
                    jnp.where(row == SUB - 1, above, up) + jnp.where(row == 0, below, down)
                )
            before, after = to_sides(q, u, pressure, enthalpy, 3, CORE_ALPHA, CORE_BETA)
            for c in range(5):
                result[c] = result[c] + (
                    pltpu.roll(before[c], full - 1, 1) + pltpu.roll(after[c], 1, 1)
                )
            held = result
        for c in range(5):
            core_out[c, planes - 1, here, :] = held[c][:size, :core_cells] + from_high[c]
            core_out[c, 0, here, :] += from_low[c]

    for copy in leaving:
        copy.wait()


def final_call(ring, core, taps, weights, got, odd, near, far, partial, blocks):
    channels, planes, sector, cells = partial.shape
    core_rows, core_cells = core.shape[2:]
    strips = -(-(core_cells + 2) // LANES)
    padded = -(-(core_rows + 2) // SUB) * SUB
    whole = pl.BlockSpec(memory_space=pltpu.VMEM)
    anywhere = pl.BlockSpec(memory_space=pltpu.HBM)
    groups = ring // 2
    edge_shape = (planes, channels, 2 * SUB, strips * LANES)
    return pl.pallas_call(
        functools.partial(final_kernel, ring),
        out_shape=(
            jax.ShapeDtypeStruct(partial.shape, f32),
            jax.ShapeDtypeStruct(core.shape, f32),
        ),
        in_specs=[whole] * 7 + [anywhere] + [whole] * groups,
        out_specs=(anywhere, whole),
        input_output_aliases={7: 0},
        scratch_shapes=[
            pltpu.VMEM((channels, planes, strips, padded, LANES), f32),
            pltpu.VMEM(edge_shape, f32),
            pltpu.VMEM(edge_shape, f32),
            pltpu.VMEM((LANES, LANES), f32),
            pltpu.VMEM((planes, channels, sector, LANES), f32),
            pltpu.VMEM((2, channels, sector, cells - LANES), f32),
            pltpu.VMEM((2, channels, planes - 2, SUB, cells - LANES), f32),
            pltpu.SemaphoreType.DMA((planes + 4,)),
            pltpu.SemaphoreType.DMA((planes + 4,)),
        ],
        compiler_params=pltpu.CompilerParams(vmem_limit_bytes=GRANT),
        name="late_terms",
    )(core, taps, weights, got, odd, near, far, partial, *blocks)


def body(cycle, core, core_taps, core_weights, cycle_taps, cycle_weights):
    planes, sector = cycle.shape[1:3]
    ring = lax.axis_size("azim")
    length = lax.axis_size("axial")
    angle_step = 2.0 * math.pi / (sector * ring)
    even_axial = [(i, i ^ 1) for i in range(length)]
    odd_axial = [(i, (i + 1) % length) for i in range(1, length, 2)]
    odd_axial += [(b, a) for a, b in odd_axial]
    even_azim = [(i, i ^ 1) for i in range(ring)]
    odd_azim = [(i, (i + 1) % ring) for i in range(1, ring, 2)]
    odd_azim += [(b, a) for a, b in odd_azim]
    far, near, odd, sent, kept = outgoing_call(ring, cycle, core, cycle_taps.T, cycle_weights.T)
    got = lax.ppermute(sent, "azim", even_azim)
    far = lax.ppermute(far, "axial", odd_axial)
    near = lax.ppermute(near, "axial", even_axial)
    odd = lax.ppermute(odd, "azim", odd_azim)
    half = planes // 2
    partial = main_call(0, half, angle_step, cycle, kept)
    blocks = list(relay_call(ring, sector, sent, kept, got, partial))
    partial = main_call(half, planes - half, angle_step, cycle, blocks[0], partial)
    for s in range(1, ring // 2):
        blocks[s] = lax.ppermute(blocks[s], "azim", [(i, i ^ (2 * s)) for i in range(ring)])
    return tuple(
        final_call(ring, core, core_taps.T, core_weights.T, got, odd, near, far, partial, blocks)
    )


def solution(mesh):
    placed = (P(None, "axial", "azim", None), P(None, "axial", "azim", None), P(), P(), P(), P())
    return jax.shard_map(
        body,
        mesh=mesh,
        in_specs=placed,
        out_specs=(P(None, "axial", "azim", None), P(None, "axial", "azim", None)),
        check_vma=False,
    )
```

```python
import functools
import math

import jax
import jax.numpy as jnp
from jax import lax
from jax.experimental import pallas as pl
from jax.experimental.pallas import tpu as pltpu
from jax.sharding import PartitionSpec as P

time_step = 0.001
axial_step = 0.004
radial_step = 1.0 / 256.0
core_step = 2.0 / 192.0
inner_radius = 1.0
viscosity = 0.002
gamma_minus = 0.4

LANES = 128
SUB = 8
PAIR = 64
GRANT = 16 * 1024 * 1024


def in_hbm(x):
    return pltpu.with_memory_space_constraint(x, pltpu.HBM)


def in_vmem(x):
    return pltpu.with_memory_space_constraint(x, pltpu.VMEM)
f32 = jnp.float32
AX_ALPHA = time_step * viscosity / (axial_step * axial_step)
AX_BETA = time_step / (2.0 * axial_step)
RAD_ALPHA = time_step * viscosity / (radial_step * radial_step)
RAD_BETA = time_step / (2.0 * radial_step)
CORE_ALPHA = time_step * viscosity / (core_step * core_step)
CORE_BETA = time_step / (2.0 * core_step)


def velocities(q):
    inv = 1.0 / q[0]
    u = (q[1] * inv, q[2] * inv, q[3] * inv)
    kinetic = 0.5 * (q[1] * u[0] + q[2] * u[1] + q[3] * u[2])
    pressure = gamma_minus * (q[4] - kinetic)
    return u, pressure, q[4] + pressure


def scaled_flux(q, u, pressure, enthalpy, k, scale):
    su = u[k - 1] * scale
    parts = [q[k] * scale, q[1] * su, q[2] * su, q[3] * su, enthalpy * su]
    parts[k] = parts[k] + pressure * scale
    return parts


def to_sides(q, u, pressure, enthalpy, k, alpha, beta):
    flux = scaled_flux(q, u, pressure, enthalpy, k, beta)
    before, after = [], []
    for c in range(5):
        spread = q[c] * alpha
        before.append(spread - flux[c])
        after.append(spread + flux[c])
    return before, after


def radial_tables(cells):
    lane = lax.broadcasted_iota(jnp.int32, (1, cells), 1).astype(f32)
    radius = inner_radius + (lane + 0.5) * radial_step
    return radius, 1.0 / radius


def azim_coefs(radius_inv, angle_step):
    arc_inv = radius_inv * (1.0 / angle_step)
    return (time_step * viscosity) * arc_inv * arc_inv, (0.5 * time_step) * arc_inv


def edge_rows(q, alpha, beta):
    u, pressure, enthalpy = velocities(q)
    return to_sides(q, u, pressure, enthalpy, 2, alpha, beta)


def all_fluxes(q):
    inv = 1.0 / q[0]
    u1, u2, u3 = q[1] * inv, q[2] * inv, q[3] * inv
    m11, m22, m33 = q[1] * u1, q[2] * u2, q[3] * u3
    m12, m13, m23 = q[1] * u2, q[1] * u3, q[2] * u3
    pressure = gamma_minus * (q[4] - 0.5 * (m11 + m22 + m33))
    enthalpy = q[4] + pressure
    return (
        [q[1], m11 + pressure, m12, m13, enthalpy * u1],
        [q[2], m12, m22 + pressure, m23, enthalpy * u2],
        [q[3], m13, m23, m33 + pressure, enthalpy * u3],
    )


def main_kernel(first, count, angle_step, q_ref, after, *rest):
    out_ref, next_ref, prev_ref = rest[0], rest[-2], rest[-1]
    if len(rest) > 3:
        rest[1][...] = after[...]
    planes, strips, sector = q_ref.shape[1:4]
    cells = strips * LANES
    unit = 1.0 / AX_BETA
    lane = lax.broadcasted_iota(jnp.int32, (1, LANES), 1)
    first_lane = lane == 0
    last_lane = lane == LANES - 1
    row = lax.broadcasted_iota(jnp.int32, (SUB, 1), 0)
    first_row = row == 0
    last_row = row == SUB - 1
    coefs = []
    for s in range(strips):
        radius = inner_radius + ((lane + s * LANES).astype(f32) + 0.5) * radial_step
        radius_inv = 1.0 / radius
        alpha2, beta2 = azim_coefs(radius_inv, angle_step)
        beta_before = RAD_BETA * radius / (radius - radial_step)
        beta_after = RAD_BETA * radius / (radius + radial_step)
        if s == strips - 1:
            wall = RAD_BETA * (radius + radial_step) / radius
            beta_after = jnp.where(last_lane, wall, beta_after)
        center = 1.0 - 2.0 * AX_ALPHA - 2.0 * RAD_ALPHA - 2.0 * alpha2
        table = (alpha2, beta2, beta_before, beta_after, center, time_step * radius_inv)
        coefs.append([jnp.broadcast_to(t * unit, (SUB, LANES)) for t in table])
    ratio = AX_ALPHA / AX_BETA
    radial_alpha = RAD_ALPHA * unit

    tiles = sector // SUB
    zero = jnp.zeros((1, cells), f32)
    for i in range(count):
        for c in range(5):
            prev_ref[i, c, SUB - 1 : SUB, :] = zero
            next_ref[i, c, tiles : tiles + 1, :] = zero

    for i in range(count):
        for s in range(strips):
            alpha2, beta2 = coefs[s][0][:1], coefs[s][1][:1]
            wide = slice(s * LANES, (s + 1) * LANES)
            q = [q_ref[c, first + i, s, pl.ds(0, tiles, stride=SUB), :] for c in range(5)]
            before, _ = edge_rows(q, alpha2, beta2)
            q = [q_ref[c, first + i, s, pl.ds(SUB - 1, tiles, stride=SUB), :] for c in range(5)]
            _, after = edge_rows(q, alpha2, beta2)
            for c in range(5):
                next_ref[i, c, 0:tiles, wide] = before[c]
                prev_ref[i, c, SUB : SUB + tiles, wide] = after[c]

    def straight(q):
        return q if abs(ratio - 1.0) < 1e-9 else q * ratio

    def tile(j):
        part = pl.ds(pl.multiple_of(j * SUB, SUB), SUB)

        def load(x):
            return [[q_ref[c, x, s, part, :] for c in range(5)] for s in range(strips)]

        def axial(q, sign):
            flux = all_fluxes(q)[0]
            return [straight(q[c]) + sign * flux[c] for c in range(5)]

        def finish(i, held, before):
            for s in range(strips):
                for c in range(5):
                    value = held[s][c] if before is None else held[s][c] + before[s][c]
                    out_ref[c, i, part, s * LANES : (s + 1) * LANES] = value * AX_BETA

        carry = [axial(q, 1.0) for q in load(first - 1)] if first > 0 else None
        held = None
        for i in range(count):
            q = load(first + i)
            flux = [all_fluxes(q[s]) for s in range(strips)]
            if held is not None:
                finish(
                    i - 1,
                    held,
                    [[straight(q[s][c]) - flux[s][0][c] for c in range(5)] for s in range(strips)],
                )
            total = []
            for s in range(strips):
                alpha2, beta2, _, _, center, source = coefs[s]
                part_sum = [q[s][c] * center for c in range(5)]
                if carry is not None:
                    part_sum = [part_sum[c] + carry[s][c] for c in range(5)]
                wide = slice(s * LANES, (s + 1) * LANES)
                for c in range(5):
                    spread = q[s][c] * alpha2
                    moved = flux[s][1][c] * beta2
                    above = next_ref[i, c, pl.ds(j + 1, 1), :][:, wide]
                    below = prev_ref[i, c, pl.ds(j + SUB - 1, 1), :][:, wide]
                    up = pltpu.roll(spread - moved, SUB - 1, 0)
                    down = pltpu.roll(spread + moved, 1, 0)
                    part_sum[c] = part_sum[c] + (
                        jnp.where(last_row, above, up) + jnp.where(first_row, below, down)
                    )
                part_sum[2] = part_sum[2] - flux[s][1][3] * source
                part_sum[3] = part_sum[3] + flux[s][1][2] * source
                total.append(part_sum)
            carry = [[straight(q[s][c]) + flux[s][0][c] for c in range(5)] for s in range(strips)]
            for c in range(5):
                ups, downs, walls = [], [], None
                for s in range(strips):
                    spread = q[s][c] * radial_alpha
                    outward = spread + flux[s][2][c] * coefs[s][3]
                    ups.append(pltpu.roll(spread - flux[s][2][c] * coefs[s][2], LANES - 1, 1))
                    downs.append(pltpu.roll(outward, 1, 1))
                    walls = -outward if c == 3 else outward
                for s in range(strips):
                    up = jnp.where(last_lane, ups[s + 1] if s + 1 < strips else walls, ups[s])
                    down = jnp.where(first_lane, downs[s - 1] if s else 0.0, downs[s])
                    total[s][c] = total[s][c] + (up + down)
            held = total
        before = None
        if first + count < planes:
            before = [axial(q, -1.0) for q in load(first + count)]
        finish(count - 1, held, before)

    @pl.loop(0, tiles)
    def _(j):
        tile(j)


def main_call(first, count, angle_step, held, after, handed_on):
    channels, planes, strips, sector = held.shape[:4]
    cells = strips * LANES
    whole = pl.BlockSpec(memory_space=pltpu.VMEM)
    edge = (count, channels, sector // SUB + SUB, cells)
    shapes = [pltpu.VMEM((channels, count, sector, cells), f32)]
    if handed_on:
        shapes.append(jax.ShapeDtypeStruct(after.shape, f32))
    return pl.pallas_call(
        functools.partial(main_kernel, first, count, angle_step),
        out_shape=tuple(shapes),
        in_specs=[whole, whole if handed_on else pl.BlockSpec(memory_space=pl.ANY)],
        out_specs=(whole,) * len(shapes),
        scratch_shapes=[pltpu.VMEM(edge, f32), pltpu.VMEM(edge, f32)],
        compiler_params=pltpu.CompilerParams(vmem_limit_bytes=GRANT),
        name="cycle_planes_%d" % first,
    )(in_vmem(held), after)


def pick(total, values, lanes, weights):
    for k in range(lanes.shape[0]):
        index = jnp.broadcast_to(lanes[k : k + 1], values.shape)
        term = jnp.take_along_axis(values, index, axis=1, mode="promise_in_bounds") * weights[k : k + 1]
        total = term if total is None else total + term
    return total


def norm_rows(weights):
    total = weights[0:1]
    for k in range(1, weights.shape[0]):
        total = total + weights[k : k + 1]
    return weights / total


def angles_of(own, sector, count):
    lane = lax.broadcasted_iota(jnp.int32, (1, sector), 1) + own * sector
    angle = (lane.astype(f32) + 0.5) * (2.0 * math.pi / count)
    return jnp.cos(angle), jnp.sin(angle)


DEEP = 4
SLOT = 32


def outgoing_kernel(ring, cycle, core, taps, raw_weights, held_ref, far_ref, near_ref, odd_ref, send_ref,
                    keep_ref, core_ref, taps_ref, weights_ref, side_ref, turn_ref, vals_ref, lane_ref,
                    weight_ref, flag_ref, used_ref, share_ref, sems):
    channels, planes, sector, cells = cycle.shape
    core_rows, core_cells = core_ref.shape[2:]
    lead = channels * planes
    own = lax.axis_index("azim")
    parity = lax.rem(own, 2)
    ring_even = parity == 0
    near = jnp.where(lax.rem(lax.axis_index("axial"), 2) == 0, planes - 1, 0)
    far = planes - 1 - near
    lane = lax.broadcasted_iota(jnp.int32, (1, LANES), 1)
    per = LANES // DEEP
    early = [
        pltpu.make_async_copy(core, core_ref, sems.at[0]),
        pltpu.make_async_copy(taps, taps_ref, sems.at[1]),
        pltpu.make_async_copy(raw_weights, weights_ref, sems.at[2]),
    ]
    cycle_strips = cells // LANES
    copies = [
        pltpu.make_async_copy(
            cycle.at[:, :, :, pl.ds(n * LANES, LANES)], held_ref.at[:, :, n], sems.at[3 + n]
        )
        for n in range(cycle_strips)
    ]
    for copy in early + copies:
        copy.start()
    groups = ring // 2
    for copy in early:
        copy.wait()

    sides = []
    side_ref[...] = jnp.zeros_like(side_ref)
    strips = -(-core_cells // LANES)
    width = core_cells - (strips - 1) * LANES
    for side in range(2):
        start = 0 if side == 0 else (strips - 1) * LANES
        at = 0 if side == 0 else width - DEEP
        for part in range(-(-lead // per)):
            total = None
            for i in range(part * per, min(lead, (part + 1) * per)):
                block = core_ref[i // planes, i % planes, :, start : min(start + LANES, core_cells)]
                if block.shape[1] < LANES:
                    block = jnp.concatenate(
                        [block, jnp.zeros((core_rows, LANES - block.shape[1]), f32)], axis=1
                    )
                turn = (DEEP * (i - part * per) - at) % LANES
                moved = pltpu.roll(block, turn, 1) if turn else block
                total = moved if total is None else jnp.where(lane // DEEP == i - part * per, moved, total)
            side_ref[0:core_rows, :] = total
            turn_ref[part * LANES : (part + 1) * LANES, 0:SLOT] = jnp.transpose(side_ref[...])
        total = turn_ref[pl.ds(0, lead, stride=DEEP), :]
        for d in range(1, DEEP):
            moved = pltpu.roll(turn_ref[pl.ds(d, lead, stride=DEEP), :], d * SLOT, 1)
            total = jnp.where(lane // SLOT == d, moved, total)
        sides.append(jnp.where(lane < DEEP * SLOT, total, 0.0))

    whole = (strips - 1) * DEEP
    slots = vals_ref.shape[0]
    pairs = slots - 2 - whole
    fold = DEEP // pairs
    vals_ref[0] = sides[0]
    vals_ref[1] = sides[1]
    at_end = (own == 0) | (own == ring - 1)
    base = jnp.where(own == 0, 0, core_rows - DEEP)

    @pl.when(at_end)
    def _():
        if fold * width < LANES:
            vals_ref[2:] = jnp.zeros((slots - 2, lead, LANES), f32)
        for i in range(lead):
            plane = core_ref[i // planes, i % planes]
            rows = jnp.where(own == 0, plane[:DEEP], plane[core_rows - DEEP :])
            for d in range(DEEP):
                for s in range(strips - 1):
                    vals_ref[2 + s * DEEP + d, i : i + 1, :] = rows[d : d + 1, s * LANES : (s + 1) * LANES]
                at = (d % fold) * width
                vals_ref[2 + whole + d // fold, i : i + 1, at : at + width] = rows[d : d + 1, (strips - 1) * LANES :]

    weights = norm_rows(weights_ref[...])
    cell = taps_ref[...]
    row = ((cell.astype(f32) + 0.5) * (1.0 / core_cells)).astype(jnp.int32)
    column = cell - row * core_cells
    row = row - own * core_rows
    here = (row >= 0) & (row < core_rows)
    left = column < DEEP
    right = column >= core_cells - DEEP
    side_lane = jnp.where(left, column, column - (core_cells - DEEP)) * SLOT + row
    depth = row - base
    tail = column >= (strips - 1) * LANES
    end_slot = jnp.where(tail, whole + depth // fold, (column // LANES) * DEEP + depth) + 2
    end_lane = jnp.where(tail, column - (strips - 1) * LANES + (depth % fold) * width, column % LANES)
    inside = here & at_end & (depth >= 0) & (depth < DEEP)
    slot = jnp.where(here & left, 0, jnp.where(here & right, 1, jnp.where(inside, end_slot, slots)))
    lane_ref[...] = jnp.where(slot < 2, side_lane, jnp.where(slot < slots, end_lane, 0))
    for d in range(slots):
        mine = jnp.where(slot == d, weights, 0.0)
        weight_ref[d] = mine
        flag_ref[d : d + 1, :] = jnp.max(mine, axis=0, keepdims=True)
    power = jnp.left_shift(1, lax.broadcasted_iota(jnp.int32, (slots, 1), 0)).astype(f32)
    for s in range(ring):
        most = jnp.max(flag_ref[:, s * sector : (s + 1) * sector], axis=1, keepdims=True)
        used_ref[s] = jnp.sum(jnp.where(most > 0.0, power, 0.0)).astype(jnp.int32)

    @pl.loop(0, ring)
    def _(s):
        part = pl.ds(pl.multiple_of(s * sector, sector), sector)
        share_ref[:, part] = jnp.zeros((lead, sector), f32)
        used = used_ref[s]

        def add(d):
            @pl.when(lax.rem(lax.div(used, 1 << d), 2) == 1)
            def _():
                share_ref[:, part] = pick(
                    share_ref[:, part], vals_ref[d], lane_ref[:, part], weight_ref[d, :, part]
                )

        add(0)
        add(1)

        @pl.when(used > 3)
        def _():
            for d in range(2, slots):
                add(d)

    copies[0].wait()
    trace = None
    for i in range(lead):
        block = held_ref[i // planes, i % planes, 0]
        moved = pltpu.roll(block, i, 1) if i else block
        trace = moved if trace is None else jnp.where(lane == i, moved, trace)
    trace = jnp.transpose(trace)[:lead]
    cosine, sine = angles_of(own, sector, sector * ring)
    last = pl.ds(groups * sector, sector)
    azimuthal, radial = trace[2 * planes : 3 * planes], trace[3 * planes : 4 * planes]
    send_ref[0 : 2 * planes, last] = trace[0 : 2 * planes]
    send_ref[2 * planes : 3 * planes, last] = radial * cosine - azimuthal * sine
    send_ref[3 * planes : 4 * planes, last] = radial * sine + azimuthal * cosine
    send_ref[4 * planes :, last] = trace[4 * planes :]

    for g in range(groups):
        to = pl.ds(g * sector, sector)
        mine = pl.ds(pl.multiple_of((2 * g + parity) * sector, sector), sector)
        other = pl.ds(pl.multiple_of((2 * g + 1 - parity) * sector, sector), sector)
        keep_ref[:, to] = share_ref[:, mine]
        send_ref[:, to] = share_ref[:, other]

    for c in range(channels):
        near_ref[c, sector:, 0:core_cells] = core_ref[c, near]
        far_ref[c, sector:, 0:core_cells] = core_ref[c, far]
    for copy in copies[1:]:
        copy.wait()
    for c in range(channels):
        for n in range(cycle_strips):
            wide = slice(n * LANES, (n + 1) * LANES)
            near_ref[c, 0:sector, wide] = held_ref[c, near, n]
            far_ref[c, 0:sector, wide] = held_ref[c, far, n]
    at = (groups + 1) * sector
    for c in range(channels):
        for x in range(planes):
            i = c * planes + x
            for n in range(cycle_strips):
                low = held_ref[c, x, n, 0:1, :]
                high = held_ref[c, x, n, sector - 1 : sector, :]
                start = n * LANES
                send_ref[i : i + 1, at + start : at + start + LANES] = jnp.where(ring_even, high, low)
                odd_ref[i : i + 1, start : start + LANES] = jnp.where(ring_even, low, high)
            low = core_ref[c, x, 0:1, :]
            high = core_ref[c, x, core_rows - 1 : core_rows, :]
            send_ref[i : i + 1, at + cells : at + cells + core_cells] = jnp.where(ring_even, high, low)
            odd_ref[i : i + 1, cells : cells + core_cells] = jnp.where(ring_even, low, high)


def outgoing_call(ring, cycle, core, taps, weights):
    channels, planes, sector, cells = cycle.shape
    core_rows, core_cells = core.shape[2:]
    lead = channels * planes
    groups = ring // 2
    strips = -(-core_cells // LANES)
    fold = 2 if 2 * (core_cells - (strips - 1) * LANES) <= LANES else 1
    slots = 2 + (strips - 1) * DEEP + DEEP // fold
    parts = -(-lead * DEEP // LANES)
    whole = pl.BlockSpec(memory_space=pltpu.VMEM)
    anywhere = pl.BlockSpec(memory_space=pl.ANY)
    edge = cells + strips * LANES
    plane = jax.ShapeDtypeStruct((channels, sector + core_rows, cells), f32)
    return pl.pallas_call(
        functools.partial(outgoing_kernel, ring),
        out_shape=(
            pltpu.VMEM((channels, planes, cells // LANES, sector, LANES), f32),
            plane,
            plane,
            jax.ShapeDtypeStruct((lead, edge), f32),
            jax.ShapeDtypeStruct((lead, (groups + 1) * sector + edge), f32),
            jax.ShapeDtypeStruct((lead, groups * sector), f32),
        ),
        in_specs=[anywhere] * 4,
        out_specs=(whole,) * 6,
        scratch_shapes=[
            pltpu.VMEM(core.shape, f32),
            pltpu.VMEM(taps.shape, jnp.int32),
            pltpu.VMEM(weights.shape, f32),
            pltpu.VMEM((SLOT, LANES), f32),
            pltpu.VMEM((parts * LANES, LANES), f32),
            pltpu.VMEM((slots, lead, LANES), f32),
            pltpu.VMEM(taps.shape, jnp.int32),
            pltpu.VMEM((slots,) + taps.shape, f32),
            pltpu.VMEM((slots, taps.shape[1]), f32),
            pltpu.SMEM((ring,), jnp.int32),
            pltpu.VMEM((lead, ring * sector), f32),
            pltpu.SemaphoreType.DMA((3 + cells // LANES,)),
        ],
        compiler_params=pltpu.CompilerParams(vmem_limit_bytes=GRANT),
        cost_estimate=pl.CostEstimate(flops=0, bytes_accessed=16 * 1024 * 1024, transcendentals=0),
        name="outgoing",
    )(in_hbm(cycle), in_hbm(core), in_hbm(taps), in_hbm(weights))


def relay_kernel(groups, sent, kept, got, after, own_ref, *outs):
    sector = own_ref.shape[1] // 3
    own = lax.axis_index("azim")
    group = own // 2
    even = lax.rem(own, 2) == 0
    last = pl.ds(groups * sector, sector)
    mine, other = sent[:, last], got[:, last]
    first = jnp.where(even, mine, other)
    second = jnp.where(even, other, mine)
    for s in range(groups):
        to = own_ref if s == 0 else outs[s - 1]
        target = group ^ s
        part = pl.ds(pl.multiple_of(target * sector, sector), sector)
        to[:, 0:sector] = kept[:, part] + got[:, part]
        to[:, sector : 2 * sector] = first
        to[:, 2 * sector :] = second


def relay_call(ring, sector, sent, kept, got, after):
    groups = ring // 2
    whole = pl.BlockSpec(memory_space=pltpu.VMEM)
    block = jax.ShapeDtypeStruct((kept.shape[0], 3 * sector), f32)
    return pl.pallas_call(
        functools.partial(relay_kernel, groups),
        out_shape=(block,) * groups,
        in_specs=[whole] * 3 + [pl.BlockSpec(memory_space=pl.ANY)],
        out_specs=(whole,) * groups,
        compiler_params=pltpu.CompilerParams(vmem_limit_bytes=GRANT),
        name="ghost_relay",
    )(sent, kept, got, after)


def final_kernel(ring, core_ref, taps_ref, weights_ref, got_ref, odd_ref, near_ref, far_ref, lower, upper, *rest):
    groups = ring // 2
    blocks = rest[:groups]
    (cycle_out, core_out, k_ref, next_ref, prev_ref, turn_ref, found_ref, strip, wing, brim,
     out_sem) = rest[groups:]
    channels, planes, sector, cells = cycle_out.shape
    core_rows, core_cells = core_ref.shape[2:]
    lead = channels * planes
    own = lax.axis_index("azim")
    group = own // 2
    ring_even = lax.rem(own, 2) == 0
    core_even = lax.rem(lax.axis_index("axial"), 2) == 0
    inner = pl.ds(0, LANES)
    outer = pl.ds(LANES, cells - LANES)
    middle = pl.ds(1, planes - 2)
    ends = (pl.ds(0, SUB), pl.ds(sector - SUB, SUB))

    half = lower.shape[1]

    def block(x):
        return (lower, x) if x < half else (upper, x - half)

    bulk = pl.ds(SUB, sector - 2 * SUB)
    places = [
        (lower.at[:, pl.ds(1, half - 1), bulk, outer], cycle_out.at[:, pl.ds(1, half - 1), bulk, outer]),
        (
            upper.at[:, pl.ds(0, planes - 1 - half), bulk, outer],
            cycle_out.at[:, pl.ds(half, planes - 1 - half), bulk, outer],
        ),
    ]
    places += [(strip.at[x], cycle_out.at[:, x, :, inner]) for x in range(planes)]
    places += [(wing.at[n], cycle_out.at[:, x, :, outer]) for n, x in enumerate((0, planes - 1))]
    places += [(brim.at[n], cycle_out.at[:, middle, ends[n], outer]) for n in range(2)]
    leaving = [
        pltpu.make_async_copy(a, b, out_sem.at[n]) for n, (a, b) in enumerate(places)
    ]
    for copy in leaving[:2]:
        copy.start()
    lane = lax.broadcasted_iota(jnp.int32, (1, LANES), 1)

    total = blocks[0][:, 0:sector]
    for s in range(1, groups):
        total = total + blocks[s][:, 0:sector]
    cosine, sine = angles_of(own, sector, sector * ring)
    q = [total[c * planes : (c + 1) * planes] for c in range(5)]
    q[2], q[3] = q[3] * cosine - q[2] * sine, q[2] * cosine + q[3] * sine
    u, pressure, enthalpy = velocities(q)
    inside = inner_radius - 0.5 * radial_step
    beta = RAD_BETA * inside / (inside + radial_step)
    _, after = to_sides(q, u, pressure, enthalpy, 3, RAD_ALPHA, beta)
    turn_ref[...] = jnp.zeros_like(turn_ref)
    for c in range(5):
        turn_ref[c * planes : (c + 1) * planes, :] = after[c]
    gift = jnp.transpose(turn_ref[...])

    taps, weights = taps_ref[...], norm_rows(weights_ref[...])
    ghosts = taps.shape[1]
    wide = 2 * LANES
    span = lax.broadcasted_iota(jnp.int32, (1, wide), 1)
    shift = own * core_rows
    side_end = jnp.where(own == 0, 2 * core_cells, 3 * core_cells)

    def targets(t):
        left = pltpu.roll(t, ghosts - shift, 1)[:, :wide]
        right = pltpu.roll(t, lax.rem(2 * ghosts + core_rows - core_cells - shift, ghosts), 1)[:, :wide]
        end = pltpu.roll(t, lax.rem(2 * ghosts + PAIR - side_end, ghosts), 1)[:, :wide]
        return jnp.where(span < core_rows, left, jnp.where(span < PAIR, right, end))

    taps, weights = targets(taps), targets(weights)
    lanes = taps % sector
    home = taps // sector
    found_ref[1] = jnp.zeros((lead, LANES), f32)
    def collect(h):
        part = slice(h * LANES, (h + 1) * LANES)
        total = None
        for s in range(groups):
            for y in range(2):
                values = blocks[s][:, (1 + y) * sector : (2 + y) * sector]
                masked = jnp.where(home[:, part] == 2 * (group ^ s) + y, weights[:, part], 0.0)
                total = pick(total, values, lanes[:, part], masked)
        found_ref[h] = total

    collect(0)

    @pl.when((own == 0) | (own == ring - 1))
    def _():
        collect(1)

    found = jnp.concatenate([found_ref[0], found_ref[1]], axis=1)
    turn_ref[0:lead, :] = found[:, 0:LANES]
    sides = jnp.transpose(turn_ref[...])
    left_side = sides[0:core_rows]
    right_side = sides[core_rows : 2 * core_rows]
    found = found[:, PAIR : PAIR + core_cells]

    for x in range(planes):
        part, at = block(x)
        for c in range(5):
            i = c * planes + x
            moved = pltpu.roll(gift, (LANES - i) % LANES, 1)
            strip[x, c] = part[c, at, :, 0:LANES] + jnp.where(lane == 0, moved, 0.0)

    def sides(q):
        u, pressure, enthalpy = velocities(q)
        return to_sides(q, u, pressure, enthalpy, 1, AX_ALPHA, AX_BETA)

    @pl.loop(0, sector // SUB)
    def _(j):
        part = pl.ds(pl.multiple_of(j * SUB, SUB), SUB)
        near = [near_ref[c, part, :] for c in range(5)]
        far = [far_ref[c, part, :] for c in range(5)]
        _, low = sides([jnp.where(core_even, far[c], near[c]) for c in range(5)])
        high, _ = sides([jnp.where(core_even, near[c], far[c]) for c in range(5)])
        for n, value in enumerate((low, high)):
            ref, at = block(n * (planes - 1))
            for c in range(5):
                strip[n * (planes - 1), c, part, :] += value[c][:, :LANES]
                wing[n, c, part, :] = ref[c, at, part, LANES:] + value[c][:, LANES:]

    _, radius_inv = radial_tables(cells)
    alpha2, beta2 = azim_coefs(radius_inv, 2.0 * math.pi / (sector * ring))
    def row_pair(start, width):
        pairs = []
        for c in range(5):
            odd = odd_ref[c * planes : (c + 1) * planes, start : start + width]
            even = got_ref[c * planes : (c + 1) * planes, edge + start : edge + start + width]
            pairs.append((jnp.where(ring_even, odd, even), jnp.where(ring_even, even, odd)))
        return [p[0] for p in pairs], [p[1] for p in pairs]

    edge = (groups + 1) * sector
    low, high = row_pair(0, cells)
    _, low = edge_rows(low, alpha2, beta2)
    high, _ = edge_rows(high, alpha2, beta2)
    for n, value in enumerate((low, high)):
        at = n * (sector - 1)
        small = n * (SUB - 1)
        for c in range(5):
            for x in range(planes):
                strip[x, c, at : at + 1, :] += value[c][x : x + 1, :LANES]
                rest_row = value[c][x : x + 1, LANES:]
                if 0 < x < planes - 1:
                    ref, spot = block(x)
                    brim[n, c, x - 1] = ref[c, spot, ends[n], LANES:]
                    brim[n, c, x - 1, small : small + 1, :] += rest_row
                else:
                    wing[min(x, 1), c, at : at + 1, :] += rest_row
    for copy in leaving[2:]:
        copy.start()

    strips = k_ref.shape[2]
    padded = k_ref.shape[3]
    tail = strips * LANES - core_cells
    body = LANES - tail
    both_sides = jnp.where(lane < lead, left_side, pltpu.roll(right_side, (body + 1) % LANES, 1))
    lows, highs = row_pair(cells, core_cells)
    for c in range(5):
        low, high = lows[c], highs[c]
        ends = found[c * planes : (c + 1) * planes]
        low = jnp.where(own == 0, ends, low)
        high = jnp.where(own == ring - 1, ends, high)
        for x in range(planes):
            i = c * planes + x
            for s in range(strips - 1):
                k_ref[c, x, s, 0:core_rows, :] = core_ref[c, x, :, s * LANES : (s + 1) * LANES]
            k_ref[c, x, strips - 1, 0:core_rows, 0:body] = core_ref[c, x, :, (strips - 1) * LANES :]
            pad = pltpu.roll(both_sides, (LANES - 1 - i) % LANES, 1)
            k_ref[c, x, strips - 1, 0:core_rows, body:] = pad[:, body:]
            for row, value in ((core_rows, high), (padded - 1, low)):
                for s in range(strips - 1):
                    k_ref[c, x, s, row : row + 1, :] = value[x : x + 1, s * LANES : (s + 1) * LANES]
                k_ref[c, x, strips - 1, row : row + 1, 0:body] = value[x : x + 1, (strips - 1) * LANES :]

    def load(c, x, part):
        return jnp.concatenate([k_ref[c, x, s, part, :] for s in range(strips)], axis=1)

    tiles = padded // SUB
    for x in range(planes):
        start = [load(c, x, pl.ds(0, tiles, stride=SUB)) for c in range(5)]
        before, _ = edge_rows(start, CORE_ALPHA, CORE_BETA)
        end = [load(c, x, pl.ds(SUB - 1, tiles, stride=SUB)) for c in range(5)]
        _, after = edge_rows(end, CORE_ALPHA, CORE_BETA)
        for c in range(5):
            next_ref[x, c, 0:tiles, :] = before[c]
            prev_ref[x, c, SUB : SUB + tiles, :] = after[c]
            prev_ref[x, c, SUB - 1 : SUB, :] = after[c][tiles - 1 : tiles]

    row = lax.broadcasted_iota(jnp.int32, (SUB, 1), 0)
    center = 1.0 - 2.0 * AX_ALPHA - 4.0 * CORE_ALPHA
    full = strips * LANES
    for j in range(-(-core_rows // SUB)):
        size = min(SUB, core_rows - j * SUB)
        part = pl.ds(j * SUB, SUB)
        here = pl.ds(j * SUB, size)

        def outside(ref):
            q = [ref[c, pl.ds(sector + j * SUB, size), 0:core_cells] for c in range(5)]
            u, pressure, enthalpy = velocities(q)
            return to_sides(q, u, pressure, enthalpy, 1, AX_ALPHA, AX_BETA)

        near_before, near_after = outside(near_ref)
        far_before, far_after = outside(far_ref)
        from_low = [jnp.where(core_even, a, b) for a, b in zip(far_after, near_after)]
        from_high = [jnp.where(core_even, a, b) for a, b in zip(near_before, far_before)]
        carry, held = None, None
        for x in range(planes):
            q = [load(c, x, part) for c in range(5)]
            u, pressure, enthalpy = velocities(q)
            before, after = to_sides(q, u, pressure, enthalpy, 1, AX_ALPHA, AX_BETA)
            if held is not None:
                for c in range(5):
                    core_out[c, x - 1, here, :] = (held[c] + before[c])[:size, :core_cells]
            result = [q[c] * center for c in range(5)]
            if carry is not None:
                result = [result[c] + carry[c] for c in range(5)]
            carry = after
            before, after = to_sides(q, u, pressure, enthalpy, 2, CORE_ALPHA, CORE_BETA)
            for c in range(5):
                above = next_ref[x, c, pl.ds((j + 1) % tiles, 1), :]
                below = prev_ref[x, c, pl.ds(j + SUB - 1, 1), :]
                up = pltpu.roll(before[c], SUB - 1, 0)
                down = pltpu.roll(after[c], 1, 0)
                result[c] = result[c] + (
                    jnp.where(row == SUB - 1, above, up) + jnp.where(row == 0, below, down)
                )
            before, after = to_sides(q, u, pressure, enthalpy, 3, CORE_ALPHA, CORE_BETA)
            for c in range(5):
                result[c] = result[c] + (
                    pltpu.roll(before[c], full - 1, 1) + pltpu.roll(after[c], 1, 1)
                )
            held = result
        for c in range(5):
            core_out[c, planes - 1, here, :] = held[c][:size, :core_cells] + from_high[c]
            core_out[c, 0, here, :] += from_low[c]

    for copy in leaving:
        copy.wait()


def final_call(ring, shape, core, taps, weights, got, odd, near, far, lower, upper, blocks):
    channels, planes, sector, cells = shape
    core_rows, core_cells = core.shape[2:]
    strips = -(-(core_cells + 2) // LANES)
    padded = -(-(core_rows + 2) // SUB) * SUB
    lead = channels * planes
    whole = pl.BlockSpec(memory_space=pltpu.VMEM)
    anywhere = pl.BlockSpec(memory_space=pltpu.HBM)
    groups = ring // 2
    edge_shape = (planes, channels, 2 * SUB, strips * LANES)
    return pl.pallas_call(
        functools.partial(final_kernel, ring),
        out_shape=(
            jax.ShapeDtypeStruct(shape, f32),
            jax.ShapeDtypeStruct(core.shape, f32),
        ),
        in_specs=[whole] * (9 + groups),
        out_specs=(anywhere, whole),
        scratch_shapes=[
            pltpu.VMEM((channels, planes, strips, padded, LANES), f32),
            pltpu.VMEM(edge_shape, f32),
            pltpu.VMEM(edge_shape, f32),
            pltpu.VMEM((LANES, LANES), f32),
            pltpu.VMEM((2, lead, LANES), f32),
            pltpu.VMEM((planes, channels, sector, LANES), f32),
            pltpu.VMEM((2, channels, sector, cells - LANES), f32),
            pltpu.VMEM((2, channels, planes - 2, SUB, cells - LANES), f32),
            pltpu.SemaphoreType.DMA((planes + 6,)),
        ],
        compiler_params=pltpu.CompilerParams(vmem_limit_bytes=GRANT),
        name="late_terms",
    )(core, taps, weights, got, odd, near, far, in_vmem(lower), in_vmem(upper), *blocks)


def body(cycle, core, core_taps, core_weights, cycle_taps, cycle_weights):
    planes, sector = cycle.shape[1:3]
    ring = lax.axis_size("azim")
    length = lax.axis_size("axial")
    angle_step = 2.0 * math.pi / (sector * ring)
    even_axial = [(i, i ^ 1) for i in range(length)]
    odd_axial = [(i, (i + 1) % length) for i in range(1, length, 2)]
    odd_axial += [(b, a) for a, b in odd_axial]
    even_azim = [(i, i ^ 1) for i in range(ring)]
    odd_azim = [(i, (i + 1) % ring) for i in range(1, ring, 2)]
    odd_azim += [(b, a) for a, b in odd_azim]
    held, far, near, odd, sent, kept = outgoing_call(ring, cycle, core, cycle_taps.T, cycle_weights.T)
    got = lax.ppermute(sent, "azim", even_azim)
    far = lax.ppermute(far, "axial", odd_axial)
    near = lax.ppermute(near, "axial", even_axial)
    half = planes // 2
    lower, odd = main_call(0, half, angle_step, held, odd, True)
    odd = lax.ppermute(odd, "azim", odd_azim)
    blocks = list(relay_call(ring, sector, sent, kept, got, lower))
    (upper,) = main_call(half, planes - half, angle_step, held, blocks[0], False)
    for s in range(1, ring // 2):
        blocks[s] = lax.ppermute(blocks[s], "azim", [(i, i ^ (2 * s)) for i in range(ring)])
    return tuple(
        final_call(
            ring, cycle.shape, core, core_taps.T, core_weights.T, got, odd, near, far, lower, upper, blocks
        )
    )


def solution(mesh):
    placed = (P(None, "axial", "azim", None), P(None, "axial", "azim", None), P(), P(), P(), P())
    return jax.shard_map(
        body,
        mesh=mesh,
        in_specs=placed,
        out_specs=(P(None, "axial", "azim", None), P(None, "axial", "azim", None)),
        check_vma=False,
    )
```

```python
import functools
import math

import jax
import jax.numpy as jnp
from jax import lax
from jax.experimental import pallas as pl
from jax.experimental.pallas import tpu as pltpu
from jax.sharding import PartitionSpec as P

time_step = 0.001
axial_step = 0.004
radial_step = 1.0 / 256.0
core_step = 2.0 / 192.0
inner_radius = 1.0
viscosity = 0.002
gamma_minus = 0.4

LANES = 128
SUB = 8
PAIR = 64
GRANT = 16 * 1024 * 1024


def in_hbm(x):
    return pltpu.with_memory_space_constraint(x, pltpu.HBM)


def in_vmem(x):
    return pltpu.with_memory_space_constraint(x, pltpu.VMEM)
f32 = jnp.float32
AX_ALPHA = time_step * viscosity / (axial_step * axial_step)
AX_BETA = time_step / (2.0 * axial_step)
RAD_ALPHA = time_step * viscosity / (radial_step * radial_step)
RAD_BETA = time_step / (2.0 * radial_step)
CORE_ALPHA = time_step * viscosity / (core_step * core_step)
CORE_BETA = time_step / (2.0 * core_step)


def velocities(q):
    inv = 1.0 / q[0]
    u = (q[1] * inv, q[2] * inv, q[3] * inv)
    kinetic = 0.5 * (q[1] * u[0] + q[2] * u[1] + q[3] * u[2])
    pressure = gamma_minus * (q[4] - kinetic)
    return u, pressure, q[4] + pressure


def scaled_flux(q, u, pressure, enthalpy, k, scale):
    su = u[k - 1] * scale
    parts = [q[k] * scale, q[1] * su, q[2] * su, q[3] * su, enthalpy * su]
    parts[k] = parts[k] + pressure * scale
    return parts


def to_sides(q, u, pressure, enthalpy, k, alpha, beta):
    flux = scaled_flux(q, u, pressure, enthalpy, k, beta)
    before, after = [], []
    for c in range(5):
        spread = q[c] * alpha
        before.append(spread - flux[c])
        after.append(spread + flux[c])
    return before, after


def radial_tables(cells):
    lane = lax.broadcasted_iota(jnp.int32, (1, cells), 1).astype(f32)
    radius = inner_radius + (lane + 0.5) * radial_step
    return radius, 1.0 / radius


def azim_coefs(radius_inv, angle_step):
    arc_inv = radius_inv * (1.0 / angle_step)
    return (time_step * viscosity) * arc_inv * arc_inv, (0.5 * time_step) * arc_inv


def edge_rows(q, alpha, beta):
    u, pressure, enthalpy = velocities(q)
    return to_sides(q, u, pressure, enthalpy, 2, alpha, beta)


def all_fluxes(q):
    inv = 1.0 / q[0]
    u1, u2, u3 = q[1] * inv, q[2] * inv, q[3] * inv
    m11, m22, m33 = q[1] * u1, q[2] * u2, q[3] * u3
    m12, m13, m23 = q[1] * u2, q[1] * u3, q[2] * u3
    pressure = gamma_minus * (q[4] - 0.5 * (m11 + m22 + m33))
    enthalpy = q[4] + pressure
    return (
        [q[1], m11 + pressure, m12, m13, enthalpy * u1],
        [q[2], m12, m22 + pressure, m23, enthalpy * u2],
        [q[3], m13, m23, m33 + pressure, enthalpy * u3],
    )


def main_kernel(first, count, angle_step, q_ref, after, *rest):
    out_ref, next_ref, prev_ref = rest[0], rest[-2], rest[-1]
    if len(rest) > 3:
        rest[1][...] = after[...]
    planes, strips, sector = q_ref.shape[1:4]
    cells = strips * LANES
    unit = 1.0 / AX_BETA
    lane = lax.broadcasted_iota(jnp.int32, (1, LANES), 1)
    first_lane = lane == 0
    last_lane = lane == LANES - 1
    row = lax.broadcasted_iota(jnp.int32, (SUB, 1), 0)
    first_row = row == 0
    last_row = row == SUB - 1
    coefs = []
    for s in range(strips):
        radius = inner_radius + ((lane + s * LANES).astype(f32) + 0.5) * radial_step
        radius_inv = 1.0 / radius
        alpha2, beta2 = azim_coefs(radius_inv, angle_step)
        beta_before = RAD_BETA * radius / (radius - radial_step)
        beta_after = RAD_BETA * radius / (radius + radial_step)
        if s == strips - 1:
            wall = RAD_BETA * (radius + radial_step) / radius
            beta_after = jnp.where(last_lane, wall, beta_after)
        center = 1.0 - 2.0 * AX_ALPHA - 2.0 * RAD_ALPHA - 2.0 * alpha2
        table = (alpha2, beta2, beta_before, beta_after, center, time_step * radius_inv)
        coefs.append([jnp.broadcast_to(t * unit, (SUB, LANES)) for t in table])
    ratio = AX_ALPHA / AX_BETA
    radial_alpha = RAD_ALPHA * unit

    tiles = sector // SUB
    zero = jnp.zeros((1, cells), f32)
    for i in range(count):
        for c in range(5):
            prev_ref[i, c, SUB - 1 : SUB, :] = zero
            next_ref[i, c, tiles : tiles + 1, :] = zero

    for i in range(count):
        for s in range(strips):
            alpha2, beta2 = coefs[s][0][:1], coefs[s][1][:1]
            wide = slice(s * LANES, (s + 1) * LANES)
            q = [q_ref[c, first + i, s, pl.ds(0, tiles, stride=SUB), :] for c in range(5)]
            before, _ = edge_rows(q, alpha2, beta2)
            q = [q_ref[c, first + i, s, pl.ds(SUB - 1, tiles, stride=SUB), :] for c in range(5)]
            _, after = edge_rows(q, alpha2, beta2)
            for c in range(5):
                next_ref[i, c, 0:tiles, wide] = before[c]
                prev_ref[i, c, SUB : SUB + tiles, wide] = after[c]

    def straight(q):
        return q if abs(ratio - 1.0) < 1e-9 else q * ratio

    def tile(j):
        part = pl.ds(pl.multiple_of(j * SUB, SUB), SUB)

        def load(x):
            return [[q_ref[c, x, s, part, :] for c in range(5)] for s in range(strips)]

        def axial(q, sign):
            flux = all_fluxes(q)[0]
            return [straight(q[c]) + sign * flux[c] for c in range(5)]

        def finish(i, held, before):
            for s in range(strips):
                for c in range(5):
                    value = held[s][c] if before is None else held[s][c] + before[s][c]
                    out_ref[c, i, part, s * LANES : (s + 1) * LANES] = value * AX_BETA

        carry = [axial(q, 1.0) for q in load(first - 1)] if first > 0 else None
        held = None
        for i in range(count):
            q = load(first + i)
            flux = [all_fluxes(q[s]) for s in range(strips)]
            if held is not None:
                finish(
                    i - 1,
                    held,
                    [[straight(q[s][c]) - flux[s][0][c] for c in range(5)] for s in range(strips)],
                )
            total = []
            for s in range(strips):
                alpha2, beta2, _, _, center, source = coefs[s]
                part_sum = [q[s][c] * center for c in range(5)]
                if carry is not None:
                    part_sum = [part_sum[c] + carry[s][c] for c in range(5)]
                wide = slice(s * LANES, (s + 1) * LANES)
                for c in range(5):
                    spread = q[s][c] * alpha2
                    moved = flux[s][1][c] * beta2
                    above = next_ref[i, c, pl.ds(j + 1, 1), :][:, wide]
                    below = prev_ref[i, c, pl.ds(j + SUB - 1, 1), :][:, wide]
                    up = pltpu.roll(spread - moved, SUB - 1, 0)
                    down = pltpu.roll(spread + moved, 1, 0)
                    part_sum[c] = part_sum[c] + (
                        jnp.where(last_row, above, up) + jnp.where(first_row, below, down)
                    )
                part_sum[2] = part_sum[2] - flux[s][1][3] * source
                part_sum[3] = part_sum[3] + flux[s][1][2] * source
                total.append(part_sum)
            carry = [[straight(q[s][c]) + flux[s][0][c] for c in range(5)] for s in range(strips)]
            for c in range(5):
                ups, downs, walls = [], [], None
                for s in range(strips):
                    spread = q[s][c] * radial_alpha
                    outward = spread + flux[s][2][c] * coefs[s][3]
                    ups.append(pltpu.roll(spread - flux[s][2][c] * coefs[s][2], LANES - 1, 1))
                    downs.append(pltpu.roll(outward, 1, 1))
                    walls = -outward if c == 3 else outward
                for s in range(strips):
                    up = jnp.where(last_lane, ups[s + 1] if s + 1 < strips else walls, ups[s])
                    down = jnp.where(first_lane, downs[s - 1] if s else 0.0, downs[s])
                    total[s][c] = total[s][c] + (up + down)
            held = total
        before = None
        if first + count < planes:
            before = [axial(q, -1.0) for q in load(first + count)]
        finish(count - 1, held, before)

    @pl.loop(0, tiles)
    def _(j):
        tile(j)


def main_call(first, count, angle_step, held, after, handed_on):
    channels, planes, strips, sector = held.shape[:4]
    cells = strips * LANES
    whole = pl.BlockSpec(memory_space=pltpu.VMEM)
    edge = (count, channels, sector // SUB + SUB, cells)
    shapes = [pltpu.VMEM((channels, count, sector, cells), f32)]
    if handed_on:
        shapes.append(jax.ShapeDtypeStruct(after.shape, f32))
    return pl.pallas_call(
        functools.partial(main_kernel, first, count, angle_step),
        out_shape=tuple(shapes),
        in_specs=[whole, whole if handed_on else pl.BlockSpec(memory_space=pl.ANY)],
        out_specs=(whole,) * len(shapes),
        scratch_shapes=[pltpu.VMEM(edge, f32), pltpu.VMEM(edge, f32)],
        compiler_params=pltpu.CompilerParams(vmem_limit_bytes=GRANT),
        name="cycle_planes_%d" % first,
    )(in_vmem(held), after)


def pick(total, values, lanes, weights):
    for k in range(lanes.shape[0]):
        index = jnp.broadcast_to(lanes[k : k + 1], values.shape)
        term = jnp.take_along_axis(values, index, axis=1, mode="promise_in_bounds") * weights[k : k + 1]
        total = term if total is None else total + term
    return total


def norm_rows(weights):
    total = weights[0:1]
    for k in range(1, weights.shape[0]):
        total = total + weights[k : k + 1]
    return weights / total


def angles_of(own, sector, count):
    lane = lax.broadcasted_iota(jnp.int32, (1, sector), 1) + own * sector
    angle = (lane.astype(f32) + 0.5) * (2.0 * math.pi / count)
    return jnp.cos(angle), jnp.sin(angle)


DEEP = 4
SLOT = 32


def outgoing_kernel(ring, cycle, core, taps, raw_weights, held_ref, far_ref, near_ref, odd_ref, even_ref, send_ref,
                    keep_ref, core_ref, taps_ref, weights_ref, side_ref, turn_ref, vals_ref, lane_ref,
                    weight_ref, flag_ref, used_ref, share_ref, sems):
    channels, planes, sector, cells = cycle.shape
    core_rows, core_cells = core_ref.shape[2:]
    lead = channels * planes
    own = lax.axis_index("azim")
    parity = lax.rem(own, 2)
    ring_even = parity == 0
    near = jnp.where(lax.rem(lax.axis_index("axial"), 2) == 0, planes - 1, 0)
    far = planes - 1 - near
    lane = lax.broadcasted_iota(jnp.int32, (1, LANES), 1)
    per = LANES // DEEP
    early = [
        pltpu.make_async_copy(core, core_ref, sems.at[0]),
        pltpu.make_async_copy(taps, taps_ref, sems.at[1]),
        pltpu.make_async_copy(raw_weights, weights_ref, sems.at[2]),
    ]
    cycle_strips = cells // LANES
    copies = [
        pltpu.make_async_copy(
            cycle.at[:, :, :, pl.ds(n * LANES, LANES)], held_ref.at[:, :, n], sems.at[3 + n]
        )
        for n in range(cycle_strips)
    ]
    for copy in early + copies:
        copy.start()
    groups = ring // 2
    for copy in early:
        copy.wait()

    sides = []
    side_ref[...] = jnp.zeros_like(side_ref)
    strips = -(-core_cells // LANES)
    width = core_cells - (strips - 1) * LANES
    for side in range(2):
        start = 0 if side == 0 else (strips - 1) * LANES
        at = 0 if side == 0 else width - DEEP
        for part in range(-(-lead // per)):
            total = None
            for i in range(part * per, min(lead, (part + 1) * per)):
                block = core_ref[i // planes, i % planes, :, start : min(start + LANES, core_cells)]
                if block.shape[1] < LANES:
                    block = jnp.concatenate(
                        [block, jnp.zeros((core_rows, LANES - block.shape[1]), f32)], axis=1
                    )
                turn = (DEEP * (i - part * per) - at) % LANES
                moved = pltpu.roll(block, turn, 1) if turn else block
                total = moved if total is None else jnp.where(lane // DEEP == i - part * per, moved, total)
            side_ref[0:core_rows, :] = total
            turn_ref[part * LANES : (part + 1) * LANES, 0:SLOT] = jnp.transpose(side_ref[...])
        total = turn_ref[pl.ds(0, lead, stride=DEEP), :]
        for d in range(1, DEEP):
            moved = pltpu.roll(turn_ref[pl.ds(d, lead, stride=DEEP), :], d * SLOT, 1)
            total = jnp.where(lane // SLOT == d, moved, total)
        sides.append(jnp.where(lane < DEEP * SLOT, total, 0.0))

    whole = (strips - 1) * DEEP
    slots = vals_ref.shape[0]
    pairs = slots - 2 - whole
    fold = DEEP // pairs
    vals_ref[0] = sides[0]
    vals_ref[1] = sides[1]
    at_end = (own == 0) | (own == ring - 1)
    base = jnp.where(own == 0, 0, core_rows - DEEP)

    @pl.when(at_end)
    def _():
        if fold * width < LANES:
            vals_ref[2:] = jnp.zeros((slots - 2, lead, LANES), f32)
        for i in range(lead):
            plane = core_ref[i // planes, i % planes]
            rows = jnp.where(own == 0, plane[:DEEP], plane[core_rows - DEEP :])
            for d in range(DEEP):
                for s in range(strips - 1):
                    vals_ref[2 + s * DEEP + d, i : i + 1, :] = rows[d : d + 1, s * LANES : (s + 1) * LANES]
                at = (d % fold) * width
                vals_ref[2 + whole + d // fold, i : i + 1, at : at + width] = rows[d : d + 1, (strips - 1) * LANES :]

    weights = norm_rows(weights_ref[...])
    cell = taps_ref[...]
    row = ((cell.astype(f32) + 0.5) * (1.0 / core_cells)).astype(jnp.int32)
    column = cell - row * core_cells
    row = row - own * core_rows
    here = (row >= 0) & (row < core_rows)
    left = column < DEEP
    right = column >= core_cells - DEEP
    side_lane = jnp.where(left, column, column - (core_cells - DEEP)) * SLOT + row
    depth = row - base
    tail = column >= (strips - 1) * LANES
    end_slot = jnp.where(tail, whole + depth // fold, (column // LANES) * DEEP + depth) + 2
    end_lane = jnp.where(tail, column - (strips - 1) * LANES + (depth % fold) * width, column % LANES)
    inside = here & at_end & (depth >= 0) & (depth < DEEP)
    slot = jnp.where(here & left, 0, jnp.where(here & right, 1, jnp.where(inside, end_slot, slots)))
    lane_ref[...] = jnp.where(slot < 2, side_lane, jnp.where(slot < slots, end_lane, 0))
    for d in range(slots):
        mine = jnp.where(slot == d, weights, 0.0)
        weight_ref[d] = mine
        flag_ref[d : d + 1, :] = jnp.max(mine, axis=0, keepdims=True)
    power = jnp.left_shift(1, lax.broadcasted_iota(jnp.int32, (slots, 1), 0)).astype(f32)
    for s in range(ring):
        most = jnp.max(flag_ref[:, s * sector : (s + 1) * sector], axis=1, keepdims=True)
        used_ref[s] = jnp.sum(jnp.where(most > 0.0, power, 0.0)).astype(jnp.int32)

    @pl.loop(0, ring)
    def _(s):
        part = pl.ds(pl.multiple_of(s * sector, sector), sector)
        share_ref[:, part] = jnp.zeros((lead, sector), f32)
        used = used_ref[s]

        def add(d):
            @pl.when(lax.rem(lax.div(used, 1 << d), 2) == 1)
            def _():
                share_ref[:, part] = pick(
                    share_ref[:, part], vals_ref[d], lane_ref[:, part], weight_ref[d, :, part]
                )

        add(0)
        add(1)

        @pl.when(used > 3)
        def _():
            for d in range(2, slots):
                add(d)

    copies[0].wait()
    trace = None
    for i in range(lead):
        block = held_ref[i // planes, i % planes, 0]
        moved = pltpu.roll(block, i, 1) if i else block
        trace = moved if trace is None else jnp.where(lane == i, moved, trace)
    trace = jnp.transpose(trace)[:lead]
    cosine, sine = angles_of(own, sector, sector * ring)
    last = pl.ds(groups * sector, sector)
    azimuthal, radial = trace[2 * planes : 3 * planes], trace[3 * planes : 4 * planes]
    send_ref[0 : 2 * planes, last] = trace[0 : 2 * planes]
    send_ref[2 * planes : 3 * planes, last] = radial * cosine - azimuthal * sine
    send_ref[3 * planes : 4 * planes, last] = radial * sine + azimuthal * cosine
    send_ref[4 * planes :, last] = trace[4 * planes :]

    for g in range(groups):
        to = pl.ds(g * sector, sector)
        mine = pl.ds(pl.multiple_of((2 * g + parity) * sector, sector), sector)
        other = pl.ds(pl.multiple_of((2 * g + 1 - parity) * sector, sector), sector)
        keep_ref[:, to] = share_ref[:, mine]
        send_ref[:, to] = share_ref[:, other]

    for c in range(channels):
        near_ref[c, sector:, 0:core_cells] = core_ref[c, near]
        far_ref[c, sector:, 0:core_cells] = core_ref[c, far]
    for copy in copies[1:]:
        copy.wait()
    for c in range(channels):
        for n in range(cycle_strips):
            wide = slice(n * LANES, (n + 1) * LANES)
            near_ref[c, 0:sector, wide] = held_ref[c, near, n]
            far_ref[c, 0:sector, wide] = held_ref[c, far, n]
    for c in range(channels):
        for x in range(planes):
            i = c * planes + x
            for n in range(cycle_strips):
                low = held_ref[c, x, n, 0:1, :]
                high = held_ref[c, x, n, sector - 1 : sector, :]
                start = n * LANES
                even_ref[i : i + 1, start : start + LANES] = jnp.where(ring_even, high, low)
                odd_ref[i : i + 1, start : start + LANES] = jnp.where(ring_even, low, high)
            low = core_ref[c, x, 0:1, :]
            high = core_ref[c, x, core_rows - 1 : core_rows, :]
            even_ref[i : i + 1, cells : cells + core_cells] = jnp.where(ring_even, high, low)
            odd_ref[i : i + 1, cells : cells + core_cells] = jnp.where(ring_even, low, high)


def outgoing_call(ring, cycle, core, taps, weights):
    channels, planes, sector, cells = cycle.shape
    core_rows, core_cells = core.shape[2:]
    lead = channels * planes
    groups = ring // 2
    strips = -(-core_cells // LANES)
    fold = 2 if 2 * (core_cells - (strips - 1) * LANES) <= LANES else 1
    slots = 2 + (strips - 1) * DEEP + DEEP // fold
    parts = -(-lead * DEEP // LANES)
    whole = pl.BlockSpec(memory_space=pltpu.VMEM)
    anywhere = pl.BlockSpec(memory_space=pl.ANY)
    edge = cells + strips * LANES
    plane = jax.ShapeDtypeStruct((channels, sector + core_rows, cells), f32)
    return pl.pallas_call(
        functools.partial(outgoing_kernel, ring),
        out_shape=(
            pltpu.VMEM((channels, planes, cells // LANES, sector, LANES), f32),
            plane,
            plane,
            jax.ShapeDtypeStruct((lead, edge), f32),
            jax.ShapeDtypeStruct((lead, edge), f32),
            jax.ShapeDtypeStruct((lead, (groups + 1) * sector), f32),
            jax.ShapeDtypeStruct((lead, groups * sector), f32),
        ),
        in_specs=[anywhere] * 4,
        out_specs=(whole,) * 7,
        scratch_shapes=[
            pltpu.VMEM(core.shape, f32),
            pltpu.VMEM(taps.shape, jnp.int32),
            pltpu.VMEM(weights.shape, f32),
            pltpu.VMEM((SLOT, LANES), f32),
            pltpu.VMEM((parts * LANES, LANES), f32),
            pltpu.VMEM((slots, lead, LANES), f32),
            pltpu.VMEM(taps.shape, jnp.int32),
            pltpu.VMEM((slots,) + taps.shape, f32),
            pltpu.VMEM((slots, taps.shape[1]), f32),
            pltpu.SMEM((ring,), jnp.int32),
            pltpu.VMEM((lead, ring * sector), f32),
            pltpu.SemaphoreType.DMA((3 + cells // LANES,)),
        ],
        compiler_params=pltpu.CompilerParams(vmem_limit_bytes=GRANT),
        cost_estimate=pl.CostEstimate(flops=0, bytes_accessed=16 * 1024 * 1024, transcendentals=0),
        name="outgoing",
    )(in_hbm(cycle), in_hbm(core), in_hbm(taps), in_hbm(weights))


def relay_kernel(groups, sent, kept, got, rows, after, rows_ref, own_ref, *outs):
    rows_ref[...] = rows[...]
    sector = own_ref.shape[1] // 3
    own = lax.axis_index("azim")
    group = own // 2
    even = lax.rem(own, 2) == 0
    last = pl.ds(groups * sector, sector)
    mine, other = sent[:, last], got[:, last]
    first = jnp.where(even, mine, other)
    second = jnp.where(even, other, mine)
    for s in range(groups):
        to = own_ref if s == 0 else outs[s - 1]
        target = group ^ s
        part = pl.ds(pl.multiple_of(target * sector, sector), sector)
        to[:, 0:sector] = kept[:, part] + got[:, part]
        to[:, sector : 2 * sector] = first
        to[:, 2 * sector :] = second


def relay_call(ring, sector, sent, kept, got, rows, after):
    groups = ring // 2
    whole = pl.BlockSpec(memory_space=pltpu.VMEM)
    block = jax.ShapeDtypeStruct((kept.shape[0], 3 * sector), f32)
    return pl.pallas_call(
        functools.partial(relay_kernel, groups),
        out_shape=(jax.ShapeDtypeStruct(rows.shape, f32),) + (block,) * groups,
        in_specs=[whole] * 4 + [pl.BlockSpec(memory_space=pl.ANY)],
        out_specs=(whole,) * (1 + groups),
        compiler_params=pltpu.CompilerParams(vmem_limit_bytes=GRANT),
        name="ghost_relay",
    )(sent, kept, got, rows, after)


def final_kernel(ring, core_ref, taps_ref, weights_ref, even_ref, odd_ref, near_ref, far_ref, lower, upper, *rest):
    groups = ring // 2
    blocks = rest[:groups]
    (cycle_out, core_out, k_ref, next_ref, prev_ref, turn_ref, found_ref, strip, wing, brim,
     out_sem) = rest[groups:]
    channels, planes, sector, cells = cycle_out.shape
    core_rows, core_cells = core_ref.shape[2:]
    lead = channels * planes
    own = lax.axis_index("azim")
    group = own // 2
    ring_even = lax.rem(own, 2) == 0
    core_even = lax.rem(lax.axis_index("axial"), 2) == 0
    inner = pl.ds(0, LANES)
    outer = pl.ds(LANES, cells - LANES)
    middle = pl.ds(1, planes - 2)
    ends = (pl.ds(0, SUB), pl.ds(sector - SUB, SUB))

    half = lower.shape[1]

    def block(x):
        return (lower, x) if x < half else (upper, x - half)

    bulk = pl.ds(SUB, sector - 2 * SUB)
    places = [
        (lower.at[:, pl.ds(1, half - 1), bulk, outer], cycle_out.at[:, pl.ds(1, half - 1), bulk, outer]),
        (
            upper.at[:, pl.ds(0, planes - 1 - half), bulk, outer],
            cycle_out.at[:, pl.ds(half, planes - 1 - half), bulk, outer],
        ),
    ]
    places += [(strip.at[x], cycle_out.at[:, x, :, inner]) for x in range(planes)]
    places += [(wing.at[n], cycle_out.at[:, x, :, outer]) for n, x in enumerate((0, planes - 1))]
    places += [(brim.at[n], cycle_out.at[:, middle, ends[n], outer]) for n in range(2)]
    leaving = [
        pltpu.make_async_copy(a, b, out_sem.at[n]) for n, (a, b) in enumerate(places)
    ]
    for copy in leaving[:2]:
        copy.start()
    lane = lax.broadcasted_iota(jnp.int32, (1, LANES), 1)

    total = blocks[0][:, 0:sector]
    for s in range(1, groups):
        total = total + blocks[s][:, 0:sector]
    cosine, sine = angles_of(own, sector, sector * ring)
    q = [total[c * planes : (c + 1) * planes] for c in range(5)]
    q[2], q[3] = q[3] * cosine - q[2] * sine, q[2] * cosine + q[3] * sine
    u, pressure, enthalpy = velocities(q)
    inside = inner_radius - 0.5 * radial_step
    beta = RAD_BETA * inside / (inside + radial_step)
    _, after = to_sides(q, u, pressure, enthalpy, 3, RAD_ALPHA, beta)
    turn_ref[...] = jnp.zeros_like(turn_ref)
    for c in range(5):
        turn_ref[c * planes : (c + 1) * planes, :] = after[c]
    gift = jnp.transpose(turn_ref[...])

    taps, weights = taps_ref[...], norm_rows(weights_ref[...])
    ghosts = taps.shape[1]
    wide = 2 * LANES
    span = lax.broadcasted_iota(jnp.int32, (1, wide), 1)
    shift = own * core_rows
    side_end = jnp.where(own == 0, 2 * core_cells, 3 * core_cells)

    def targets(t):
        left = pltpu.roll(t, ghosts - shift, 1)[:, :wide]
        right = pltpu.roll(t, lax.rem(2 * ghosts + core_rows - core_cells - shift, ghosts), 1)[:, :wide]
        end = pltpu.roll(t, lax.rem(2 * ghosts + PAIR - side_end, ghosts), 1)[:, :wide]
        return jnp.where(span < core_rows, left, jnp.where(span < PAIR, right, end))

    taps, weights = targets(taps), targets(weights)
    lanes = taps % sector
    home = taps // sector
    found_ref[1] = jnp.zeros((lead, LANES), f32)
    def collect(h):
        part = slice(h * LANES, (h + 1) * LANES)
        total = None
        for s in range(groups):
            for y in range(2):
                values = blocks[s][:, (1 + y) * sector : (2 + y) * sector]
                masked = jnp.where(home[:, part] == 2 * (group ^ s) + y, weights[:, part], 0.0)
                total = pick(total, values, lanes[:, part], masked)
        found_ref[h] = total

    collect(0)

    @pl.when((own == 0) | (own == ring - 1))
    def _():
        collect(1)

    found = jnp.concatenate([found_ref[0], found_ref[1]], axis=1)
    turn_ref[0:lead, :] = found[:, 0:LANES]
    sides = jnp.transpose(turn_ref[...])
    left_side = sides[0:core_rows]
    right_side = sides[core_rows : 2 * core_rows]
    found = found[:, PAIR : PAIR + core_cells]

    for x in range(planes):
        part, at = block(x)
        for c in range(5):
            i = c * planes + x
            moved = pltpu.roll(gift, (LANES - i) % LANES, 1)
            strip[x, c] = part[c, at, :, 0:LANES] + jnp.where(lane == 0, moved, 0.0)

    def sides(q):
        u, pressure, enthalpy = velocities(q)
        return to_sides(q, u, pressure, enthalpy, 1, AX_ALPHA, AX_BETA)

    @pl.loop(0, sector // SUB)
    def _(j):
        part = pl.ds(pl.multiple_of(j * SUB, SUB), SUB)
        near = [near_ref[c, part, :] for c in range(5)]
        far = [far_ref[c, part, :] for c in range(5)]
        _, low = sides([jnp.where(core_even, far[c], near[c]) for c in range(5)])
        high, _ = sides([jnp.where(core_even, near[c], far[c]) for c in range(5)])
        for n, value in enumerate((low, high)):
            ref, at = block(n * (planes - 1))
            for c in range(5):
                strip[n * (planes - 1), c, part, :] += value[c][:, :LANES]
                wing[n, c, part, :] = ref[c, at, part, LANES:] + value[c][:, LANES:]

    _, radius_inv = radial_tables(cells)
    alpha2, beta2 = azim_coefs(radius_inv, 2.0 * math.pi / (sector * ring))
    def row_pair(start, width):
        pairs = []
        for c in range(5):
            odd = odd_ref[c * planes : (c + 1) * planes, start : start + width]
            even = even_ref[c * planes : (c + 1) * planes, start : start + width]
            pairs.append((jnp.where(ring_even, odd, even), jnp.where(ring_even, even, odd)))
        return [p[0] for p in pairs], [p[1] for p in pairs]

    low, high = row_pair(0, cells)
    _, low = edge_rows(low, alpha2, beta2)
    high, _ = edge_rows(high, alpha2, beta2)
    for n, value in enumerate((low, high)):
        at = n * (sector - 1)
        small = n * (SUB - 1)
        for c in range(5):
            for x in range(planes):
                strip[x, c, at : at + 1, :] += value[c][x : x + 1, :LANES]
                rest_row = value[c][x : x + 1, LANES:]
                if 0 < x < planes - 1:
                    ref, spot = block(x)
                    brim[n, c, x - 1] = ref[c, spot, ends[n], LANES:]
                    brim[n, c, x - 1, small : small + 1, :] += rest_row
                else:
                    wing[min(x, 1), c, at : at + 1, :] += rest_row
    for copy in leaving[2:]:
        copy.start()

    strips = k_ref.shape[2]
    padded = k_ref.shape[3]
    tail = strips * LANES - core_cells
    body = LANES - tail
    both_sides = jnp.where(lane < lead, left_side, pltpu.roll(right_side, (body + 1) % LANES, 1))
    lows, highs = row_pair(cells, core_cells)
    for c in range(5):
        low, high = lows[c], highs[c]
        ends = found[c * planes : (c + 1) * planes]
        low = jnp.where(own == 0, ends, low)
        high = jnp.where(own == ring - 1, ends, high)
        for x in range(planes):
            i = c * planes + x
            for s in range(strips - 1):
                k_ref[c, x, s, 0:core_rows, :] = core_ref[c, x, :, s * LANES : (s + 1) * LANES]
            k_ref[c, x, strips - 1, 0:core_rows, 0:body] = core_ref[c, x, :, (strips - 1) * LANES :]
            pad = pltpu.roll(both_sides, (LANES - 1 - i) % LANES, 1)
            k_ref[c, x, strips - 1, 0:core_rows, body:] = pad[:, body:]
            for row, value in ((core_rows, high), (padded - 1, low)):
                for s in range(strips - 1):
                    k_ref[c, x, s, row : row + 1, :] = value[x : x + 1, s * LANES : (s + 1) * LANES]
                k_ref[c, x, strips - 1, row : row + 1, 0:body] = value[x : x + 1, (strips - 1) * LANES :]

    def load(c, x, part):
        return jnp.concatenate([k_ref[c, x, s, part, :] for s in range(strips)], axis=1)

    tiles = padded // SUB
    for x in range(planes):
        start = [load(c, x, pl.ds(0, tiles, stride=SUB)) for c in range(5)]
        before, _ = edge_rows(start, CORE_ALPHA, CORE_BETA)
        end = [load(c, x, pl.ds(SUB - 1, tiles, stride=SUB)) for c in range(5)]
        _, after = edge_rows(end, CORE_ALPHA, CORE_BETA)
        for c in range(5):
            next_ref[x, c, 0:tiles, :] = before[c]
            prev_ref[x, c, SUB : SUB + tiles, :] = after[c]
            prev_ref[x, c, SUB - 1 : SUB, :] = after[c][tiles - 1 : tiles]

    row = lax.broadcasted_iota(jnp.int32, (SUB, 1), 0)
    center = 1.0 - 2.0 * AX_ALPHA - 4.0 * CORE_ALPHA
    full = strips * LANES
    for j in range(-(-core_rows // SUB)):
        size = min(SUB, core_rows - j * SUB)
        part = pl.ds(j * SUB, SUB)
        here = pl.ds(j * SUB, size)

        def outside(ref):
            q = [ref[c, pl.ds(sector + j * SUB, size), 0:core_cells] for c in range(5)]
            u, pressure, enthalpy = velocities(q)
            return to_sides(q, u, pressure, enthalpy, 1, AX_ALPHA, AX_BETA)

        near_before, near_after = outside(near_ref)
        far_before, far_after = outside(far_ref)
        from_low = [jnp.where(core_even, a, b) for a, b in zip(far_after, near_after)]
        from_high = [jnp.where(core_even, a, b) for a, b in zip(near_before, far_before)]
        carry, held = None, None
        for x in range(planes):
            q = [load(c, x, part) for c in range(5)]
            u, pressure, enthalpy = velocities(q)
            before, after = to_sides(q, u, pressure, enthalpy, 1, AX_ALPHA, AX_BETA)
            if held is not None:
                for c in range(5):
                    core_out[c, x - 1, here, :] = (held[c] + before[c])[:size, :core_cells]
            result = [q[c] * center for c in range(5)]
            if carry is not None:
                result = [result[c] + carry[c] for c in range(5)]
            carry = after
            before, after = to_sides(q, u, pressure, enthalpy, 2, CORE_ALPHA, CORE_BETA)
            for c in range(5):
                above = next_ref[x, c, pl.ds((j + 1) % tiles, 1), :]
                below = prev_ref[x, c, pl.ds(j + SUB - 1, 1), :]
                up = pltpu.roll(before[c], SUB - 1, 0)
                down = pltpu.roll(after[c], 1, 0)
                result[c] = result[c] + (
                    jnp.where(row == SUB - 1, above, up) + jnp.where(row == 0, below, down)
                )
            before, after = to_sides(q, u, pressure, enthalpy, 3, CORE_ALPHA, CORE_BETA)
            for c in range(5):
                result[c] = result[c] + (
                    pltpu.roll(before[c], full - 1, 1) + pltpu.roll(after[c], 1, 1)
                )
            held = result
        for c in range(5):
            core_out[c, planes - 1, here, :] = held[c][:size, :core_cells] + from_high[c]
            core_out[c, 0, here, :] += from_low[c]

    for copy in leaving:
        copy.wait()


def final_call(ring, shape, core, taps, weights, even, odd, near, far, lower, upper, blocks):
    channels, planes, sector, cells = shape
    core_rows, core_cells = core.shape[2:]
    strips = -(-(core_cells + 2) // LANES)
    padded = -(-(core_rows + 2) // SUB) * SUB
    lead = channels * planes
    whole = pl.BlockSpec(memory_space=pltpu.VMEM)
    anywhere = pl.BlockSpec(memory_space=pltpu.HBM)
    groups = ring // 2
    edge_shape = (planes, channels, 2 * SUB, strips * LANES)
    return pl.pallas_call(
        functools.partial(final_kernel, ring),
        out_shape=(
            jax.ShapeDtypeStruct(shape, f32),
            jax.ShapeDtypeStruct(core.shape, f32),
        ),
        in_specs=[whole] * (9 + groups),
        out_specs=(anywhere, whole),
        scratch_shapes=[
            pltpu.VMEM((channels, planes, strips, padded, LANES), f32),
            pltpu.VMEM(edge_shape, f32),
            pltpu.VMEM(edge_shape, f32),
            pltpu.VMEM((LANES, LANES), f32),
            pltpu.VMEM((2, lead, LANES), f32),
            pltpu.VMEM((planes, channels, sector, LANES), f32),
            pltpu.VMEM((2, channels, sector, cells - LANES), f32),
            pltpu.VMEM((2, channels, planes - 2, SUB, cells - LANES), f32),
            pltpu.SemaphoreType.DMA((planes + 6,)),
        ],
        compiler_params=pltpu.CompilerParams(vmem_limit_bytes=GRANT),
        name="late_terms",
    )(core, taps, weights, even, odd, near, far, in_vmem(lower), in_vmem(upper), *blocks)


def body(cycle, core, core_taps, core_weights, cycle_taps, cycle_weights):
    planes, sector = cycle.shape[1:3]
    ring = lax.axis_size("azim")
    length = lax.axis_size("axial")
    angle_step = 2.0 * math.pi / (sector * ring)
    even_axial = [(i, i ^ 1) for i in range(length)]
    odd_axial = [(i, (i + 1) % length) for i in range(1, length, 2)]
    odd_axial += [(b, a) for a, b in odd_axial]
    even_azim = [(i, i ^ 1) for i in range(ring)]
    odd_azim = [(i, (i + 1) % ring) for i in range(1, ring, 2)]
    odd_azim += [(b, a) for a, b in odd_azim]
    held, far, near, odd, even, sent, kept = outgoing_call(ring, cycle, core, cycle_taps.T, cycle_weights.T)
    got = lax.ppermute(sent, "azim", even_azim)
    far = lax.ppermute(far, "axial", odd_axial)
    near = lax.ppermute(near, "axial", even_axial)
    half = planes // 2
    lower, even = main_call(0, half, angle_step, held, even, True)
    even = lax.ppermute(even, "azim", even_azim)
    odd, *blocks = relay_call(ring, sector, sent, kept, got, odd, lower)
    odd = lax.ppermute(odd, "azim", odd_azim)
    (upper,) = main_call(half, planes - half, angle_step, held, blocks[0], False)
    for s in range(1, ring // 2):
        blocks[s] = lax.ppermute(blocks[s], "azim", [(i, i ^ (2 * s)) for i in range(ring)])
    return tuple(
        final_call(
            ring, cycle.shape, core, core_taps.T, core_weights.T, even, odd, near, far, lower, upper, blocks
        )
    )


def solution(mesh):
    placed = (P(None, "axial", "azim", None), P(None, "axial", "azim", None), P(), P(), P(), P())
    return jax.shard_map(
        body,
        mesh=mesh,
        in_specs=placed,
        out_specs=(P(None, "axial", "azim", None), P(None, "axial", "azim", None)),
        check_vma=False,
    )
```

```python
import functools
import math

import jax
import jax.numpy as jnp
from jax import lax
from jax.experimental import pallas as pl
from jax.experimental.pallas import tpu as pltpu
from jax.sharding import PartitionSpec as P

time_step = 0.001
axial_step = 0.004
radial_step = 1.0 / 256.0
core_step = 2.0 / 192.0
inner_radius = 1.0
viscosity = 0.002
gamma_minus = 0.4

LANES = 128
SUB = 8
PAIR = 64
GRANT = 16 * 1024 * 1024


def in_hbm(x):
    return pltpu.with_memory_space_constraint(x, pltpu.HBM)


def in_vmem(x):
    return pltpu.with_memory_space_constraint(x, pltpu.VMEM)
f32 = jnp.float32
AX_ALPHA = time_step * viscosity / (axial_step * axial_step)
AX_BETA = time_step / (2.0 * axial_step)
RAD_ALPHA = time_step * viscosity / (radial_step * radial_step)
RAD_BETA = time_step / (2.0 * radial_step)
CORE_ALPHA = time_step * viscosity / (core_step * core_step)
CORE_BETA = time_step / (2.0 * core_step)


def velocities(q):
    inv = 1.0 / q[0]
    u = (q[1] * inv, q[2] * inv, q[3] * inv)
    kinetic = 0.5 * (q[1] * u[0] + q[2] * u[1] + q[3] * u[2])
    pressure = gamma_minus * (q[4] - kinetic)
    return u, pressure, q[4] + pressure


def scaled_flux(q, u, pressure, enthalpy, k, scale):
    su = u[k - 1] * scale
    parts = [q[k] * scale, q[1] * su, q[2] * su, q[3] * su, enthalpy * su]
    parts[k] = parts[k] + pressure * scale
    return parts


def to_sides(q, u, pressure, enthalpy, k, alpha, beta):
    flux = scaled_flux(q, u, pressure, enthalpy, k, beta)
    before, after = [], []
    for c in range(5):
        spread = q[c] * alpha
        before.append(spread - flux[c])
        after.append(spread + flux[c])
    return before, after


def radial_tables(cells):
    lane = lax.broadcasted_iota(jnp.int32, (1, cells), 1).astype(f32)
    radius = inner_radius + (lane + 0.5) * radial_step
    return radius, 1.0 / radius


def azim_coefs(radius_inv, angle_step):
    arc_inv = radius_inv * (1.0 / angle_step)
    return (time_step * viscosity) * arc_inv * arc_inv, (0.5 * time_step) * arc_inv


def edge_rows(q, alpha, beta):
    u, pressure, enthalpy = velocities(q)
    return to_sides(q, u, pressure, enthalpy, 2, alpha, beta)


def all_fluxes(q):
    inv = 1.0 / q[0]
    u1, u2, u3 = q[1] * inv, q[2] * inv, q[3] * inv
    m11, m22, m33 = q[1] * u1, q[2] * u2, q[3] * u3
    m12, m13, m23 = q[1] * u2, q[1] * u3, q[2] * u3
    pressure = gamma_minus * (q[4] - 0.5 * (m11 + m22 + m33))
    enthalpy = q[4] + pressure
    return (
        [q[1], m11 + pressure, m12, m13, enthalpy * u1],
        [q[2], m12, m22 + pressure, m23, enthalpy * u2],
        [q[3], m13, m23, m33 + pressure, enthalpy * u3],
    )


def main_kernel(first, count, angle_step, q_ref, after, *rest):
    out_ref, next_ref, prev_ref = rest[0], rest[-2], rest[-1]
    if len(rest) > 3:
        rest[1][...] = after[...]
    planes, strips, sector = q_ref.shape[1:4]
    cells = strips * LANES
    unit = 1.0 / AX_BETA
    lane = lax.broadcasted_iota(jnp.int32, (1, LANES), 1)
    first_lane = lane == 0
    last_lane = lane == LANES - 1
    row = lax.broadcasted_iota(jnp.int32, (SUB, 1), 0)
    first_row = row == 0
    last_row = row == SUB - 1
    coefs = []
    for s in range(strips):
        radius = inner_radius + ((lane + s * LANES).astype(f32) + 0.5) * radial_step
        radius_inv = 1.0 / radius
        alpha2, beta2 = azim_coefs(radius_inv, angle_step)
        beta_before = RAD_BETA * radius / (radius - radial_step)
        beta_after = RAD_BETA * radius / (radius + radial_step)
        if s == strips - 1:
            wall = RAD_BETA * (radius + radial_step) / radius
            beta_after = jnp.where(last_lane, wall, beta_after)
        center = 1.0 - 2.0 * AX_ALPHA - 2.0 * RAD_ALPHA - 2.0 * alpha2
        table = (alpha2, beta2, beta_before, beta_after, center, time_step * radius_inv)
        coefs.append([jnp.broadcast_to(t * unit, (SUB, LANES)) for t in table])
    ratio = AX_ALPHA / AX_BETA
    radial_alpha = RAD_ALPHA * unit

    tiles = sector // SUB
    zero = jnp.zeros((1, cells), f32)
    for i in range(count):
        for c in range(5):
            prev_ref[i, c, SUB - 1 : SUB, :] = zero
            next_ref[i, c, tiles : tiles + 1, :] = zero

    for i in range(count):
        for s in range(strips):
            alpha2, beta2 = coefs[s][0][:1], coefs[s][1][:1]
            wide = slice(s * LANES, (s + 1) * LANES)
            q = [q_ref[c, first + i, s, pl.ds(0, tiles, stride=SUB), :] for c in range(5)]
            before, _ = edge_rows(q, alpha2, beta2)
            q = [q_ref[c, first + i, s, pl.ds(SUB - 1, tiles, stride=SUB), :] for c in range(5)]
            _, after = edge_rows(q, alpha2, beta2)
            for c in range(5):
                next_ref[i, c, 0:tiles, wide] = before[c]
                prev_ref[i, c, SUB : SUB + tiles, wide] = after[c]

    def straight(q):
        return q if abs(ratio - 1.0) < 1e-9 else q * ratio

    def tile(j):
        part = pl.ds(pl.multiple_of(j * SUB, SUB), SUB)

        def load(x):
            return [[q_ref[c, x, s, part, :] for c in range(5)] for s in range(strips)]

        def axial(q, sign):
            flux = all_fluxes(q)[0]
            return [straight(q[c]) + sign * flux[c] for c in range(5)]

        def finish(i, held, before):
            for s in range(strips):
                for c in range(5):
                    value = held[s][c] if before is None else held[s][c] + before[s][c]
                    out_ref[c, i, part, s * LANES : (s + 1) * LANES] = value * AX_BETA

        carry = [axial(q, 1.0) for q in load(first - 1)] if first > 0 else None
        held = None
        for i in range(count):
            q = load(first + i)
            flux = [all_fluxes(q[s]) for s in range(strips)]
            if held is not None:
                finish(
                    i - 1,
                    held,
                    [[straight(q[s][c]) - flux[s][0][c] for c in range(5)] for s in range(strips)],
                )
            total = []
            for s in range(strips):
                alpha2, beta2, _, _, center, source = coefs[s]
                part_sum = [q[s][c] * center for c in range(5)]
                if carry is not None:
                    part_sum = [part_sum[c] + carry[s][c] for c in range(5)]
                wide = slice(s * LANES, (s + 1) * LANES)
                for c in range(5):
                    spread = q[s][c] * alpha2
                    moved = flux[s][1][c] * beta2
                    above = next_ref[i, c, pl.ds(j + 1, 1), :][:, wide]
                    below = prev_ref[i, c, pl.ds(j + SUB - 1, 1), :][:, wide]
                    up = pltpu.roll(spread - moved, SUB - 1, 0)
                    down = pltpu.roll(spread + moved, 1, 0)
                    part_sum[c] = part_sum[c] + (
                        jnp.where(last_row, above, up) + jnp.where(first_row, below, down)
                    )
                part_sum[2] = part_sum[2] - flux[s][1][3] * source
                part_sum[3] = part_sum[3] + flux[s][1][2] * source
                total.append(part_sum)
            carry = [[straight(q[s][c]) + flux[s][0][c] for c in range(5)] for s in range(strips)]
            for c in range(5):
                ups, downs, walls = [], [], None
                for s in range(strips):
                    spread = q[s][c] * radial_alpha
                    outward = spread + flux[s][2][c] * coefs[s][3]
                    ups.append(pltpu.roll(spread - flux[s][2][c] * coefs[s][2], LANES - 1, 1))
                    downs.append(pltpu.roll(outward, 1, 1))
                    walls = -outward if c == 3 else outward
                for s in range(strips):
                    up = jnp.where(last_lane, ups[s + 1] if s + 1 < strips else walls, ups[s])
                    down = jnp.where(first_lane, downs[s - 1] if s else 0.0, downs[s])
                    total[s][c] = total[s][c] + (up + down)
            held = total
        before = None
        if first + count < planes:
            before = [axial(q, -1.0) for q in load(first + count)]
        finish(count - 1, held, before)

    @pl.loop(0, tiles)
    def _(j):
        tile(j)


def main_call(first, count, angle_step, held, after, handed_on):
    channels, planes, strips, sector = held.shape[:4]
    cells = strips * LANES
    whole = pl.BlockSpec(memory_space=pltpu.VMEM)
    edge = (count, channels, sector // SUB + SUB, cells)
    shapes = [pltpu.VMEM((channels, count, sector, cells), f32)]
    if handed_on:
        shapes.append(jax.ShapeDtypeStruct(after.shape, f32))
    return pl.pallas_call(
        functools.partial(main_kernel, first, count, angle_step),
        out_shape=tuple(shapes),
        in_specs=[whole, whole if handed_on else pl.BlockSpec(memory_space=pl.ANY)],
        out_specs=(whole,) * len(shapes),
        scratch_shapes=[pltpu.VMEM(edge, f32), pltpu.VMEM(edge, f32)],
        compiler_params=pltpu.CompilerParams(vmem_limit_bytes=GRANT),
        name="cycle_planes_%d" % first,
    )(in_vmem(held), after)


def pick(total, values, lanes, weights):
    for k in range(lanes.shape[0]):
        index = jnp.broadcast_to(lanes[k : k + 1], values.shape)
        term = jnp.take_along_axis(values, index, axis=1, mode="promise_in_bounds") * weights[k : k + 1]
        total = term if total is None else total + term
    return total


def norm_rows(weights):
    total = weights[0:1]
    for k in range(1, weights.shape[0]):
        total = total + weights[k : k + 1]
    return weights / total


def angles_of(own, sector, count):
    lane = lax.broadcasted_iota(jnp.int32, (1, sector), 1) + own * sector
    angle = (lane.astype(f32) + 0.5) * (2.0 * math.pi / count)
    return jnp.cos(angle), jnp.sin(angle)


DEEP = 4
SLOT = 32


def outgoing_kernel(ring, cycle, core, taps, raw_weights, held_ref, far_ref, near_ref, odd_ref, even_ref, send_ref,
                    keep_ref, core_ref, taps_ref, weights_ref, side_ref, turn_ref, vals_ref, lane_ref,
                    weight_ref, flag_ref, used_ref, share_ref, sems):
    channels, planes, sector, cells = cycle.shape
    core_rows, core_cells = core_ref.shape[2:]
    lead = channels * planes
    own = lax.axis_index("azim")
    parity = lax.rem(own, 2)
    ring_even = parity == 0
    near = jnp.where(lax.rem(lax.axis_index("axial"), 2) == 0, planes - 1, 0)
    far = planes - 1 - near
    lane = lax.broadcasted_iota(jnp.int32, (1, LANES), 1)
    per = LANES // DEEP
    early = [
        pltpu.make_async_copy(core, core_ref, sems.at[0]),
        pltpu.make_async_copy(taps, taps_ref, sems.at[1]),
        pltpu.make_async_copy(raw_weights, weights_ref, sems.at[2]),
    ]
    cycle_strips = cells // LANES
    copies = [
        pltpu.make_async_copy(
            cycle.at[:, :, :, pl.ds(n * LANES, LANES)], held_ref.at[:, :, n], sems.at[3 + n]
        )
        for n in range(cycle_strips)
    ]
    for copy in early + copies:
        copy.start()
    groups = ring // 2
    for copy in early:
        copy.wait()

    sides = []
    side_ref[...] = jnp.zeros_like(side_ref)
    strips = -(-core_cells // LANES)
    width = core_cells - (strips - 1) * LANES
    for side in range(2):
        start = 0 if side == 0 else (strips - 1) * LANES
        at = 0 if side == 0 else width - DEEP
        for part in range(-(-lead // per)):
            total = None
            for i in range(part * per, min(lead, (part + 1) * per)):
                block = core_ref[i // planes, i % planes, :, start : min(start + LANES, core_cells)]
                if block.shape[1] < LANES:
                    block = jnp.concatenate(
                        [block, jnp.zeros((core_rows, LANES - block.shape[1]), f32)], axis=1
                    )
                turn = (DEEP * (i - part * per) - at) % LANES
                moved = pltpu.roll(block, turn, 1) if turn else block
                total = moved if total is None else jnp.where(lane // DEEP == i - part * per, moved, total)
            side_ref[0:core_rows, :] = total
            turn_ref[part * LANES : (part + 1) * LANES, 0:SLOT] = jnp.transpose(side_ref[...])
        total = turn_ref[pl.ds(0, lead, stride=DEEP), :]
        for d in range(1, DEEP):
            moved = pltpu.roll(turn_ref[pl.ds(d, lead, stride=DEEP), :], d * SLOT, 1)
            total = jnp.where(lane // SLOT == d, moved, total)
        sides.append(jnp.where(lane < DEEP * SLOT, total, 0.0))

    whole = (strips - 1) * DEEP
    slots = vals_ref.shape[0]
    pairs = slots - 2 - whole
    fold = DEEP // pairs
    vals_ref[0] = sides[0]
    vals_ref[1] = sides[1]
    at_end = (own == 0) | (own == ring - 1)
    base = jnp.where(own == 0, 0, core_rows - DEEP)

    @pl.when(at_end)
    def _():
        if fold * width < LANES:
            vals_ref[2:] = jnp.zeros((slots - 2, lead, LANES), f32)
        for i in range(lead):
            plane = core_ref[i // planes, i % planes]
            rows = jnp.where(own == 0, plane[:DEEP], plane[core_rows - DEEP :])
            for d in range(DEEP):
                for s in range(strips - 1):
                    vals_ref[2 + s * DEEP + d, i : i + 1, :] = rows[d : d + 1, s * LANES : (s + 1) * LANES]
                at = (d % fold) * width
                vals_ref[2 + whole + d // fold, i : i + 1, at : at + width] = rows[d : d + 1, (strips - 1) * LANES :]

    weights = norm_rows(weights_ref[...])
    cell = taps_ref[...]
    row = ((cell.astype(f32) + 0.5) * (1.0 / core_cells)).astype(jnp.int32)
    column = cell - row * core_cells
    row = row - own * core_rows
    here = (row >= 0) & (row < core_rows)
    left = column < DEEP
    right = column >= core_cells - DEEP
    side_lane = jnp.where(left, column, column - (core_cells - DEEP)) * SLOT + row
    depth = row - base
    tail = column >= (strips - 1) * LANES
    end_slot = jnp.where(tail, whole + depth // fold, (column // LANES) * DEEP + depth) + 2
    end_lane = jnp.where(tail, column - (strips - 1) * LANES + (depth % fold) * width, column % LANES)
    inside = here & at_end & (depth >= 0) & (depth < DEEP)
    slot = jnp.where(here & left, 0, jnp.where(here & right, 1, jnp.where(inside, end_slot, slots)))
    lane_ref[...] = jnp.where(slot < 2, side_lane, jnp.where(slot < slots, end_lane, 0))
    for d in range(slots):
        mine = jnp.where(slot == d, weights, 0.0)
        weight_ref[d] = mine
        flag_ref[d : d + 1, :] = jnp.max(mine, axis=0, keepdims=True)
    power = jnp.left_shift(1, lax.broadcasted_iota(jnp.int32, (slots, 1), 0)).astype(f32)
    for s in range(ring):
        most = jnp.max(flag_ref[:, s * sector : (s + 1) * sector], axis=1, keepdims=True)
        used_ref[s] = jnp.sum(jnp.where(most > 0.0, power, 0.0)).astype(jnp.int32)

    @pl.loop(0, ring)
    def _(s):
        part = pl.ds(pl.multiple_of(s * sector, sector), sector)
        share_ref[:, part] = jnp.zeros((lead, sector), f32)
        used = used_ref[s]

        def add(d):
            @pl.when(lax.rem(lax.div(used, 1 << d), 2) == 1)
            def _():
                share_ref[:, part] = pick(
                    share_ref[:, part], vals_ref[d], lane_ref[:, part], weight_ref[d, :, part]
                )

        add(0)
        add(1)

        @pl.when(used > 3)
        def _():
            for d in range(2, slots):
                add(d)

    copies[0].wait()
    trace = None
    for i in range(lead):
        block = held_ref[i // planes, i % planes, 0]
        moved = pltpu.roll(block, i, 1) if i else block
        trace = moved if trace is None else jnp.where(lane == i, moved, trace)
    trace = jnp.transpose(trace)[:lead]
    cosine, sine = angles_of(own, sector, sector * ring)
    last = pl.ds(groups * sector, sector)
    azimuthal, radial = trace[2 * planes : 3 * planes], trace[3 * planes : 4 * planes]
    send_ref[0 : 2 * planes, last] = trace[0 : 2 * planes]
    send_ref[2 * planes : 3 * planes, last] = radial * cosine - azimuthal * sine
    send_ref[3 * planes : 4 * planes, last] = radial * sine + azimuthal * cosine
    send_ref[4 * planes :, last] = trace[4 * planes :]

    for g in range(groups):
        to = pl.ds(g * sector, sector)
        mine = pl.ds(pl.multiple_of((2 * g + parity) * sector, sector), sector)
        other = pl.ds(pl.multiple_of((2 * g + 1 - parity) * sector, sector), sector)
        keep_ref[:, to] = share_ref[:, mine]
        send_ref[:, to] = share_ref[:, other]

    for c in range(channels):
        near_ref[c, sector:, 0:core_cells] = core_ref[c, near]
        far_ref[c, sector:, 0:core_cells] = core_ref[c, far]
    for copy in copies[1:]:
        copy.wait()
    for c in range(channels):
        for n in range(cycle_strips):
            wide = slice(n * LANES, (n + 1) * LANES)
            near_ref[c, 0:sector, wide] = held_ref[c, near, n]
            far_ref[c, 0:sector, wide] = held_ref[c, far, n]
    for c in range(channels):
        for x in range(planes):
            i = c * planes + x
            for n in range(cycle_strips):
                low = held_ref[c, x, n, 0:1, :]
                high = held_ref[c, x, n, sector - 1 : sector, :]
                start = n * LANES
                even_ref[i : i + 1, start : start + LANES] = jnp.where(ring_even, high, low)
                odd_ref[i : i + 1, start : start + LANES] = jnp.where(ring_even, low, high)
            low = core_ref[c, x, 0:1, :]
            high = core_ref[c, x, core_rows - 1 : core_rows, :]
            even_ref[i : i + 1, cells : cells + core_cells] = jnp.where(ring_even, high, low)
            odd_ref[i : i + 1, cells : cells + core_cells] = jnp.where(ring_even, low, high)


def outgoing_call(ring, cycle, core, taps, weights):
    channels, planes, sector, cells = cycle.shape
    core_rows, core_cells = core.shape[2:]
    lead = channels * planes
    groups = ring // 2
    strips = -(-core_cells // LANES)
    fold = 2 if 2 * (core_cells - (strips - 1) * LANES) <= LANES else 1
    slots = 2 + (strips - 1) * DEEP + DEEP // fold
    parts = -(-lead * DEEP // LANES)
    whole = pl.BlockSpec(memory_space=pltpu.VMEM)
    anywhere = pl.BlockSpec(memory_space=pl.ANY)
    edge = cells + strips * LANES
    plane = jax.ShapeDtypeStruct((channels, sector + core_rows, cells), f32)
    return pl.pallas_call(
        functools.partial(outgoing_kernel, ring),
        out_shape=(
            pltpu.VMEM((channels, planes, cells // LANES, sector, LANES), f32),
            plane,
            plane,
            jax.ShapeDtypeStruct((lead, edge), f32),
            jax.ShapeDtypeStruct((lead, edge), f32),
            jax.ShapeDtypeStruct((lead, (groups + 1) * sector), f32),
            jax.ShapeDtypeStruct((lead, groups * sector), f32),
        ),
        in_specs=[anywhere] * 4,
        out_specs=(whole,) * 7,
        scratch_shapes=[
            pltpu.VMEM(core.shape, f32),
            pltpu.VMEM(taps.shape, jnp.int32),
            pltpu.VMEM(weights.shape, f32),
            pltpu.VMEM((SLOT, LANES), f32),
            pltpu.VMEM((parts * LANES, LANES), f32),
            pltpu.VMEM((slots, lead, LANES), f32),
            pltpu.VMEM(taps.shape, jnp.int32),
            pltpu.VMEM((slots,) + taps.shape, f32),
            pltpu.VMEM((slots, taps.shape[1]), f32),
            pltpu.SMEM((ring,), jnp.int32),
            pltpu.VMEM((lead, ring * sector), f32),
            pltpu.SemaphoreType.DMA((3 + cells // LANES,)),
        ],
        compiler_params=pltpu.CompilerParams(vmem_limit_bytes=GRANT),
        cost_estimate=pl.CostEstimate(flops=0, bytes_accessed=16 * 1024 * 1024, transcendentals=0),
        name="outgoing",
    )(in_hbm(cycle), in_hbm(core), in_hbm(taps), in_hbm(weights))


def relay_kernel(groups, sent, kept, got, rows, after, rows_ref, own_ref, *outs):
    rows_ref[...] = rows[...]
    sector = own_ref.shape[1] // 3
    own = lax.axis_index("azim")
    group = own // 2
    even = lax.rem(own, 2) == 0
    last = pl.ds(groups * sector, sector)
    mine, other = sent[:, last], got[:, last]
    first = jnp.where(even, mine, other)
    second = jnp.where(even, other, mine)
    for s in range(groups):
        to = own_ref if s == 0 else outs[s - 1]
        target = group ^ s
        part = pl.ds(pl.multiple_of(target * sector, sector), sector)
        to[:, 0:sector] = kept[:, part] + got[:, part]
        to[:, sector : 2 * sector] = first
        to[:, 2 * sector :] = second


def relay_call(ring, sector, sent, kept, got, rows, after):
    groups = ring // 2
    whole = pl.BlockSpec(memory_space=pltpu.VMEM)
    block = jax.ShapeDtypeStruct((kept.shape[0], 3 * sector), f32)
    return pl.pallas_call(
        functools.partial(relay_kernel, groups),
        out_shape=(jax.ShapeDtypeStruct(rows.shape, f32),) + (block,) * groups,
        in_specs=[whole] * 4 + [pl.BlockSpec(memory_space=pl.ANY)],
        out_specs=(whole,) * (1 + groups),
        compiler_params=pltpu.CompilerParams(vmem_limit_bytes=GRANT),
        name="ghost_relay",
    )(sent, kept, got, rows, after)


def final_kernel(ring, core_ref, taps_ref, weights_ref, even_ref, odd_ref, near_ref, far_ref, lower, upper, *rest):
    groups = ring // 2
    blocks = rest[:groups]
    (cycle_out, core_out, k_ref, next_ref, prev_ref, turn_ref, found_ref, strip, wing, brim,
     out_sem) = rest[groups:]
    channels, planes, sector, cells = cycle_out.shape
    core_rows, core_cells = core_ref.shape[2:]
    lead = channels * planes
    own = lax.axis_index("azim")
    group = own // 2
    ring_even = lax.rem(own, 2) == 0
    core_even = lax.rem(lax.axis_index("axial"), 2) == 0
    inner = pl.ds(0, LANES)
    outer = pl.ds(LANES, cells - LANES)
    middle = pl.ds(1, planes - 2)
    ends = (pl.ds(0, SUB), pl.ds(sector - SUB, SUB))

    half = lower.shape[1]

    def block(x):
        return (lower, x) if x < half else (upper, x - half)

    bulk = pl.ds(SUB, sector - 2 * SUB)
    places = [
        (lower.at[:, pl.ds(1, half - 1), bulk, outer], cycle_out.at[:, pl.ds(1, half - 1), bulk, outer]),
        (
            upper.at[:, pl.ds(0, planes - 1 - half), bulk, outer],
            cycle_out.at[:, pl.ds(half, planes - 1 - half), bulk, outer],
        ),
    ]
    places += [(strip.at[x], cycle_out.at[:, x, :, inner]) for x in range(planes)]
    places += [(wing.at[n], cycle_out.at[:, x, :, outer]) for n, x in enumerate((0, planes - 1))]
    places += [(brim.at[n], cycle_out.at[:, middle, ends[n], outer]) for n in range(2)]
    leaving = [
        pltpu.make_async_copy(a, b, out_sem.at[n]) for n, (a, b) in enumerate(places)
    ]
    for copy in leaving[:2]:
        copy.start()
    lane = lax.broadcasted_iota(jnp.int32, (1, LANES), 1)

    total = blocks[0][:, 0:sector]
    for s in range(1, groups):
        total = total + blocks[s][:, 0:sector]
    cosine, sine = angles_of(own, sector, sector * ring)
    q = [total[c * planes : (c + 1) * planes] for c in range(5)]
    q[2], q[3] = q[3] * cosine - q[2] * sine, q[2] * cosine + q[3] * sine
    u, pressure, enthalpy = velocities(q)
    inside = inner_radius - 0.5 * radial_step
    beta = RAD_BETA * inside / (inside + radial_step)
    _, after = to_sides(q, u, pressure, enthalpy, 3, RAD_ALPHA, beta)
    turn_ref[...] = jnp.zeros_like(turn_ref)
    for c in range(5):
        turn_ref[c * planes : (c + 1) * planes, :] = after[c]
    gift = jnp.transpose(turn_ref[...])

    taps, weights = taps_ref[...], norm_rows(weights_ref[...])
    ghosts = taps.shape[1]
    wide = 2 * LANES
    span = lax.broadcasted_iota(jnp.int32, (1, wide), 1)
    shift = own * core_rows
    side_end = jnp.where(own == 0, 2 * core_cells, 3 * core_cells)

    def targets(t):
        left = pltpu.roll(t, ghosts - shift, 1)[:, :wide]
        right = pltpu.roll(t, lax.rem(2 * ghosts + core_rows - core_cells - shift, ghosts), 1)[:, :wide]
        end = pltpu.roll(t, lax.rem(2 * ghosts + PAIR - side_end, ghosts), 1)[:, :wide]
        return jnp.where(span < core_rows, left, jnp.where(span < PAIR, right, end))

    taps, weights = targets(taps), targets(weights)
    lanes = taps % sector
    home = taps // sector
    found_ref[1] = jnp.zeros((lead, LANES), f32)
    def collect(h):
        part = slice(h * LANES, (h + 1) * LANES)
        total = None
        for s in range(groups):
            for y in range(2):
                values = blocks[s][:, (1 + y) * sector : (2 + y) * sector]
                masked = jnp.where(home[:, part] == 2 * (group ^ s) + y, weights[:, part], 0.0)
                total = pick(total, values, lanes[:, part], masked)
        found_ref[h] = total

    collect(0)

    @pl.when((own == 0) | (own == ring - 1))
    def _():
        collect(1)

    found = jnp.concatenate([found_ref[0], found_ref[1]], axis=1)
    turn_ref[0:lead, :] = found[:, 0:LANES]
    sides = jnp.transpose(turn_ref[...])
    left_side = sides[0:core_rows]
    right_side = sides[core_rows : 2 * core_rows]
    found = found[:, PAIR : PAIR + core_cells]

    for x in range(planes):
        part, at = block(x)
        for c in range(5):
            i = c * planes + x
            moved = pltpu.roll(gift, (LANES - i) % LANES, 1)
            strip[x, c] = part[c, at, :, 0:LANES] + jnp.where(lane == 0, moved, 0.0)

    def sides(q):
        u, pressure, enthalpy = velocities(q)
        return to_sides(q, u, pressure, enthalpy, 1, AX_ALPHA, AX_BETA)

    @pl.loop(0, sector // SUB)
    def _(j):
        part = pl.ds(pl.multiple_of(j * SUB, SUB), SUB)
        near = [near_ref[c, part, :] for c in range(5)]
        far = [far_ref[c, part, :] for c in range(5)]
        _, low = sides([jnp.where(core_even, far[c], near[c]) for c in range(5)])
        high, _ = sides([jnp.where(core_even, near[c], far[c]) for c in range(5)])
        for n, value in enumerate((low, high)):
            ref, at = block(n * (planes - 1))
            for c in range(5):
                strip[n * (planes - 1), c, part, :] += value[c][:, :LANES]
                wing[n, c, part, :] = ref[c, at, part, LANES:] + value[c][:, LANES:]

    _, radius_inv = radial_tables(cells)
    alpha2, beta2 = azim_coefs(radius_inv, 2.0 * math.pi / (sector * ring))
    def row_pair(start, width):
        pairs = []
        for c in range(5):
            odd = odd_ref[c * planes : (c + 1) * planes, start : start + width]
            even = even_ref[c * planes : (c + 1) * planes, start : start + width]
            pairs.append((jnp.where(ring_even, odd, even), jnp.where(ring_even, even, odd)))
        return [p[0] for p in pairs], [p[1] for p in pairs]

    low, high = row_pair(0, cells)
    _, low = edge_rows(low, alpha2, beta2)
    high, _ = edge_rows(high, alpha2, beta2)
    for n, value in enumerate((low, high)):
        at = n * (sector - 1)
        small = n * (SUB - 1)
        for c in range(5):
            for x in range(planes):
                strip[x, c, at : at + 1, :] += value[c][x : x + 1, :LANES]
                rest_row = value[c][x : x + 1, LANES:]
                if 0 < x < planes - 1:
                    ref, spot = block(x)
                    brim[n, c, x - 1] = ref[c, spot, ends[n], LANES:]
                    brim[n, c, x - 1, small : small + 1, :] += rest_row
                else:
                    wing[min(x, 1), c, at : at + 1, :] += rest_row
    for copy in leaving[2:]:
        copy.start()

    strips = k_ref.shape[2]
    padded = k_ref.shape[3]
    tail = strips * LANES - core_cells
    body = LANES - tail
    both_sides = jnp.where(lane < lead, left_side, pltpu.roll(right_side, (body + 1) % LANES, 1))
    lows, highs = row_pair(cells, core_cells)
    for c in range(5):
        low, high = lows[c], highs[c]
        ends = found[c * planes : (c + 1) * planes]
        low = jnp.where(own == 0, ends, low)
        high = jnp.where(own == ring - 1, ends, high)
        for x in range(planes):
            i = c * planes + x
            for s in range(strips - 1):
                k_ref[c, x, s, 0:core_rows, :] = core_ref[c, x, :, s * LANES : (s + 1) * LANES]
            k_ref[c, x, strips - 1, 0:core_rows, 0:body] = core_ref[c, x, :, (strips - 1) * LANES :]
            pad = pltpu.roll(both_sides, (LANES - 1 - i) % LANES, 1)
            k_ref[c, x, strips - 1, 0:core_rows, body:] = pad[:, body:]
            for row, value in ((core_rows, high), (padded - 1, low)):
                for s in range(strips - 1):
                    k_ref[c, x, s, row : row + 1, :] = value[x : x + 1, s * LANES : (s + 1) * LANES]
                k_ref[c, x, strips - 1, row : row + 1, 0:body] = value[x : x + 1, (strips - 1) * LANES :]

    def load(c, x, part):
        return jnp.concatenate([k_ref[c, x, s, part, :] for s in range(strips)], axis=1)

    tiles = padded // SUB
    for x in range(planes):
        start = [load(c, x, pl.ds(0, tiles, stride=SUB)) for c in range(5)]
        before, _ = edge_rows(start, CORE_ALPHA, CORE_BETA)
        end = [load(c, x, pl.ds(SUB - 1, tiles, stride=SUB)) for c in range(5)]
        _, after = edge_rows(end, CORE_ALPHA, CORE_BETA)
        for c in range(5):
            next_ref[x, c, 0:tiles, :] = before[c]
            prev_ref[x, c, SUB : SUB + tiles, :] = after[c]
            prev_ref[x, c, SUB - 1 : SUB, :] = after[c][tiles - 1 : tiles]

    row = lax.broadcasted_iota(jnp.int32, (SUB, 1), 0)
    center = 1.0 - 2.0 * AX_ALPHA - 4.0 * CORE_ALPHA
    full = strips * LANES
    for j in range(-(-core_rows // SUB)):
        size = min(SUB, core_rows - j * SUB)
        part = pl.ds(j * SUB, SUB)
        here = pl.ds(j * SUB, size)

        def outside(ref):
            q = [ref[c, pl.ds(sector + j * SUB, size), 0:core_cells] for c in range(5)]
            u, pressure, enthalpy = velocities(q)
            return to_sides(q, u, pressure, enthalpy, 1, AX_ALPHA, AX_BETA)

        near_before, near_after = outside(near_ref)
        far_before, far_after = outside(far_ref)
        from_low = [jnp.where(core_even, a, b) for a, b in zip(far_after, near_after)]
        from_high = [jnp.where(core_even, a, b) for a, b in zip(near_before, far_before)]
        carry, held = None, None
        for x in range(planes):
            q = [load(c, x, part) for c in range(5)]
            u, pressure, enthalpy = velocities(q)
            before, after = to_sides(q, u, pressure, enthalpy, 1, AX_ALPHA, AX_BETA)
            if held is not None:
                for c in range(5):
                    core_out[c, x - 1, here, :] = (held[c] + before[c])[:size, :core_cells]
            result = [q[c] * center for c in range(5)]
            if carry is not None:
                result = [result[c] + carry[c] for c in range(5)]
            carry = after
            before, after = to_sides(q, u, pressure, enthalpy, 2, CORE_ALPHA, CORE_BETA)
            for c in range(5):
                above = next_ref[x, c, pl.ds((j + 1) % tiles, 1), :]
                below = prev_ref[x, c, pl.ds(j + SUB - 1, 1), :]
                up = pltpu.roll(before[c], SUB - 1, 0)
                down = pltpu.roll(after[c], 1, 0)
                result[c] = result[c] + (
                    jnp.where(row == SUB - 1, above, up) + jnp.where(row == 0, below, down)
                )
            before, after = to_sides(q, u, pressure, enthalpy, 3, CORE_ALPHA, CORE_BETA)
            for c in range(5):
                result[c] = result[c] + (
                    pltpu.roll(before[c], full - 1, 1) + pltpu.roll(after[c], 1, 1)
                )
            held = result
        for c in range(5):
            core_out[c, planes - 1, here, :] = held[c][:size, :core_cells] + from_high[c]
            core_out[c, 0, here, :] += from_low[c]

    for copy in leaving:
        copy.wait()


def final_call(ring, shape, core, taps, weights, even, odd, near, far, lower, upper, blocks):
    channels, planes, sector, cells = shape
    core_rows, core_cells = core.shape[2:]
    strips = -(-(core_cells + 2) // LANES)
    padded = -(-(core_rows + 2) // SUB) * SUB
    lead = channels * planes
    whole = pl.BlockSpec(memory_space=pltpu.VMEM)
    anywhere = pl.BlockSpec(memory_space=pltpu.HBM)
    groups = ring // 2
    edge_shape = (planes, channels, 2 * SUB, strips * LANES)
    return pl.pallas_call(
        functools.partial(final_kernel, ring),
        out_shape=(
            jax.ShapeDtypeStruct(shape, f32),
            jax.ShapeDtypeStruct(core.shape, f32),
        ),
        in_specs=[whole] * (9 + groups),
        out_specs=(anywhere, whole),
        scratch_shapes=[
            pltpu.VMEM((channels, planes, strips, padded, LANES), f32),
            pltpu.VMEM(edge_shape, f32),
            pltpu.VMEM(edge_shape, f32),
            pltpu.VMEM((LANES, LANES), f32),
            pltpu.VMEM((2, lead, LANES), f32),
            pltpu.VMEM((planes, channels, sector, LANES), f32),
            pltpu.VMEM((2, channels, sector, cells - LANES), f32),
            pltpu.VMEM((2, channels, planes - 2, SUB, cells - LANES), f32),
            pltpu.SemaphoreType.DMA((planes + 6,)),
        ],
        compiler_params=pltpu.CompilerParams(vmem_limit_bytes=GRANT),
        name="late_terms",
    )(core, taps, weights, even, odd, near, far, in_vmem(lower), in_vmem(upper), *blocks)


def body(cycle, core, core_taps, core_weights, cycle_taps, cycle_weights):
    planes, sector = cycle.shape[1:3]
    ring = lax.axis_size("azim")
    length = lax.axis_size("axial")
    angle_step = 2.0 * math.pi / (sector * ring)
    even_axial = [(i, i ^ 1) for i in range(length)]
    odd_axial = [(i, (i + 1) % length) for i in range(1, length, 2)]
    odd_axial += [(b, a) for a, b in odd_axial]
    even_azim = [(i, i ^ 1) for i in range(ring)]
    odd_azim = [(i, (i + 1) % ring) for i in range(1, ring, 2)]
    odd_azim += [(b, a) for a, b in odd_azim]
    held, far, near, odd, even, sent, kept = outgoing_call(ring, cycle, core, cycle_taps.T, cycle_weights.T)
    got = lax.ppermute(sent, "azim", even_azim)
    near = lax.ppermute(near, "axial", even_axial)
    far = lax.ppermute(far, "axial", odd_axial)
    half = planes // 2 - 1
    lower, even = main_call(0, half, angle_step, held, even, True)
    even = lax.ppermute(even, "azim", even_azim)
    odd, *blocks = relay_call(ring, sector, sent, kept, got, odd, lower)
    odd = lax.ppermute(odd, "azim", odd_azim)
    (upper,) = main_call(half, planes - half, angle_step, held, blocks[0], False)
    for s in range(1, ring // 2):
        blocks[s] = lax.ppermute(blocks[s], "azim", [(i, i ^ (2 * s)) for i in range(ring)])
    return tuple(
        final_call(
            ring, cycle.shape, core, core_taps.T, core_weights.T, even, odd, near, far, lower, upper, blocks
        )
    )


def solution(mesh):
    placed = (P(None, "axial", "azim", None), P(None, "axial", "azim", None), P(), P(), P(), P())
    return jax.shard_map(
        body,
        mesh=mesh,
        in_specs=placed,
        out_specs=(P(None, "axial", "azim", None), P(None, "axial", "azim", None)),
        check_vma=False,
    )
```

```python
import functools
import math

import jax
import jax.numpy as jnp
from jax import lax
from jax.experimental import pallas as pl
from jax.experimental.pallas import tpu as pltpu
from jax.sharding import PartitionSpec as P

time_step = 0.001
axial_step = 0.004
radial_step = 1.0 / 256.0
core_step = 2.0 / 192.0
inner_radius = 1.0
viscosity = 0.002
gamma_minus = 0.4

LANES = 128
SUB = 8
PAIR = 64
GRANT = 16 * 1024 * 1024


def in_hbm(x):
    return pltpu.with_memory_space_constraint(x, pltpu.HBM)


def in_vmem(x):
    return pltpu.with_memory_space_constraint(x, pltpu.VMEM)
f32 = jnp.float32
AX_ALPHA = time_step * viscosity / (axial_step * axial_step)
AX_BETA = time_step / (2.0 * axial_step)
RAD_ALPHA = time_step * viscosity / (radial_step * radial_step)
RAD_BETA = time_step / (2.0 * radial_step)
CORE_ALPHA = time_step * viscosity / (core_step * core_step)
CORE_BETA = time_step / (2.0 * core_step)


def velocities(q):
    inv = 1.0 / q[0]
    u = (q[1] * inv, q[2] * inv, q[3] * inv)
    kinetic = 0.5 * (q[1] * u[0] + q[2] * u[1] + q[3] * u[2])
    pressure = gamma_minus * (q[4] - kinetic)
    return u, pressure, q[4] + pressure


def scaled_flux(q, u, pressure, enthalpy, k, scale):
    su = u[k - 1] * scale
    parts = [q[k] * scale, q[1] * su, q[2] * su, q[3] * su, enthalpy * su]
    parts[k] = parts[k] + pressure * scale
    return parts


def to_sides(q, u, pressure, enthalpy, k, alpha, beta):
    flux = scaled_flux(q, u, pressure, enthalpy, k, beta)
    before, after = [], []
    for c in range(5):
        spread = q[c] * alpha
        before.append(spread - flux[c])
        after.append(spread + flux[c])
    return before, after


def radial_tables(cells):
    lane = lax.broadcasted_iota(jnp.int32, (1, cells), 1).astype(f32)
    radius = inner_radius + (lane + 0.5) * radial_step
    return radius, 1.0 / radius


def azim_coefs(radius_inv, angle_step):
    arc_inv = radius_inv * (1.0 / angle_step)
    return (time_step * viscosity) * arc_inv * arc_inv, (0.5 * time_step) * arc_inv


def edge_rows(q, alpha, beta):
    u, pressure, enthalpy = velocities(q)
    return to_sides(q, u, pressure, enthalpy, 2, alpha, beta)


def all_fluxes(q):
    inv = 1.0 / q[0]
    u1, u2, u3 = q[1] * inv, q[2] * inv, q[3] * inv
    m11, m22, m33 = q[1] * u1, q[2] * u2, q[3] * u3
    m12, m13, m23 = q[1] * u2, q[1] * u3, q[2] * u3
    pressure = gamma_minus * (q[4] - 0.5 * (m11 + m22 + m33))
    enthalpy = q[4] + pressure
    return (
        [q[1], m11 + pressure, m12, m13, enthalpy * u1],
        [q[2], m12, m22 + pressure, m23, enthalpy * u2],
        [q[3], m13, m23, m33 + pressure, enthalpy * u3],
    )


def main_kernel(first, count, angle_step, q_ref, after, *rest):
    out_ref, next_ref, prev_ref = rest[0], rest[-2], rest[-1]
    if len(rest) > 3:
        rest[1][...] = after[...]
    planes, strips, sector = q_ref.shape[1:4]
    cells = strips * LANES
    unit = 1.0 / AX_BETA
    lane = lax.broadcasted_iota(jnp.int32, (1, LANES), 1)
    first_lane = lane == 0
    last_lane = lane == LANES - 1
    row = lax.broadcasted_iota(jnp.int32, (SUB, 1), 0)
    first_row = row == 0
    last_row = row == SUB - 1
    coefs = []
    for s in range(strips):
        radius = inner_radius + ((lane + s * LANES).astype(f32) + 0.5) * radial_step
        radius_inv = 1.0 / radius
        alpha2, beta2 = azim_coefs(radius_inv, angle_step)
        beta_before = RAD_BETA * radius / (radius - radial_step)
        beta_after = RAD_BETA * radius / (radius + radial_step)
        if s == strips - 1:
            wall = RAD_BETA * (radius + radial_step) / radius
            beta_after = jnp.where(last_lane, wall, beta_after)
        center = 1.0 - 2.0 * AX_ALPHA - 2.0 * RAD_ALPHA - 2.0 * alpha2
        table = (alpha2, beta2, beta_before, beta_after, center, time_step * radius_inv)
        coefs.append([jnp.broadcast_to(t * unit, (SUB, LANES)) for t in table])
    ratio = AX_ALPHA / AX_BETA
    radial_alpha = RAD_ALPHA * unit

    tiles = sector // SUB
    zero = jnp.zeros((1, cells), f32)
    for i in range(count):
        for c in range(5):
            prev_ref[i, c, SUB - 1 : SUB, :] = zero
            next_ref[i, c, tiles : tiles + 1, :] = zero

    for i in range(count):
        for s in range(strips):
            alpha2, beta2 = coefs[s][0][:1], coefs[s][1][:1]
            wide = slice(s * LANES, (s + 1) * LANES)
            q = [q_ref[c, first + i, s, pl.ds(0, tiles, stride=SUB), :] for c in range(5)]
            before, _ = edge_rows(q, alpha2, beta2)
            q = [q_ref[c, first + i, s, pl.ds(SUB - 1, tiles, stride=SUB), :] for c in range(5)]
            _, after = edge_rows(q, alpha2, beta2)
            for c in range(5):
                next_ref[i, c, 0:tiles, wide] = before[c]
                prev_ref[i, c, SUB : SUB + tiles, wide] = after[c]

    def straight(q):
        return q if abs(ratio - 1.0) < 1e-9 else q * ratio

    def tile(j):
        part = pl.ds(pl.multiple_of(j * SUB, SUB), SUB)

        def load(x):
            return [[q_ref[c, x, s, part, :] for c in range(5)] for s in range(strips)]

        def axial(q, sign):
            flux = all_fluxes(q)[0]
            return [straight(q[c]) + sign * flux[c] for c in range(5)]

        def finish(i, held, before):
            for s in range(strips):
                for c in range(5):
                    value = held[s][c] if before is None else held[s][c] + before[s][c]
                    out_ref[c, i, part, s * LANES : (s + 1) * LANES] = value * AX_BETA

        carry = [axial(q, 1.0) for q in load(first - 1)] if first > 0 else None
        held = None
        for i in range(count):
            q = load(first + i)
            flux = [all_fluxes(q[s]) for s in range(strips)]
            if held is not None:
                finish(
                    i - 1,
                    held,
                    [[straight(q[s][c]) - flux[s][0][c] for c in range(5)] for s in range(strips)],
                )
            total = []
            for s in range(strips):
                alpha2, beta2, _, _, center, source = coefs[s]
                part_sum = [q[s][c] * center for c in range(5)]
                if carry is not None:
                    part_sum = [part_sum[c] + carry[s][c] for c in range(5)]
                wide = slice(s * LANES, (s + 1) * LANES)
                for c in range(5):
                    spread = q[s][c] * alpha2
                    moved = flux[s][1][c] * beta2
                    above = next_ref[i, c, pl.ds(j + 1, 1), :][:, wide]
                    below = prev_ref[i, c, pl.ds(j + SUB - 1, 1), :][:, wide]
                    up = pltpu.roll(spread - moved, SUB - 1, 0)
                    down = pltpu.roll(spread + moved, 1, 0)
                    part_sum[c] = part_sum[c] + (
                        jnp.where(last_row, above, up) + jnp.where(first_row, below, down)
                    )
                part_sum[2] = part_sum[2] - flux[s][1][3] * source
                part_sum[3] = part_sum[3] + flux[s][1][2] * source
                total.append(part_sum)
            carry = [[straight(q[s][c]) + flux[s][0][c] for c in range(5)] for s in range(strips)]
            for c in range(5):
                ups, downs, walls = [], [], None
                for s in range(strips):
                    spread = q[s][c] * radial_alpha
                    outward = spread + flux[s][2][c] * coefs[s][3]
                    ups.append(pltpu.roll(spread - flux[s][2][c] * coefs[s][2], LANES - 1, 1))
                    downs.append(pltpu.roll(outward, 1, 1))
                    walls = -outward if c == 3 else outward
                for s in range(strips):
                    up = jnp.where(last_lane, ups[s + 1] if s + 1 < strips else walls, ups[s])
                    down = jnp.where(first_lane, downs[s - 1] if s else 0.0, downs[s])
                    total[s][c] = total[s][c] + (up + down)
            held = total
        before = None
        if first + count < planes:
            before = [axial(q, -1.0) for q in load(first + count)]
        finish(count - 1, held, before)

    @pl.loop(0, tiles, unroll=2)
    def _(j):
        tile(j)


def main_call(first, count, angle_step, held, after, handed_on):
    channels, planes, strips, sector = held.shape[:4]
    cells = strips * LANES
    whole = pl.BlockSpec(memory_space=pltpu.VMEM)
    edge = (count, channels, sector // SUB + SUB, cells)
    shapes = [pltpu.VMEM((channels, count, sector, cells), f32)]
    if handed_on:
        shapes.append(jax.ShapeDtypeStruct(after.shape, f32))
    return pl.pallas_call(
        functools.partial(main_kernel, first, count, angle_step),
        out_shape=tuple(shapes),
        in_specs=[whole, whole if handed_on else pl.BlockSpec(memory_space=pl.ANY)],
        out_specs=(whole,) * len(shapes),
        scratch_shapes=[pltpu.VMEM(edge, f32), pltpu.VMEM(edge, f32)],
        compiler_params=pltpu.CompilerParams(vmem_limit_bytes=GRANT),
        name="cycle_planes_%d" % first,
    )(in_vmem(held), after)


def pick(total, values, lanes, weights):
    for k in range(lanes.shape[0]):
        index = jnp.broadcast_to(lanes[k : k + 1], values.shape)
        term = jnp.take_along_axis(values, index, axis=1, mode="promise_in_bounds") * weights[k : k + 1]
        total = term if total is None else total + term
    return total


def norm_rows(weights):
    total = weights[0:1]
    for k in range(1, weights.shape[0]):
        total = total + weights[k : k + 1]
    return weights / total


def angles_of(own, sector, count):
    lane = lax.broadcasted_iota(jnp.int32, (1, sector), 1) + own * sector
    angle = (lane.astype(f32) + 0.5) * (2.0 * math.pi / count)
    return jnp.cos(angle), jnp.sin(angle)


DEEP = 4
SLOT = 32


def outgoing_kernel(ring, cycle, core, taps, raw_weights, held_ref, far_ref, near_ref, odd_ref, even_ref, send_ref,
                    keep_ref, core_ref, taps_ref, weights_ref, side_ref, turn_ref, vals_ref, lane_ref,
                    weight_ref, flag_ref, used_ref, share_ref, sems):
    channels, planes, sector, cells = cycle.shape
    core_rows, core_cells = core_ref.shape[2:]
    lead = channels * planes
    own = lax.axis_index("azim")
    parity = lax.rem(own, 2)
    ring_even = parity == 0
    near = jnp.where(lax.rem(lax.axis_index("axial"), 2) == 0, planes - 1, 0)
    far = planes - 1 - near
    lane = lax.broadcasted_iota(jnp.int32, (1, LANES), 1)
    per = LANES // DEEP
    early = [
        pltpu.make_async_copy(core, core_ref, sems.at[0]),
        pltpu.make_async_copy(taps, taps_ref, sems.at[1]),
        pltpu.make_async_copy(raw_weights, weights_ref, sems.at[2]),
    ]
    cycle_strips = cells // LANES
    copies = [
        pltpu.make_async_copy(
            cycle.at[:, :, :, pl.ds(n * LANES, LANES)], held_ref.at[:, :, n], sems.at[3 + n]
        )
        for n in range(cycle_strips)
    ]
    for copy in early + copies:
        copy.start()
    groups = ring // 2
    for copy in early:
        copy.wait()

    sides = []
    side_ref[...] = jnp.zeros_like(side_ref)
    strips = -(-core_cells // LANES)
    width = core_cells - (strips - 1) * LANES
    for side in range(2):
        start = 0 if side == 0 else (strips - 1) * LANES
        at = 0 if side == 0 else width - DEEP
        for part in range(-(-lead // per)):
            total = None
            for i in range(part * per, min(lead, (part + 1) * per)):
                block = core_ref[i // planes, i % planes, :, start : min(start + LANES, core_cells)]
                if block.shape[1] < LANES:
                    block = jnp.concatenate(
                        [block, jnp.zeros((core_rows, LANES - block.shape[1]), f32)], axis=1
                    )
                turn = (DEEP * (i - part * per) - at) % LANES
                moved = pltpu.roll(block, turn, 1) if turn else block
                total = moved if total is None else jnp.where(lane // DEEP == i - part * per, moved, total)
            side_ref[0:core_rows, :] = total
            turn_ref[part * LANES : (part + 1) * LANES, 0:SLOT] = jnp.transpose(side_ref[...])
        total = turn_ref[pl.ds(0, lead, stride=DEEP), :]
        for d in range(1, DEEP):
            moved = pltpu.roll(turn_ref[pl.ds(d, lead, stride=DEEP), :], d * SLOT, 1)
            total = jnp.where(lane // SLOT == d, moved, total)
        sides.append(jnp.where(lane < DEEP * SLOT, total, 0.0))

    whole = (strips - 1) * DEEP
    slots = vals_ref.shape[0]
    pairs = slots - 2 - whole
    fold = DEEP // pairs
    vals_ref[0] = sides[0]
    vals_ref[1] = sides[1]
    at_end = (own == 0) | (own == ring - 1)
    base = jnp.where(own == 0, 0, core_rows - DEEP)

    @pl.when(at_end)
    def _():
        if fold * width < LANES:
            vals_ref[2:] = jnp.zeros((slots - 2, lead, LANES), f32)
        for i in range(lead):
            plane = core_ref[i // planes, i % planes]
            rows = jnp.where(own == 0, plane[:DEEP], plane[core_rows - DEEP :])
            for d in range(DEEP):
                for s in range(strips - 1):
                    vals_ref[2 + s * DEEP + d, i : i + 1, :] = rows[d : d + 1, s * LANES : (s + 1) * LANES]
                at = (d % fold) * width
                vals_ref[2 + whole + d // fold, i : i + 1, at : at + width] = rows[d : d + 1, (strips - 1) * LANES :]

    weights = norm_rows(weights_ref[...])
    cell = taps_ref[...]
    row = ((cell.astype(f32) + 0.5) * (1.0 / core_cells)).astype(jnp.int32)
    column = cell - row * core_cells
    row = row - own * core_rows
    here = (row >= 0) & (row < core_rows)
    left = column < DEEP
    right = column >= core_cells - DEEP
    side_lane = jnp.where(left, column, column - (core_cells - DEEP)) * SLOT + row
    depth = row - base
    tail = column >= (strips - 1) * LANES
    end_slot = jnp.where(tail, whole + depth // fold, (column // LANES) * DEEP + depth) + 2
    end_lane = jnp.where(tail, column - (strips - 1) * LANES + (depth % fold) * width, column % LANES)
    inside = here & at_end & (depth >= 0) & (depth < DEEP)
    slot = jnp.where(here & left, 0, jnp.where(here & right, 1, jnp.where(inside, end_slot, slots)))
    lane_ref[...] = jnp.where(slot < 2, side_lane, jnp.where(slot < slots, end_lane, 0))
    for d in range(slots):
        mine = jnp.where(slot == d, weights, 0.0)
        weight_ref[d] = mine
        flag_ref[d : d + 1, :] = jnp.max(mine, axis=0, keepdims=True)
    power = jnp.left_shift(1, lax.broadcasted_iota(jnp.int32, (slots, 1), 0)).astype(f32)
    for s in range(ring):
        most = jnp.max(flag_ref[:, s * sector : (s + 1) * sector], axis=1, keepdims=True)
        used_ref[s] = jnp.sum(jnp.where(most > 0.0, power, 0.0)).astype(jnp.int32)

    @pl.loop(0, ring)
    def _(s):
        part = pl.ds(pl.multiple_of(s * sector, sector), sector)
        share_ref[:, part] = jnp.zeros((lead, sector), f32)
        used = used_ref[s]

        def add(d):
            @pl.when(lax.rem(lax.div(used, 1 << d), 2) == 1)
            def _():
                share_ref[:, part] = pick(
                    share_ref[:, part], vals_ref[d], lane_ref[:, part], weight_ref[d, :, part]
                )

        add(0)
        add(1)

        @pl.when(used > 3)
        def _():
            for d in range(2, slots):
                add(d)

    copies[0].wait()
    trace = None
    for i in range(lead):
        block = held_ref[i // planes, i % planes, 0]
        moved = pltpu.roll(block, i, 1) if i else block
        trace = moved if trace is None else jnp.where(lane == i, moved, trace)
    trace = jnp.transpose(trace)[:lead]
    cosine, sine = angles_of(own, sector, sector * ring)
    last = pl.ds(groups * sector, sector)
    azimuthal, radial = trace[2 * planes : 3 * planes], trace[3 * planes : 4 * planes]
    send_ref[0 : 2 * planes, last] = trace[0 : 2 * planes]
    send_ref[2 * planes : 3 * planes, last] = radial * cosine - azimuthal * sine
    send_ref[3 * planes : 4 * planes, last] = radial * sine + azimuthal * cosine
    send_ref[4 * planes :, last] = trace[4 * planes :]

    for g in range(groups):
        to = pl.ds(g * sector, sector)
        mine = pl.ds(pl.multiple_of((2 * g + parity) * sector, sector), sector)
        other = pl.ds(pl.multiple_of((2 * g + 1 - parity) * sector, sector), sector)
        keep_ref[:, to] = share_ref[:, mine]
        send_ref[:, to] = share_ref[:, other]

    for c in range(channels):
        near_ref[c, sector:, 0:core_cells] = core_ref[c, near]
        far_ref[c, sector:, 0:core_cells] = core_ref[c, far]
    for copy in copies[1:]:
        copy.wait()
    for c in range(channels):
        for n in range(cycle_strips):
            wide = slice(n * LANES, (n + 1) * LANES)
            near_ref[c, 0:sector, wide] = held_ref[c, near, n]
            far_ref[c, 0:sector, wide] = held_ref[c, far, n]
    for c in range(channels):
        for x in range(planes):
            i = c * planes + x
            for n in range(cycle_strips):
                low = held_ref[c, x, n, 0:1, :]
                high = held_ref[c, x, n, sector - 1 : sector, :]
                start = n * LANES
                even_ref[i : i + 1, start : start + LANES] = jnp.where(ring_even, high, low)
                odd_ref[i : i + 1, start : start + LANES] = jnp.where(ring_even, low, high)
            low = core_ref[c, x, 0:1, :]
            high = core_ref[c, x, core_rows - 1 : core_rows, :]
            even_ref[i : i + 1, cells : cells + core_cells] = jnp.where(ring_even, high, low)
            odd_ref[i : i + 1, cells : cells + core_cells] = jnp.where(ring_even, low, high)


def outgoing_call(ring, cycle, core, taps, weights):
    channels, planes, sector, cells = cycle.shape
    core_rows, core_cells = core.shape[2:]
    lead = channels * planes
    groups = ring // 2
    strips = -(-core_cells // LANES)
    fold = 2 if 2 * (core_cells - (strips - 1) * LANES) <= LANES else 1
    slots = 2 + (strips - 1) * DEEP + DEEP // fold
    parts = -(-lead * DEEP // LANES)
    whole = pl.BlockSpec(memory_space=pltpu.VMEM)
    anywhere = pl.BlockSpec(memory_space=pl.ANY)
    edge = cells + strips * LANES
    plane = jax.ShapeDtypeStruct((channels, sector + core_rows, cells), f32)
    return pl.pallas_call(
        functools.partial(outgoing_kernel, ring),
        out_shape=(
            pltpu.VMEM((channels, planes, cells // LANES, sector, LANES), f32),
            plane,
            plane,
            jax.ShapeDtypeStruct((lead, edge), f32),
            jax.ShapeDtypeStruct((lead, edge), f32),
            jax.ShapeDtypeStruct((lead, (groups + 1) * sector), f32),
            jax.ShapeDtypeStruct((lead, groups * sector), f32),
        ),
        in_specs=[anywhere] * 4,
        out_specs=(whole,) * 7,
        scratch_shapes=[
            pltpu.VMEM(core.shape, f32),
            pltpu.VMEM(taps.shape, jnp.int32),
            pltpu.VMEM(weights.shape, f32),
            pltpu.VMEM((SLOT, LANES), f32),
            pltpu.VMEM((parts * LANES, LANES), f32),
            pltpu.VMEM((slots, lead, LANES), f32),
            pltpu.VMEM(taps.shape, jnp.int32),
            pltpu.VMEM((slots,) + taps.shape, f32),
            pltpu.VMEM((slots, taps.shape[1]), f32),
            pltpu.SMEM((ring,), jnp.int32),
            pltpu.VMEM((lead, ring * sector), f32),
            pltpu.SemaphoreType.DMA((3 + cells // LANES,)),
        ],
        compiler_params=pltpu.CompilerParams(vmem_limit_bytes=GRANT),
        cost_estimate=pl.CostEstimate(flops=0, bytes_accessed=16 * 1024 * 1024, transcendentals=0),
        name="outgoing",
    )(in_hbm(cycle), in_hbm(core), in_hbm(taps), in_hbm(weights))


def relay_kernel(groups, sent, kept, got, rows, after, rows_ref, own_ref, *outs):
    rows_ref[...] = rows[...]
    sector = own_ref.shape[1] // 3
    own = lax.axis_index("azim")
    group = own // 2
    even = lax.rem(own, 2) == 0
    last = pl.ds(groups * sector, sector)
    mine, other = sent[:, last], got[:, last]
    first = jnp.where(even, mine, other)
    second = jnp.where(even, other, mine)
    for s in range(groups):
        to = own_ref if s == 0 else outs[s - 1]
        target = group ^ s
        part = pl.ds(pl.multiple_of(target * sector, sector), sector)
        to[:, 0:sector] = kept[:, part] + got[:, part]
        to[:, sector : 2 * sector] = first
        to[:, 2 * sector :] = second


def relay_call(ring, sector, sent, kept, got, rows, after):
    groups = ring // 2
    whole = pl.BlockSpec(memory_space=pltpu.VMEM)
    block = jax.ShapeDtypeStruct((kept.shape[0], 3 * sector), f32)
    return pl.pallas_call(
        functools.partial(relay_kernel, groups),
        out_shape=(jax.ShapeDtypeStruct(rows.shape, f32),) + (block,) * groups,
        in_specs=[whole] * 4 + [pl.BlockSpec(memory_space=pl.ANY)],
        out_specs=(whole,) * (1 + groups),
        compiler_params=pltpu.CompilerParams(vmem_limit_bytes=GRANT),
        name="ghost_relay",
    )(sent, kept, got, rows, after)


def final_kernel(ring, core_ref, taps_ref, weights_ref, even_ref, odd_ref, near_ref, far_ref, lower, upper, *rest):
    groups = ring // 2
    blocks = rest[:groups]
    (cycle_out, core_out, k_ref, next_ref, prev_ref, turn_ref, found_ref, strip, wing, brim,
     out_sem) = rest[groups:]
    channels, planes, sector, cells = cycle_out.shape
    core_rows, core_cells = core_ref.shape[2:]
    lead = channels * planes
    own = lax.axis_index("azim")
    group = own // 2
    ring_even = lax.rem(own, 2) == 0
    core_even = lax.rem(lax.axis_index("axial"), 2) == 0
    inner = pl.ds(0, LANES)
    outer = pl.ds(LANES, cells - LANES)
    middle = pl.ds(1, planes - 2)
    ends = (pl.ds(0, SUB), pl.ds(sector - SUB, SUB))

    half = lower.shape[1]

    def block(x):
        return (lower, x) if x < half else (upper, x - half)

    bulk = pl.ds(SUB, sector - 2 * SUB)
    places = [
        (lower.at[:, pl.ds(1, half - 1), bulk, outer], cycle_out.at[:, pl.ds(1, half - 1), bulk, outer]),
        (
            upper.at[:, pl.ds(0, planes - 1 - half), bulk, outer],
            cycle_out.at[:, pl.ds(half, planes - 1 - half), bulk, outer],
        ),
    ]
    places += [(strip.at[x], cycle_out.at[:, x, :, inner]) for x in range(planes)]
    places += [(wing.at[n], cycle_out.at[:, x, :, outer]) for n, x in enumerate((0, planes - 1))]
    places += [(brim.at[n], cycle_out.at[:, middle, ends[n], outer]) for n in range(2)]
    leaving = [
        pltpu.make_async_copy(a, b, out_sem.at[n]) for n, (a, b) in enumerate(places)
    ]
    for copy in leaving[:2]:
        copy.start()
    lane = lax.broadcasted_iota(jnp.int32, (1, LANES), 1)

    total = blocks[0][:, 0:sector]
    for s in range(1, groups):
        total = total + blocks[s][:, 0:sector]
    cosine, sine = angles_of(own, sector, sector * ring)
    q = [total[c * planes : (c + 1) * planes] for c in range(5)]
    q[2], q[3] = q[3] * cosine - q[2] * sine, q[2] * cosine + q[3] * sine
    u, pressure, enthalpy = velocities(q)
    inside = inner_radius - 0.5 * radial_step
    beta = RAD_BETA * inside / (inside + radial_step)
    _, after = to_sides(q, u, pressure, enthalpy, 3, RAD_ALPHA, beta)
    turn_ref[...] = jnp.zeros_like(turn_ref)
    for c in range(5):
        turn_ref[c * planes : (c + 1) * planes, :] = after[c]
    gift = jnp.transpose(turn_ref[...])

    taps, weights = taps_ref[...], norm_rows(weights_ref[...])
    ghosts = taps.shape[1]
    wide = 2 * LANES
    span = lax.broadcasted_iota(jnp.int32, (1, wide), 1)
    shift = own * core_rows
    side_end = jnp.where(own == 0, 2 * core_cells, 3 * core_cells)

    def targets(t):
        left = pltpu.roll(t, ghosts - shift, 1)[:, :wide]
        right = pltpu.roll(t, lax.rem(2 * ghosts + core_rows - core_cells - shift, ghosts), 1)[:, :wide]
        end = pltpu.roll(t, lax.rem(2 * ghosts + PAIR - side_end, ghosts), 1)[:, :wide]
        return jnp.where(span < core_rows, left, jnp.where(span < PAIR, right, end))

    taps, weights = targets(taps), targets(weights)
    lanes = taps % sector
    home = taps // sector
    found_ref[1] = jnp.zeros((lead, LANES), f32)
    def collect(h):
        part = slice(h * LANES, (h + 1) * LANES)
        total = None
        for s in range(groups):
            for y in range(2):
                values = blocks[s][:, (1 + y) * sector : (2 + y) * sector]
                masked = jnp.where(home[:, part] == 2 * (group ^ s) + y, weights[:, part], 0.0)
                total = pick(total, values, lanes[:, part], masked)
        found_ref[h] = total

    collect(0)

    @pl.when((own == 0) | (own == ring - 1))
    def _():
        collect(1)

    found = jnp.concatenate([found_ref[0], found_ref[1]], axis=1)
    turn_ref[0:lead, :] = found[:, 0:LANES]
    sides = jnp.transpose(turn_ref[...])
    left_side = sides[0:core_rows]
    right_side = sides[core_rows : 2 * core_rows]
    found = found[:, PAIR : PAIR + core_cells]

    for x in range(planes):
        part, at = block(x)
        for c in range(5):
            i = c * planes + x
            moved = pltpu.roll(gift, (LANES - i) % LANES, 1)
            strip[x, c] = part[c, at, :, 0:LANES] + jnp.where(lane == 0, moved, 0.0)

    def sides(q):
        u, pressure, enthalpy = velocities(q)
        return to_sides(q, u, pressure, enthalpy, 1, AX_ALPHA, AX_BETA)

    @pl.loop(0, sector // SUB)
    def _(j):
        part = pl.ds(pl.multiple_of(j * SUB, SUB), SUB)
        near = [near_ref[c, part, :] for c in range(5)]
        far = [far_ref[c, part, :] for c in range(5)]
        _, low = sides([jnp.where(core_even, far[c], near[c]) for c in range(5)])
        high, _ = sides([jnp.where(core_even, near[c], far[c]) for c in range(5)])
        for n, value in enumerate((low, high)):
            ref, at = block(n * (planes - 1))
            for c in range(5):
                strip[n * (planes - 1), c, part, :] += value[c][:, :LANES]
                wing[n, c, part, :] = ref[c, at, part, LANES:] + value[c][:, LANES:]

    _, radius_inv = radial_tables(cells)
    alpha2, beta2 = azim_coefs(radius_inv, 2.0 * math.pi / (sector * ring))
    def row_pair(start, width):
        pairs = []
        for c in range(5):
            odd = odd_ref[c * planes : (c + 1) * planes, start : start + width]
            even = even_ref[c * planes : (c + 1) * planes, start : start + width]
            pairs.append((jnp.where(ring_even, odd, even), jnp.where(ring_even, even, odd)))
        return [p[0] for p in pairs], [p[1] for p in pairs]

    low, high = row_pair(0, cells)
    _, low = edge_rows(low, alpha2, beta2)
    high, _ = edge_rows(high, alpha2, beta2)
    for n, value in enumerate((low, high)):
        at = n * (sector - 1)
        small = n * (SUB - 1)
        for c in range(5):
            for x in range(planes):
                strip[x, c, at : at + 1, :] += value[c][x : x + 1, :LANES]
                rest_row = value[c][x : x + 1, LANES:]
                if 0 < x < planes - 1:
                    ref, spot = block(x)
                    brim[n, c, x - 1] = ref[c, spot, ends[n], LANES:]
                    brim[n, c, x - 1, small : small + 1, :] += rest_row
                else:
                    wing[min(x, 1), c, at : at + 1, :] += rest_row
    for copy in leaving[2:]:
        copy.start()

    strips = k_ref.shape[2]
    padded = k_ref.shape[3]
    tail = strips * LANES - core_cells
    body = LANES - tail
    both_sides = jnp.where(lane < lead, left_side, pltpu.roll(right_side, (body + 1) % LANES, 1))
    lows, highs = row_pair(cells, core_cells)
    for c in range(5):
        low, high = lows[c], highs[c]
        ends = found[c * planes : (c + 1) * planes]
        low = jnp.where(own == 0, ends, low)
        high = jnp.where(own == ring - 1, ends, high)
        for x in range(planes):
            i = c * planes + x
            for s in range(strips - 1):
                k_ref[c, x, s, 0:core_rows, :] = core_ref[c, x, :, s * LANES : (s + 1) * LANES]
            k_ref[c, x, strips - 1, 0:core_rows, 0:body] = core_ref[c, x, :, (strips - 1) * LANES :]
            pad = pltpu.roll(both_sides, (LANES - 1 - i) % LANES, 1)
            k_ref[c, x, strips - 1, 0:core_rows, body:] = pad[:, body:]
            for row, value in ((core_rows, high), (padded - 1, low)):
                for s in range(strips - 1):
                    k_ref[c, x, s, row : row + 1, :] = value[x : x + 1, s * LANES : (s + 1) * LANES]
                k_ref[c, x, strips - 1, row : row + 1, 0:body] = value[x : x + 1, (strips - 1) * LANES :]

    def load(c, x, part):
        return jnp.concatenate([k_ref[c, x, s, part, :] for s in range(strips)], axis=1)

    tiles = padded // SUB
    for x in range(planes):
        start = [load(c, x, pl.ds(0, tiles, stride=SUB)) for c in range(5)]
        before, _ = edge_rows(start, CORE_ALPHA, CORE_BETA)
        end = [load(c, x, pl.ds(SUB - 1, tiles, stride=SUB)) for c in range(5)]
        _, after = edge_rows(end, CORE_ALPHA, CORE_BETA)
        for c in range(5):
            next_ref[x, c, 0:tiles, :] = before[c]
            prev_ref[x, c, SUB : SUB + tiles, :] = after[c]
            prev_ref[x, c, SUB - 1 : SUB, :] = after[c][tiles - 1 : tiles]

    row = lax.broadcasted_iota(jnp.int32, (SUB, 1), 0)
    center = 1.0 - 2.0 * AX_ALPHA - 4.0 * CORE_ALPHA
    full = strips * LANES
    for j in range(-(-core_rows // SUB)):
        size = min(SUB, core_rows - j * SUB)
        part = pl.ds(j * SUB, SUB)
        here = pl.ds(j * SUB, size)

        def outside(ref):
            q = [ref[c, pl.ds(sector + j * SUB, size), 0:core_cells] for c in range(5)]
            u, pressure, enthalpy = velocities(q)
            return to_sides(q, u, pressure, enthalpy, 1, AX_ALPHA, AX_BETA)

        near_before, near_after = outside(near_ref)
        far_before, far_after = outside(far_ref)
        from_low = [jnp.where(core_even, a, b) for a, b in zip(far_after, near_after)]
        from_high = [jnp.where(core_even, a, b) for a, b in zip(near_before, far_before)]
        carry, held = None, None
        for x in range(planes):
            q = [load(c, x, part) for c in range(5)]
            u, pressure, enthalpy = velocities(q)
            before, after = to_sides(q, u, pressure, enthalpy, 1, AX_ALPHA, AX_BETA)
            if held is not None:
                for c in range(5):
                    core_out[c, x - 1, here, :] = (held[c] + before[c])[:size, :core_cells]
            result = [q[c] * center for c in range(5)]
            if carry is not None:
                result = [result[c] + carry[c] for c in range(5)]
            carry = after
            before, after = to_sides(q, u, pressure, enthalpy, 2, CORE_ALPHA, CORE_BETA)
            for c in range(5):
                above = next_ref[x, c, pl.ds((j + 1) % tiles, 1), :]
                below = prev_ref[x, c, pl.ds(j + SUB - 1, 1), :]
                up = pltpu.roll(before[c], SUB - 1, 0)
                down = pltpu.roll(after[c], 1, 0)
                result[c] = result[c] + (
                    jnp.where(row == SUB - 1, above, up) + jnp.where(row == 0, below, down)
                )
            before, after = to_sides(q, u, pressure, enthalpy, 3, CORE_ALPHA, CORE_BETA)
            for c in range(5):
                result[c] = result[c] + (
                    pltpu.roll(before[c], full - 1, 1) + pltpu.roll(after[c], 1, 1)
                )
            held = result
        for c in range(5):
            core_out[c, planes - 1, here, :] = held[c][:size, :core_cells] + from_high[c]
            core_out[c, 0, here, :] += from_low[c]

    for copy in leaving:
        copy.wait()


def final_call(ring, shape, core, taps, weights, even, odd, near, far, lower, upper, blocks):
    channels, planes, sector, cells = shape
    core_rows, core_cells = core.shape[2:]
    strips = -(-(core_cells + 2) // LANES)
    padded = -(-(core_rows + 2) // SUB) * SUB
    lead = channels * planes
    whole = pl.BlockSpec(memory_space=pltpu.VMEM)
    anywhere = pl.BlockSpec(memory_space=pltpu.HBM)
    groups = ring // 2
    edge_shape = (planes, channels, 2 * SUB, strips * LANES)
    return pl.pallas_call(
        functools.partial(final_kernel, ring),
        out_shape=(
            jax.ShapeDtypeStruct(shape, f32),
            jax.ShapeDtypeStruct(core.shape, f32),
        ),
        in_specs=[whole] * (9 + groups),
        out_specs=(anywhere, whole),
        scratch_shapes=[
            pltpu.VMEM((channels, planes, strips, padded, LANES), f32),
            pltpu.VMEM(edge_shape, f32),
            pltpu.VMEM(edge_shape, f32),
            pltpu.VMEM((LANES, LANES), f32),
            pltpu.VMEM((2, lead, LANES), f32),
            pltpu.VMEM((planes, channels, sector, LANES), f32),
            pltpu.VMEM((2, channels, sector, cells - LANES), f32),
            pltpu.VMEM((2, channels, planes - 2, SUB, cells - LANES), f32),
            pltpu.SemaphoreType.DMA((planes + 6,)),
        ],
        compiler_params=pltpu.CompilerParams(vmem_limit_bytes=GRANT),
        name="late_terms",
    )(core, taps, weights, even, odd, near, far, in_vmem(lower), in_vmem(upper), *blocks)


def body(cycle, core, core_taps, core_weights, cycle_taps, cycle_weights):
    planes, sector = cycle.shape[1:3]
    ring = lax.axis_size("azim")
    length = lax.axis_size("axial")
    angle_step = 2.0 * math.pi / (sector * ring)
    even_axial = [(i, i ^ 1) for i in range(length)]
    odd_axial = [(i, (i + 1) % length) for i in range(1, length, 2)]
    odd_axial += [(b, a) for a, b in odd_axial]
    even_azim = [(i, i ^ 1) for i in range(ring)]
    odd_azim = [(i, (i + 1) % ring) for i in range(1, ring, 2)]
    odd_azim += [(b, a) for a, b in odd_azim]
    held, far, near, odd, even, sent, kept = outgoing_call(ring, cycle, core, cycle_taps.T, cycle_weights.T)
    got = lax.ppermute(sent, "azim", even_azim)
    near = lax.ppermute(near, "axial", even_axial)
    far = lax.ppermute(far, "axial", odd_axial)
    half = planes // 2 - 1
    lower, even = main_call(0, half, angle_step, held, even, True)
    even = lax.ppermute(even, "azim", even_azim)
    odd, *blocks = relay_call(ring, sector, sent, kept, got, odd, lower)
    odd = lax.ppermute(odd, "azim", odd_azim)
    (upper,) = main_call(half, planes - half, angle_step, held, blocks[0], False)
    for s in range(1, ring // 2):
        blocks[s] = lax.ppermute(blocks[s], "azim", [(i, i ^ (2 * s)) for i in range(ring)])
    return tuple(
        final_call(
            ring, cycle.shape, core, core_taps.T, core_weights.T, even, odd, near, far, lower, upper, blocks
        )
    )


def solution(mesh):
    placed = (P(None, "axial", "azim", None), P(None, "axial", "azim", None), P(), P(), P(), P())
    return jax.shard_map(
        body,
        mesh=mesh,
        in_specs=placed,
        out_specs=(P(None, "axial", "azim", None), P(None, "axial", "azim", None)),
        check_vma=False,
    )
```
